32 devices in a mesh: dp: 8 (over z, y), tp: 4 (over x, core).
Axes of the slice: x: 2, y: 2, z: 4, core: 2. Of those that a mesh axis runs over, the one named last changes fastest.
Arguments:
- inputs: bfloat16 [1024, 16, 768], P('tp', 'dp'), may hold values from -6 to 6
- lengths: int32 [16], P('dp'), may hold values from 256 to 1024, as said below
- w_query: bfloat16 [768, 768], P(None, 'tp'), may hold values from -0.21875 to 0.21875
- b_query: float32 [768], P('tp'), may hold values from -3 to 3
- w_key: bfloat16 [768, 768], P(None, 'tp'), may hold values from -0.21875 to 0.21875
- w_value: bfloat16 [768, 768], P(None, 'tp'), may hold values from -0.21875 to 0.21875
- b_value: float32 [768], P('tp'), may hold values from -0.2 to 0.2
- w_out: bfloat16 [768, 768], P('tp'), may hold values from -6 to 6
- b_out: float32 [768], replicated, may hold values from -3 to 3
- norm1_gain: float32 [768], replicated, may hold values from 0.5 to 1.5
- norm1_bias: float32 [768], replicated, may hold values from -2 to 2
- w_up: bfloat16 [768, 3072], P(None, 'tp'), may hold values from -0.21875 to 0.21875
- b_up: float32 [3072], P('tp'), may hold values from -3 to 3
- w_down: bfloat16 [3072, 768], P('tp'), may hold values from -0.109375 to 0.109375
- b_down: float32 [768], replicated, may hold values from -3 to 3
- norm2_gain: float32 [768], replicated, may hold values from 0.5 to 1.5
- norm2_bias: float32 [768], replicated, may hold values from -2 to 2
- cotangent: bfloat16 [1024, 16, 768], P('tp', 'dp'), may hold values from -6 to 6
Outputs:
- outputs: bfloat16 [1024, 16, 768], P('tp', 'dp')
- input_grad: float32 [1024, 16, 768], P('tp', 'dp')
- grad_w_query: float32 [768, 768], P(None, 'tp')
- grad_b_query: float32 [768], P('tp')
- grad_w_key: float32 [768, 768], P(None, 'tp')
- grad_w_value: float32 [768, 768], P(None, 'tp')
- grad_b_value: float32 [768], P('tp')
- grad_w_out: float32 [768, 768], P('tp')
- grad_b_out: float32 [768], replicated
- grad_norm1_gain: float32 [768], replicated
- grad_norm1_bias: float32 [768], replicated
- grad_w_up: float32 [768, 3072], P(None, 'tp')
- grad_b_up: float32 [3072], P('tp')
- grad_w_down: float32 [3072, 768], P('tp')
- grad_b_down: float32 [768], replicated
- grad_norm2_gain: float32 [768], replicated
- grad_norm2_bias: float32 [768], replicated
The draws below stay inside these ranges and needn't reach their ends.
Inputs may be any that keep to these rules, and one draw needn't show every extreme that they name: Utterance b occupies its first lengths[b] slots; the rest are padding. Utterance 0 has exactly 1024 valid frames.
All inputs are finite; a program needn't handle non-finite values.
Results may differ from the reference program's by a relative error of at most 0.018.
Values may be sent and summed in bfloat16 or wider, within the bound.
A program may use at most 128 MiB of HBM per device.

```python
import jax
import jax.numpy as jnp
from jax import lax

D = 768
HEADS = 12
HEAD_DIM = 64
FF = 3072
LEN = 1024
UTT_MB = 1
UTT_DEV = 2
UTTS = 16


def draw_lengths(key, part):
    devices = UTTS // UTT_DEV
    first, second = jax.random.split(jax.random.fold_in(key, 7))
    ceiling = jax.random.randint(first, (devices, 1), LEN // 2, LEN + 1)
    drawn = jax.random.randint(second, (devices, UTT_DEV), LEN // 4, ceiling + 1)
    flat = drawn.reshape(-1)
    position = jnp.arange(UTTS)
    return jnp.where(position == 0, LEN, flat).astype(jnp.int32)


def levels(stream_key, extent, shards, smallest, top_value):
    level = 1.0
    for dim, parts in shards:
        heights = jax.random.uniform(jax.random.fold_in(jax.random.fold_in(stream_key, 6), dim), (parts,), jnp.float32, smallest / len(shards), top_value / len(shards))
        level = level * jnp.repeat(jnp.exp(heights), extent[dim] // parts).reshape((-1,) + (1,) * (len(extent) - 1 - dim))
    return level


def normal_values(own_key, dims, scale, reach, cuts=(), kind=jnp.bfloat16):
    values = scale * jax.random.normal(own_key, dims, jnp.float32)
    if cuts:
        values = values * levels(own_key, dims, cuts, -0.22, 0.18)
    return jnp.clip(values, -reach, reach).astype(kind)


def setup_inputs(seed: int = 0) -> dict:
    streams_of = jax.random.split(jax.random.key(seed), 19)
    inputs = normal_values(streams_of[0], (LEN, UTTS, D), 1.0, 6.0, ((0, 4), (1, 8)))
    lengths = draw_lengths(jax.random.fold_in(streams_of[18], 71), 0)
    w_query = normal_values(streams_of[2], (D, D), D ** -0.5, 0.21875, ((1, 4),))
    b_query = normal_values(streams_of[3], (D,), 0.5, 3.0, ((0, 4),), jnp.float32)
    w_key = normal_values(streams_of[4], (D, D), D ** -0.5, 0.21875, ((1, 4),))
    w_value = normal_values(streams_of[5], (D, D), D ** -0.5, 0.21875, ((1, 4),))
    b_value = normal_values(streams_of[6], (D,), 0.03, 0.2, ((0, 4),), jnp.float32)
    w_out = normal_values(streams_of[7], (D, D), (max(2 * D // LEN, 1)) ** -0.5, 6.0, ((0, 4),))
    b_out = normal_values(streams_of[8], (D,), 0.5, 3.0, (), jnp.float32)
    norm1_gain = jnp.clip(1.0 + 0.1 * jax.random.normal(streams_of[9], (D,), jnp.float32), 0.5, 1.5)
    norm1_bias = normal_values(streams_of[10], (D,), 0.3, 2.0, (), jnp.float32)
    w_up = normal_values(streams_of[11], (D, FF), D ** -0.5, 0.21875, ((1, 4),))
    b_up = normal_values(streams_of[12], (FF,), 0.5, 3.0, ((0, 4),), jnp.float32)
    w_down = normal_values(streams_of[13], (FF, D), FF ** -0.5, 0.109375, ((0, 4),))
    b_down = normal_values(streams_of[14], (D,), 0.5, 3.0, (), jnp.float32)
    norm2_gain = jnp.clip(1.0 + 0.1 * jax.random.normal(streams_of[15], (D,), jnp.float32), 0.5, 1.5)
    norm2_bias = normal_values(streams_of[16], (D,), 0.3, 2.0, (), jnp.float32)
    cotangent = normal_values(streams_of[17], (LEN, UTTS, D), 1.0, 6.0, ((0, 4), (1, 8)))
    return {"inputs": inputs, "lengths": lengths, "w_query": w_query, "b_query": b_query, "w_key": w_key, "w_value": w_value, "b_value": b_value, "w_out": w_out, "b_out": b_out, "norm1_gain": norm1_gain, "norm1_bias": norm1_bias, "w_up": w_up, "b_up": b_up, "w_down": w_down, "b_down": b_down, "norm2_gain": norm2_gain, "norm2_bias": norm2_bias, "cotangent": cotangent}


@jax.custom_vjp
def low(v):
    return lax.optimization_barrier(v.astype(jnp.bfloat16)).astype(jnp.float32)

@jax.custom_vjp
def low_back(v):
    return v

def low_keep(v):
    return (low(v), None)

def low_pass(kept, grad):
    return (grad,)

def back_keep(v):
    return (v, None)

def back_low(kept, grad):
    return (low(grad),)
low.defvjp(low_keep, low_pass)
low_back.defvjp(back_keep, back_low)
EPS = 1e-05
HIGH = lax.Precision.HIGHEST

def matmul(left, right):
    return jnp.dot(left, right, precision=HIGH, preferred_element_type=jnp.float32)

def rounded_both(value):
    return low(low_back(value))

def layer_norm(value, gain, bias):
    centered = value - lax.optimization_barrier(jnp.mean(value, -1, keepdims=True))
    inverse = lax.rsqrt(lax.optimization_barrier(jnp.mean(centered * centered, -1, keepdims=True)) + EPS)
    return centered * inverse * gain + bias

def forward(frames, lens, w_query, b_query, w_key, w_value, b_value, w_out, b_out, norm1_gain, norm1_bias, w_up, b_up, w_down, b_down, norm2_gain, norm2_bias):
    length, group, width = frames.shape
    rows = frames.reshape(length * group, width)
    query = rounded_both(matmul(rows, w_query) + b_query).reshape(length, group, HEADS, HEAD_DIM)
    keys = rounded_both(matmul(rows, w_key)).reshape(length, group, HEADS, HEAD_DIM)
    values = rounded_both(matmul(rows, w_value) + b_value).reshape(length, group, HEADS, HEAD_DIM)
    valid = jnp.arange(length, dtype=jnp.int32)[None, :] < lens[:, None]
    qblock = min(512, length)
    blocks = query.reshape(length // qblock, qblock, group, HEADS, HEAD_DIM)

    def attend(block):
        scores = low_back(jnp.einsum('qghe,kghe->ghqk', block, keys, precision=HIGH) * 0.125)
        scores = jnp.where(valid[:, None, None, :], scores, -jnp.inf)
        probs = low(jax.nn.softmax(scores, axis=-1))
        return jnp.einsum('ghqk,kghe->qghe', probs, values, precision=HIGH)
    context = lax.map(jax.checkpoint(attend), blocks).reshape(length * group, width)
    context = rounded_both(context)
    attn_branch = low_back(matmul(context, w_out) + b_out)
    hidden = layer_norm(rows + attn_branch, norm1_gain, norm1_bias)
    hidden_low = low(hidden)
    upward = low_back(matmul(hidden_low, w_up) + b_up)
    active = low(jax.nn.gelu(upward, approximate=False))
    ffn_branch = low_back(matmul(active, w_down) + b_down)
    result = layer_norm(hidden + ffn_branch, norm2_gain, norm2_bias)
    return result.reshape(length, group, width)

def reference(inputs, lengths, w_query, b_query, w_key, w_value, b_value, w_out, b_out, norm1_gain, norm1_bias, w_up, b_up, w_down, b_down, norm2_gain, norm2_bias, cotangent):
    params = tuple((arr.astype(jnp.float32) for arr in (w_query, b_query, w_key, w_value, b_value, w_out, b_out, norm1_gain, norm1_bias, w_up, b_up, w_down, b_down, norm2_gain, norm2_bias)))
    groups = UTTS // UTT_MB

    def regroup(arr):
        return arr.astype(jnp.float32).reshape(LEN, groups, UTT_MB, D).transpose(1, 0, 2, 3)

    def step(carry, item):
        frames_group, tangent_group, lens_group = item

        def apply(frames_in, *weights):
            return forward(frames_in, lens_group, *weights)
        result, pullback = jax.vjp(apply, frames_group, *params)
        grads = pullback(tangent_group)
        carry = tuple((total + grad for total, grad in zip(carry, grads[1:])))
        return (carry, (result, grads[0]))
    init = tuple((jnp.zeros_like(param) for param in params))
    totals, (results, input_grads) = lax.scan(step, init, (regroup(inputs), regroup(cotangent), lengths.reshape(groups, UTT_MB)))
    outputs = results.transpose(1, 0, 2, 3).reshape(LEN, UTTS, D).astype(jnp.bfloat16)
    input_grad = input_grads.transpose(1, 0, 2, 3).reshape(LEN, UTTS, D)
    return (outputs, input_grad, totals[0], totals[1], totals[2], totals[3], totals[4], totals[5], totals[6], totals[7], totals[8], totals[9], totals[10], totals[11], totals[12], totals[13], totals[14])
```

```python
import functools
import math

import jax
import jax.numpy as jnp
from jax import lax
from jax.experimental import pallas as pl
from jax.experimental.pallas import tpu as pltpu
from jax.sharding import PartitionSpec as P

HEAD_DIM = 64
EPS = 1e-05
ROOT_HALF = 0.7071067811865476
DENSITY = 0.3989422804014327
SCALE = 0.125
NEG = -1e30
F32 = jnp.float32
BF16 = jnp.bfloat16


def dn(a, b):
    return lax.dot_general(a, b, (((1,), (0,)), ((), ())), preferred_element_type=F32)


def dnt(a, b):
    return lax.dot_general(a, b, (((1,), (1,)), ((), ())), preferred_element_type=F32)


def dtn(a, b):
    return lax.dot_general(a, b, (((0,), (0,)), ((), ())), preferred_element_type=F32)


def split3(v):
    hi = v.astype(BF16).astype(F32)
    rest = v - hi
    mid = rest.astype(BF16).astype(F32)
    return hi, mid, rest - mid


def mean(v):
    return jnp.mean(v, -1, keepdims=True)


def col_sum(v):
    return jnp.sum(v, 0, keepdims=True)


def chunk_of(n):
    for c in (96, 64, 48, 32, 16):
        if n % c == 0:
            return c
    return n


class Plan:
    def __init__(self, block, width, head_cols, ff_local, dp):
        self.block = block
        self.slots = 4 * block
        self.own = 2 * block
        self.width = width
        self.head_cols = head_cols
        self.heads = head_cols // HEAD_DIM
        self.ff = ff_local
        self.dp = dp
        self.bits = dp.bit_length() - 1
        self.wide = max(width, ff_local, 3 * head_cols)
        dpb = list(range(self.bits))
        first = dpb[:1]
        rest = dpb[1:]
        self.streams = [
            ("down", ff_local, width, ["x"] + dpb),
            ("up", width, ff_local, first + ["x"] + rest),
            ("out", head_cols, width, ["x"] + dpb),
            ("qkv", width, 3 * head_cols, ["x"] + dpb),
        ]

    def stream_buffers(self, rows, order):
        shapes = []
        n, both = rows, 2
        for dim in order:
            if dim == "x":
                shapes.append((1, n))
                both = 1
            elif (n // 2) % 16 == 0:
                n //= 2
                shapes.append((both, n))
            else:
                shapes.append((both, n))
        return shapes


def layer(plan, names, *refs):
    r = dict(zip(names, refs))
    block, slots, own, width = plan.block, plan.slots, plan.own, plan.width
    hc, heads, ff, dpn, bits = plan.head_cols, plan.heads, plan.ff, plan.dp, plan.bits
    dp = lax.axis_index("dp")
    tp = lax.axis_index("tp")
    x = lax.div(tp, 2)
    c = lax.rem(tp, 2)
    ox = 1 - x
    bit = [lax.rem(lax.div(dp, 1 << b), 2) for b in range(bits)]
    part = {b: (dp + (1 << b) * (1 - 2 * bit[b]), tp) for b in range(bits)}
    part["x"] = (dp, lax.rem(tp + 2, 4))
    part["c"] = (dp, tp + 1 - 2 * c)
    mesh_id = pl.DeviceIdType.MESH

    ssem, rsem, lsem = r["ssem"], r["rsem"], r["lsem"]
    count = {"r": 0, "l": 0}
    pending = []

    def send(src, dst, who):
        i = count["r"]
        count["r"] += 1
        copy = pltpu.make_async_remote_copy(
            src_ref=src,
            dst_ref=dst,
            send_sem=ssem.at[i],
            recv_sem=rsem.at[i],
            device_id=part[who],
            device_id_type=mesh_id,
        )
        copy.start()
        pending.append(copy)
        return copy

    def done_send(copies):
        for copy in copies:
            copy.wait_send()
            pending[:] = [p for p in pending if p is not copy]

    def local(src, dst):
        i = count["l"]
        count["l"] += 1
        copy = pltpu.make_async_copy(src, dst, lsem.at[i])
        copy.start()
        return copy

    def mult(v, m=16):
        return pl.multiple_of(v, math.gcd(m, 128))

    def row(i):
        return pl.multiple_of(lax.rem(c * own + i * block, slots), block)

    own0 = pl.multiple_of(c * own, own)
    mine = pl.multiple_of(x * block, block)
    other = pl.multiple_of(ox * block, block)

    barrier = pltpu.get_barrier_semaphore()
    for who in part.values():
        pl.semaphore_signal(barrier, inc=1, device_id=who, device_id_type=mesh_id)
    pl.semaphore_wait(barrier, len(part))

    gbits = min(2, bits)
    parts = 1 << gbits
    piece = lax.rem(dp, parts)

    def weight_x(name):
        src, dst = r[name], r["W" + name]
        n = src.shape[0] // parts
        at = pl.ds(mult(piece * n, n), n)
        return [send(src.at[at], dst.at[x, at], "x")]

    def weight_hop(name):
        dst = r["W" + name]
        n = dst.shape[1] // parts
        at = pl.ds(mult(piece * n, n), n)
        return [send(dst.at[ox, at], dst.at[ox, at], b) for b in range(gbits)]

    def weight_far(name):
        if gbits < 2:
            return []
        dst = r["W" + name]
        n = dst.shape[1] // parts
        copies = []
        rows_lo = (n // 2) // 16 * 16
        for b in range(2):
            other_bit = 1 - b
            from_piece = piece + (1 << other_bit) * (1 - 2 * bit[other_bit])
            start, size = (0, rows_lo) if b == 0 else (rows_lo, n - rows_lo)
            if size:
                at = pl.ds(mult(from_piece * n + start, 16), size)
                copies.append(send(dst.at[ox, at], dst.at[ox, at], b))
        return copies

    def arrived(copies):
        for copy in copies:
            copy.wait_recv()

    xs = r["X"]
    local_x = local(r["xin"].at[x], xs.at[pl.ds(own0 + mine, block)])
    local_w = [local(r[name], r["W" + name].at[x]) for name in ("w3", "wo", "wu", "wd")]
    local_b = [local(r["svec"], r["B"].at[x]), local(r["rvec"], r["R"])]
    local_c = local(r["cin"].at[x], r["cot"].at[pl.ds(mine, block)])
    w3_x = weight_x("w3")
    b_x = [send(r["svec"], r["B"].at[x], "x")]
    x_x = send(r["xin"].at[ox], xs.at[pl.ds(own0 + mine, block)], "x")
    local_x.wait()
    at_mine = pl.ds(own0 + mine, block)
    x_c = [send(xs.at[at_mine], xs.at[at_mine], "c")]
    arrived(w3_x)
    w3_h = weight_hop("w3")
    x_x.wait_recv()
    at_other = pl.ds(own0 + other, block)
    x_c.append(send(xs.at[at_other], xs.at[at_other], "c"))
    late_x = {name: weight_x(name) for name in ("wo", "wu", "wd")}
    c_x = send(r["cin"].at[ox], r["cot"].at[pl.ds(mine, block)], "x")
    arrived(w3_h)
    w3_f = weight_far("w3")
    for copy in local_w + local_b:
        copy.wait()
    arrived(b_x)
    arrived(x_c)

    bias = r["B"]
    rep = r["R"]

    lane = lax.broadcasted_iota(jnp.int32, (block, HEAD_DIM), 1)
    valid = r["lens"][x]

    def project(s):
        w3 = r["Ww3"]
        b3 = bias[s, 0:1, : 3 * hc]

        @pl.loop(0, 4)
        def _(i):
            at = pl.ds(pl.multiple_of(i * block, block), block)
            y = dn(xs[at, :], w3[s]) + b3
            first = i * block + block * jnp.where(i == 1, 1, 0) - block * jnp.where(i == 2, 1, 0)
            slot = first + lax.broadcasted_iota(jnp.int32, (block, HEAD_DIM), 0)
            masked = jnp.where(slot < valid, 0.0, NEG)
            k_end = jnp.where(lane == 0, masked, jnp.where(lane < 4, 1.0, 0.0)).astype(BF16)
            q_end = jnp.where(lane == 0, 1.0, 0.0).astype(BF16)
            v_end = jnp.where(lane < 3, 1.0, 0.0).astype(BF16)
            for h in range(heads):
                hs = s * heads + h
                lo = h * HEAD_DIM
                r["QP"][hs, at, :HEAD_DIM] = (y[:, lo : lo + HEAD_DIM] * SCALE).astype(BF16)
                r["QP"][hs, at, HEAD_DIM:] = q_end
                lo += hc
                r["KP"][hs, at, :HEAD_DIM] = y[:, lo : lo + HEAD_DIM].astype(BF16)
                r["KP"][hs, at, HEAD_DIM:] = k_end
                lo += hc
                r["VP"][hs, at, :HEAD_DIM] = y[:, lo : lo + HEAD_DIM].astype(BF16)
                r["VP"][hs, at, HEAD_DIM:] = v_end

    def attend(s):
        @pl.loop(0, 4)
        def _(i):
            at = pl.ds(pl.multiple_of(i * block, block), block)
            for h in range(heads):
                hs = s * heads + h
                q = r["QP"][hs, at, :]
                score = dnt(q, r["KP"][hs])
                top = jnp.max(score, -1, keepdims=True)
                expo = jnp.exp(score - top).astype(BF16)
                o = dn(expo, r["VP"][hs])
                total = o[:, HEAD_DIM : HEAD_DIM + 1]
                r["C"][s, at, h * HEAD_DIM : (h + 1) * HEAD_DIM] = (
                    o[:, :HEAD_DIM] / total
                ).astype(BF16)
                hi, mid, low = split3(-(top + jnp.log(total)))
                r["QP"][hs, at, HEAD_DIM:] = jnp.where(
                    lane == 0,
                    1.0,
                    jnp.where(
                        lane == 1, hi, jnp.where(lane == 2, mid, jnp.where(lane == 3, low, 0.0))
                    ),
                ).astype(BF16)

    project(x)
    attend(x)
    arrived(w3_f)
    late_h = {}
    for name in ("wo", "wu", "wd"):
        arrived(late_x[name])
        late_h[name] = weight_hop(name)
    project(ox)
    attend(ox)
    late_f = {}
    for name in ("wo", "wu", "wd"):
        arrived(late_h[name])
        late_f[name] = weight_far(name)

    sbuf, rbuf = r["SB"], r["RB"]

    def exchange(partial):
        copies = []
        for i in range(2):
            sbuf[i] = partial(row(2 + i)).astype(BF16)
            copies.append(send(sbuf.at[i], rbuf.at[i], "c"))
        return copies

    def share(buf, i):
        at = pl.ds(row(i), block)
        return send(buf.at[at], buf.at[at], "c")

    sums = r["sums"]
    sums[...] = jnp.zeros_like(sums)

    def add_sum(k, v, n=None):
        n = v.shape[-1]
        sums[pl.ds(k, 1), :n] = sums[pl.ds(k, 1), :n] + v

    def attn_out(at0):
        at = pl.ds(at0, block)
        return dn(r["C"][0, at, :], r["Wwo"][0]) + dn(r["C"][1, at, :], r["Wwo"][1])

    arrived(late_f["wo"])
    ex = exchange(attn_out)
    hb_c = []
    for i in range(2):
        a = attn_out(row(i)) + rep[0:1, :width]
        ex[i].wait_recv()
        z = xs[pl.ds(row(i), block), :].astype(F32) + a + rbuf[i].astype(F32)
        z = z - mean(z)
        inv = lax.rsqrt(mean(z * z) + EPS)
        n1 = z * inv
        at = pl.ds(i * block, block)
        r["N1"][at, :] = n1
        r["INV"][at, :] = jnp.broadcast_to(inv, (block, 128))
        r["HB"][pl.ds(row(i), block), :] = (n1 * rep[1:2, :width] + rep[2:3, :width]).astype(BF16)
        hb_c.append(share(r["HB"], i))
    done_send(ex)

    def up(s, first, last):
        @pl.loop(first, last)
        def _(i):
            at = pl.ds(row(i), block)
            u = dn(r["HB"][at, :], r["Wwu"][s]) + bias[s, 1:2, :ff]
            cdf = 0.5 * (1.0 + lax.erf(u * ROOT_HALF))
            r["G"][s, at, :] = (u * cdf).astype(BF16)
            r["SL"][s, at, :] = (cdf + u * (DENSITY * jnp.exp(-0.5 * u * u))).astype(BF16)

    up(x, 0, 2)
    arrived(hb_c)
    up(x, 2, 4)
    arrived(late_f["wu"])
    up(ox, 0, 4)

    def ffn_out(at0):
        at = pl.ds(at0, block)
        return dn(r["G"][0, at, :], r["Wwd"][0]) + dn(r["G"][1, at, :], r["Wwd"][1])

    arrived(late_f["wd"])
    ex = exchange(ffn_out)
    local_c.wait()
    c_x.wait_recv()
    df_c = []
    for i in range(2):
        at = pl.ds(i * block, block)
        hidden = r["N1"][at, :] * rep[1:2, :width] + rep[2:3, :width]
        f = ffn_out(row(i)) + rep[3:4, :width]
        ex[i].wait_recv()
        z = hidden + f + rbuf[i].astype(F32)
        z = z - mean(z)
        inv = lax.rsqrt(mean(z * z) + EPS)
        n2 = z * inv
        r["OB"][at, :] = (n2 * rep[4:5, :width] + rep[5:6, :width]).astype(BF16)
        dy = r["cot"][at, :].astype(F32)
        add_sum(4, col_sum(dy * n2))
        add_sum(5, col_sum(dy))
        e2 = dy * rep[4:5, :width]
        dz = inv * (e2 - mean(e2) - n2 * mean(e2 * n2))
        r["DZ"][at, :] = dz
        df = dz.astype(BF16)
        add_sum(3, col_sum(df.astype(F32)))
        r["DF"][pl.ds(row(i), block), :] = df
        df_c.append(share(r["DF"], i))
    done_send(ex)
    out_x = send(r["OB"].at[pl.ds(other, block)], r["out"].at[x], "x")
    out_l = local(r["OB"].at[pl.ds(mine, block)], r["out"].at[x])

    def adder(dst, d, row0, src, sd, n):
        size = chunk_of(n)

        @pl.loop(0, n // size)
        def _(i):
            at = pl.ds(mult(row0 + i * size), size)
            got = src[sd, pl.ds(mult(i * size), size), :].astype(F32)
            dst[d, at, :] = (dst[d, at, :].astype(F32) + got).astype(BF16)

    def stream(name, rows, order):
        grad, final = r["G_" + name], r["F_" + name]
        row0, n, both = 0, rows, True
        halved = []
        for k, dim in enumerate(order):
            got = r["S_%s_%d" % (name, k)]
            if dim == "x":
                at = pl.ds(row0, n)
                copy = send(grad.at[ox, at], got.at[0], "x")
                yield
                copy.wait_recv()
                adder(grad, x, row0, got, 0, n)
                both = False
                continue
            half = (n // 2) % 16 == 0
            if half:
                n //= 2
                halved.append(dim)
                sent = mult(row0 + (1 - bit[dim]) * n)
                row0 = mult(row0 + bit[dim] * n)
            else:
                sent = row0
            at = pl.ds(sent, n)
            src = grad.at[:, at] if both else grad.at[x, at]
            copy = send(src, got if both else got.at[0], dim)
            yield
            copy.wait_recv()
            if not half:
                done_send([copy])
            if both:
                adder(grad, 0, row0, got, 0, n)
                adder(grad, 1, row0, got, 1, n)
            else:
                adder(grad, x, row0, got, 0, n)
        first = True
        keep = local(grad.at[x, pl.ds(row0, n)], final.at[pl.ds(row0, n)])
        for dim in reversed(halved):
            at = pl.ds(row0, n)
            copy = send(grad.at[x, at] if first else final.at[at], final.at[at], dim)
            first = False
            yield
            copy.wait_recv()
            if keep is not None:
                keep.wait()
                keep = None
            row0 = mult(row0 - bit[dim] * n)
            n *= 2
        if keep is not None:
            keep.wait()

    live = []

    def begin(name):
        for n_, rows, _, order in plan.streams:
            if n_ == name:
                gen = stream(name, rows, order)
                live.append(gen)
        advance(gen)

    def advance(gen=None):
        for g in [gen] if gen is not None else list(live):
            try:
                next(g)
            except StopIteration:
                live.remove(g)

    def slope(first, last):
        @pl.loop(first, last)
        def _(i):
            at = pl.ds(row(i), block)
            for s in range(2):
                da = dnt(r["DF"][at, :], r["Wwd"][s])
                du = da * r["SL"][s, at, :].astype(F32)
                add_sum(8 + s, col_sum(du))
                r["SL"][s, at, :] = du.astype(BF16)

    def weight_grad(dst, left, right):
        for s in range(2):
            cols = dst.shape[1]
            size = min(256, cols)

            @pl.loop(0, cols // size)
            def _(j):
                at = pl.ds(pl.multiple_of(j * size, size), size)
                dst[s, at, :] = dtn(left(s, at), right(s)).astype(BF16)

    slope(0, 2)
    arrived(df_c)
    weight_grad(r["G_down"], lambda s, at: r["G"][s, :, at], lambda s: r["DF"][...])
    begin("down")
    slope(2, 4)
    weight_grad(r["G_up"], lambda s, at: r["HB"][:, at], lambda s: r["SL"][s])
    begin("up")

    def hidden_back(at0):
        at = pl.ds(at0, block)
        return dnt(r["SL"][0, at, :], r["Wwu"][0]) + dnt(r["SL"][1, at, :], r["Wwu"][1])

    ex = exchange(hidden_back)
    da_c = []
    for i in range(2):
        at = pl.ds(i * block, block)
        dh = r["DZ"][at, :] + hidden_back(row(i))
        ex[i].wait_recv()
        dh = dh + rbuf[i].astype(F32)
        n1 = r["N1"][at, :]
        add_sum(1, col_sum(dh * n1))
        add_sum(2, col_sum(dh))
        e1 = dh * rep[1:2, :width]
        dz = r["INV"][at, 0:1] * (e1 - mean(e1) - n1 * mean(e1 * n1))
        r["DZ"][at, :] = dz
        da = dz.astype(BF16)
        add_sum(0, col_sum(da.astype(F32)))
        r["DA"][pl.ds(row(i), block), :] = da
        da_c.append(share(r["DA"], i))
    done_send(ex)

    def context_back(first, last):
        @pl.loop(first, last)
        def _(i):
            at = pl.ds(row(i), block)
            for s in range(2):
                dc = dnt(r["DA"][at, :], r["Wwo"][s]).astype(BF16)
                for h in range(heads):
                    cols = slice(h * HEAD_DIM, (h + 1) * HEAD_DIM)
                    part_dc = dc[:, cols]
                    ctx = r["C"][s, at, cols].astype(F32)
                    hi, mid, low = split3(
                        -jnp.sum(part_dc.astype(F32) * ctx, -1, keepdims=True)
                    )
                    hs = s * heads + h
                    r["DC"][hs, at, :HEAD_DIM] = part_dc
                    r["DC"][hs, at, HEAD_DIM:] = jnp.where(
                        lane == 0,
                        hi,
                        jnp.where(lane == 1, mid, jnp.where(lane == 2, low, 0.0)),
                    ).astype(BF16)

    context_back(0, 2)
    arrived(da_c)
    context_back(2, 4)
    for s in range(2):
        r["G_out"][s] = dtn(r["C"][s], r["DA"][...]).astype(BF16)
    begin("out")

    acc_k, acc_v = r["AK"], r["AV"]

    def head_back(s, h):
        hs = s * heads + h

        @pl.loop(0, 4)
        def _(i):
            at = pl.ds(pl.multiple_of(i * block, block), block)
            q = r["QP"][hs, at, :]
            dc = r["DC"][hs, at, :]
            p = jnp.exp(dnt(r["KP"][hs], q))
            ds = (p * dnt(r["VP"][hs], dc)).astype(BF16)
            dv = dn(p.astype(BF16), dc)
            dk = dn(ds, q)
            dq = dtn(ds, r["KP"][hs])
            r["D3"][s, at, h * HEAD_DIM : (h + 1) * HEAD_DIM] = (
                dq[:, :HEAD_DIM] * SCALE
            ).astype(BF16)

            @pl.when(i == 0)
            def _():
                acc_k[...] = dk
                acc_v[...] = dv

            @pl.when(i > 0)
            def _():
                acc_k[...] = acc_k[...] + dk
                acc_v[...] = acc_v[...] + dv

        lo = hc + h * HEAD_DIM
        r["D3"][s, :, lo : lo + HEAD_DIM] = acc_k[:, :HEAD_DIM].astype(BF16)
        lo += hc
        r["D3"][s, :, lo : lo + HEAD_DIM] = acc_v[:, :HEAD_DIM].astype(BF16)

    for h in range(heads):

        @pl.loop(0, 2)
        def _(s):
            head_back(s, h)

        advance()

    for s in range(2):
        add_sum(10 + s, col_sum(r["D3"][s].astype(F32)))
    weight_grad(r["G_qkv"], lambda s, at: xs[:, at], lambda s: r["D3"][s])
    begin("qkv")

    def input_back(at0):
        at = pl.ds(at0, block)
        return dnt(r["D3"][0, at, :], r["Ww3"][0]) + dnt(r["D3"][1, at, :], r["Ww3"][1])

    ex = exchange(input_back)
    for i in range(2):
        at = pl.ds(i * block, block)
        dx = r["DZ"][at, :] + input_back(row(i))
        ex[i].wait_recv()
        r["DZ"][at, :] = dx + rbuf[i].astype(F32)
    r["DXS"][...] = r["DZ"][pl.ds(other, block), :].astype(BF16)
    dx_x = send(r["DXS"], r["dx_far"], "x")
    dx_l = local(r["DZ"].at[pl.ds(mine, block)], r["dx_own"])

    for k, who in enumerate(["c", "x"] + list(range(bits))):
        rows = 8 if who == "c" else 16
        copy = send(sums.at[pl.ds(0, rows)], r["SR"].at[k, pl.ds(0, rows)], who)
        advance()
        copy.wait_recv()
        done_send([copy])
        sums[0:rows, :] = sums[0:rows, :] + r["SR"][k, 0:rows, :]
    r["vec"][...] = sums[...]
    while live:
        advance()
    out_x.wait_recv()
    dx_x.wait_recv()
    out_l.wait()
    dx_l.wait()
    done_send(list(pending))


def local(
    inputs,
    lengths,
    w_query,
    b_query,
    w_key,
    w_value,
    b_value,
    w_out,
    b_out,
    norm1_gain,
    norm1_bias,
    w_up,
    b_up,
    w_down,
    b_down,
    norm2_gain,
    norm2_bias,
    cotangent,
):
    block, utts, width = inputs.shape
    dpn = lax.axis_size("dp")
    plan = Plan(block, width, w_query.shape[1], w_up.shape[1], dpn)
    hc, ff, wide = plan.head_cols, plan.ff, plan.wide
    slots, own, heads = plan.slots, plan.own, plan.heads

    xin = jnp.transpose(inputs, (1, 0, 2))
    cin = jnp.transpose(cotangent, (1, 0, 2))
    w3 = jnp.concatenate([w_query, w_key, w_value], 1)

    def rows_of(vectors):
        padded = [jnp.pad(v, (0, wide - v.shape[0])) for v in vectors]
        padded += [jnp.zeros((wide,), F32)] * (8 - len(padded))
        return jnp.stack(padded)

    b3 = jnp.concatenate([b_query, jnp.zeros_like(b_query), b_value])
    svec = rows_of([b3, b_up])
    rvec = rows_of([b_out, norm1_gain, norm1_bias, b_down, norm2_gain, norm2_bias])

    operands = [
        ("xin", xin),
        ("cin", cin),
        ("lens", lengths),
        ("w3", w3),
        ("wo", w_out),
        ("wu", w_up),
        ("wd", w_down),
        ("svec", svec),
        ("rvec", rvec),
    ]
    shape_of = jax.ShapeDtypeStruct
    hbm = pl.BlockSpec(memory_space=pl.ANY)
    vmem = pl.BlockSpec(memory_space=pltpu.VMEM)
    smem = pl.BlockSpec(memory_space=pltpu.SMEM)
    outs = [
        ("out", shape_of((2, block, width), BF16), hbm),
        ("dx_own", shape_of((block, width), F32), hbm),
        ("dx_far", shape_of((block, width), BF16), hbm),
        ("vec", shape_of((16, wide), F32), vmem),
    ]
    for name, rows, cols, _ in plan.streams:
        outs.append(("F_" + name, shape_of((rows, cols), BF16), vmem))

    def v(name, shape, dtype=BF16):
        return (name, pltpu.VMEM(shape, dtype))

    scratch = [
        v("X", (slots, width)),
        v("Ww3", (2, width, 3 * hc)),
        v("Wwo", (2, hc, width)),
        v("Wwu", (2, width, ff)),
        v("Wwd", (2, ff, width)),
        v("B", (2, 8, wide), F32),
        v("R", (8, wide), F32),
        v("cot", (own, width)),
        v("QP", (2 * heads, slots, 128)),
        v("KP", (2 * heads, slots, 128)),
        v("VP", (2 * heads, slots, 128)),
        v("DC", (2 * heads, slots, 128)),
        v("C", (2, slots, hc)),
        v("SB", (2, block, width)),
        v("RB", (2, block, width)),
        v("N1", (own, width), F32),
        v("INV", (own, 128), F32),
        v("HB", (slots, width)),
        v("G", (2, slots, ff)),
        v("SL", (2, slots, ff)),
        v("OB", (own, width)),
        v("DZ", (own, width), F32),
        v("DF", (slots, width)),
        v("DA", (slots, width)),
        v("D3", (2, slots, 3 * hc)),
        v("AK", (slots, 128), F32),
        v("AV", (slots, 128), F32),
        v("DXS", (block, width)),
        v("sums", (16, wide), F32),
        v("SR", (2 + plan.bits, 16, wide), F32),
    ]
    for name, rows, cols, order in plan.streams:
        scratch.append(v("G_" + name, (2, rows, cols)))
        for k, (both, n) in enumerate(plan.stream_buffers(rows, order)):
            scratch.append(v("S_%s_%d" % (name, k), (both, n, cols)))
    scratch += [
        ("ssem", pltpu.SemaphoreType.DMA((96,))),
        ("rsem", pltpu.SemaphoreType.DMA((96,))),
        ("lsem", pltpu.SemaphoreType.DMA((24,))),
    ]
    names = [n for n, _ in operands] + [n for n, _, _ in outs] + [n for n, _ in scratch]
    results = pl.pallas_call(
        functools.partial(layer, plan, names),
        out_shape=[s for _, s, _ in outs],
        in_specs=[smem if n == "lens" else hbm for n, _ in operands],
        out_specs=[s for _, _, s in outs],
        scratch_shapes=[s for _, s in scratch],
        compiler_params=pltpu.CompilerParams(
            collective_id=0, has_side_effects=True, vmem_limit_bytes=63 * 2**20
        ),
        name="encoder_layer",
    )(*[a for _, a in operands])
    got = dict(zip([n for n, _, _ in outs], results))
    first = lax.axis_index("tp") < 2
    near, far = got["dx_own"], got["dx_far"].astype(F32)
    input_grad = jnp.stack([jnp.where(first, near, far), jnp.where(first, far, near)], 1)
    outputs = jnp.transpose(got["out"], (1, 0, 2))
    vec = got["vec"]
    grad_b_up = jnp.where(first, vec[8], vec[9])[:ff]
    grad_b3 = jnp.where(first, vec[10], vec[11])
    qkv = got["F_qkv"].astype(F32)
    return (
        outputs,
        input_grad,
        qkv[:, :hc],
        grad_b3[:hc],
        qkv[:, hc : 2 * hc],
        qkv[:, 2 * hc :],
        grad_b3[2 * hc : 3 * hc],
        got["F_out"].astype(F32),
        vec[0, :width],
        vec[1, :width],
        vec[2, :width],
        got["F_up"].astype(F32),
        grad_b_up,
        got["F_down"].astype(F32),
        vec[3, :width],
        vec[4, :width],
        vec[5, :width],
    )


def solution(mesh):
    whole = P()
    rows = P("tp", "dp", None)
    cols = P(None, "tp")
    down = P("tp", None)
    shard = P("tp")
    return jax.shard_map(
        local,
        mesh=mesh,
        in_specs=(
            rows,
            P("dp"),
            cols,
            shard,
            cols,
            cols,
            shard,
            down,
            whole,
            whole,
            whole,
            cols,
            shard,
            down,
            whole,
            whole,
            whole,
            rows,
        ),
        out_specs=(
            rows,
            rows,
            cols,
            shard,
            cols,
            cols,
            shard,
            down,
            whole,
            whole,
            whole,
            cols,
            shard,
            down,
            whole,
            whole,
            whole,
        ),
        check_vma=False,
    )
```

```python
import functools
import math

import jax
import jax.numpy as jnp
from jax import lax
from jax.experimental import pallas as pl
from jax.experimental.pallas import tpu as pltpu
from jax.sharding import PartitionSpec as P

HEAD_DIM = 64
EPS = 1e-05
ROOT_HALF = 0.7071067811865476
DENSITY = 0.3989422804014327
SCALE = 0.125
NEG = -1e30
F32 = jnp.float32
BF16 = jnp.bfloat16


def dn(a, b):
    return lax.dot_general(a, b, (((1,), (0,)), ((), ())), preferred_element_type=F32)


def dnt(a, b):
    return lax.dot_general(a, b, (((1,), (1,)), ((), ())), preferred_element_type=F32)


def dtn(a, b):
    return lax.dot_general(a, b, (((0,), (0,)), ((), ())), preferred_element_type=F32)


def split3(v):
    hi = v.astype(BF16).astype(F32)
    rest = v - hi
    mid = rest.astype(BF16).astype(F32)
    return hi, mid, rest - mid


def mean(v):
    return jnp.mean(v, -1, keepdims=True)


def col_sum(v):
    return jnp.sum(v, 0, keepdims=True)


def chunk_of(n):
    for c in (96, 64, 48, 32, 16):
        if n % c == 0:
            return c
    return n


ORDERS = {
    ('down', 0): [1, 0, 'x', 2],
    ('down', 1): ['x', 0, 1, 2],
    ('down', 2): ['x', 0, 1, 2],
    ('down', 3): [0, 1, 2, 'x'],
    ('up', 0): [1, 0, 'x', 2],
    ('up', 1): ['x', 0, 1, 2],
    ('up', 2): ['x', 0, 1, 2],
    ('up', 3): ['x', 0, 1, 2],
    ('attn', 0): ['x', 0, 1, 2],
    ('attn', 1): ['x', 0, 1, 2],
    ('attn', 2): ['x', 1, 2, 0],
    ('attn', 3): ['x', 0, 1, 2],
}
SCHEDULE = {
    ('up', 's', 1): [('down', 1)],
    'hidden0': [('down', 0), ('down', 3)],
    'hidden1': [('down', 1), ('down', 2)],
    'ctx0': [('up', 0), ('down', 0)],
    'ctx1': [('down', 3)],
    'gout': [('down', 2), ('up', 1), ('down', 1)],
    ('head', 'o', 0): [('up', 0), ('down', 2), ('up', 1), ('up', 2)],
    ('head', 'o', 1): [('down', 3), ('down', 1), ('up', 1), ('up', 2), ('up', 3)],
    ('head', 'o', 2): [('down', 2), ('down', 0), ('down', 1), ('up', 1), ('up', 3), ('up', 2)],
    ('v', 'o'): [('attn', 3), ('down', 2)],
    ('head', 's', 0): [('up', 0), ('down', 1), ('down', 0), ('down', 3), ('up', 1), ('up', 3), ('attn', 3)],
    ('head', 's', 1): [('up', 2), ('down', 2), ('down', 0), ('down', 3), ('up', 0)],
    ('head', 's', 2): [('up', 1), ('attn', 3), ('up', 3), ('up', 2), ('down', 3)],
    ('qk', 's'): [('attn', 0), ('attn', 1), ('down', 0), ('up', 0)],
    'dx0': [('up', 3), ('attn', 2), ('up', 2), ('attn', 3)],
    'dx1': ['sums', ('up', 0), ('attn', 0)],
    "tail": [('attn', 2), ('attn', 1), ('attn', 3), ('attn', 0), ('up', 3), ('attn', 2), ('attn', 1), ('attn', 3), ('attn', 0), ('attn', 2), 'sums', ('attn', 1), ('attn', 0), 'sums', ('attn', 2), ('attn', 1), 'sums', ('attn', 0), ('attn', 2), ('attn', 1), 'sums'],
}


class Plan:
    def __init__(self, block, width, head_cols, ff_local, dp):
        self.block = block
        self.slots = 4 * block
        self.own = 2 * block
        self.width = width
        self.head_cols = head_cols
        self.heads = head_cols // HEAD_DIM
        self.ff = ff_local
        self.dp = dp
        self.bits = dp.bit_length() - 1
        self.wide = max(width, ff_local, -(-3 * head_cols // 128) * 128)
        self.qkv_cols = -(-3 * head_cols // 128) * 128
        self.out_cols = -(-head_cols // 128) * 128
        self.streams = {}
        for name, rows in (("down", ff_local), ("up", width), ("attn", 4 * head_cols)):
            for k in range(4):
                n = rows // 4
                self.streams[(name, k)] = (name, k * n, n, self.order((name, k)))

    def order(self, key):
        order = [d for d in ORDERS[key] if d == "x" or d < self.bits]
        return order + list(range(3, self.bits))

    def steps(self, n, order):
        steps, both = [], 2
        for k, dim in enumerate(order):
            if dim == "x":
                both = 1
                steps.append((dim, both, n, False))
                continue
            last = both == 1 and k == len(order) - 1
            halve = not last and (n // 2) % 16 == 0
            if halve:
                n //= 2
            steps.append((dim, both, n, halve))
        return steps


def layer(plan, names, *refs):
    r = dict(zip(names, refs))
    block, slots, own, width = plan.block, plan.slots, plan.own, plan.width
    hc, heads, ff, dpn, bits = plan.head_cols, plan.heads, plan.ff, plan.dp, plan.bits
    dp = lax.axis_index("dp")
    tp = lax.axis_index("tp")
    x = lax.div(tp, 2)
    c = lax.rem(tp, 2)
    ox = 1 - x
    bit = [lax.rem(lax.div(dp, 1 << b), 2) for b in range(bits)]
    part = {b: (dp + (1 << b) * (1 - 2 * bit[b]), tp) for b in range(bits)}
    part["x"] = (dp, lax.rem(tp + 2, 4))
    part["c"] = (dp, tp + 1 - 2 * c)
    mesh_id = pl.DeviceIdType.MESH

    ssem, rsem, lsem = r["ssem"], r["rsem"], r["lsem"]
    count = {"r": 0, "l": 0}
    pending = []

    def send(src, dst, who):
        i = count["r"]
        count["r"] += 1
        copy = pltpu.make_async_remote_copy(
            src_ref=src,
            dst_ref=dst,
            send_sem=ssem.at[i],
            recv_sem=rsem.at[i],
            device_id=part[who],
            device_id_type=mesh_id,
        )
        copy.start()
        pending.append(copy)
        return copy

    def done_send(copies):
        for copy in copies:
            copy.wait_send()
            pending[:] = [p for p in pending if p is not copy]

    def local(src, dst):
        i = count["l"]
        count["l"] += 1
        copy = pltpu.make_async_copy(src, dst, lsem.at[i])
        copy.start()
        return copy

    def mult(v, m=16):
        return pl.multiple_of(v, math.gcd(m, 128))

    def row(i):
        return pl.multiple_of(lax.rem(c * own + i * block, slots), block)

    own0 = pl.multiple_of(c * own, own)
    mine = pl.multiple_of(x * block, block)
    other = pl.multiple_of(ox * block, block)

    xs = r["X"]
    local_a = []
    for k, name in enumerate(("wq", "wk", "wv", "wo")):
        local_a.append(local(r[name], r["Wwa"].at[x, pl.ds(k * hc, hc)]))
    local_x = local(r["xin"].at[x], xs.at[pl.ds(own0 + mine, block)])
    barrier = pltpu.get_barrier_semaphore()
    for who in part.values():
        pl.semaphore_signal(barrier, inc=1, device_id=who, device_id_type=mesh_id)
    pl.semaphore_wait(barrier, len(part))

    gbits = min(2, bits)
    parts = 1 << gbits
    piece = lax.rem(dp, parts)

    def weight_x(name, lo=0, hi=2, at_piece=piece):
        dst = r["W" + name]
        src = dst.at[x] if name == "wa" else r[name]
        n = src.shape[0] // parts
        cut = (0, n // 2 // 16 * 16, n)
        at = pl.ds(mult(at_piece * n + cut[lo], 16), cut[hi] - cut[lo])
        return [send(src.at[at], dst.at[x, at], "x")]

    def weight_hop(name, lo=0, hi=2):
        dst = r["W" + name]
        n = dst.shape[1] // parts
        cut = (0, n // 2 // 16 * 16, n)
        at = pl.ds(mult(piece * n + cut[lo], 16), cut[hi] - cut[lo])
        return [send(dst.at[ox, at], dst.at[ox, at], b) for b in range(gbits)]

    def weight_far(name, lo=0, hi=2):
        if gbits < 2:
            return []
        dst = r["W" + name]
        n = dst.shape[1] // parts
        cut = (0, n // 2 // 16 * 16, n)
        first, size = cut[lo], cut[hi] - cut[lo]
        low = size // 2 // 16 * 16
        copies = []
        for b, (start, m) in enumerate(((0, low), (low, size - low))):
            o = 1 - b
            from_piece = piece + (1 << o) * (1 - 2 * bit[o])
            if m:
                at = pl.ds(mult(from_piece * n + first + start, 16), m)
                copies.append(send(dst.at[ox, at], dst.at[ox, at], b))
        return copies

    def arrived(copies):
        for copy in copies:
            copy.wait_recv()

    half = block // 2
    for copy in local_a:
        copy.wait()
    local_b = [local(r["svec"], r["B"].at[x]), local(r["rvec"], r["R"])]
    local_w = [local(r[name], r["W" + name].at[x]) for name in ("wu", "wd")]
    local_c = local(r["cin"].at[x], r["cot"].at[pl.ds(mine, block)])
    wa_x = [weight_x("wa", 0, 1), weight_x("wa", 1, 2)]
    b_x = [send(r["svec"], r["B"].at[x], "x")]
    x_x = []
    for k in range(2):
        src = r["xin"].at[ox, pl.ds(k * half, half)]
        x_x.append(send(src, xs.at[pl.ds(own0 + mine + k * half, half)], "x"))
    late_x = {name: weight_x(name) for name in ("wu", "wd")}
    wd_far = []
    if gbits == 2:
        far_piece = parts - 1 - piece
        wd_far = weight_x("wd", at_piece=far_piece)
    c_x = send(r["cin"].at[ox], r["cot"].at[pl.ds(mine, block)], "x")

    bias = r["B"]
    rep = r["R"]
    lane = lax.broadcasted_iota(jnp.int32, (block, 128), 1)
    valid = r["lens"][x]
    pad = plan.out_cols - hc
    if pad:
        for s in range(2):
            r["C"][s, :, hc:] = jnp.zeros((slots, pad), BF16)
    pad3 = plan.qkv_cols - 3 * hc
    if pad3:
        for s in range(2):
            r["D3"][s, :, 3 * hc :] = jnp.zeros((slots, pad3), BF16)

    def project(s, first):
        i = lax.div(first, block)
        at = pl.ds(pl.multiple_of(first, block), block)
        y = dnt(xs[at, :], r["Wwa"][s, : plan.qkv_cols, :]) + bias[s, 0:1, : plan.qkv_cols]
        slot0 = first + block * jnp.where(i == 1, 1, 0) - block * jnp.where(i == 2, 1, 0)
        slot = slot0 + lax.broadcasted_iota(jnp.int32, (block, 128), 0)
        masked = jnp.where(slot < valid, 0.0, NEG)
        real = lane < HEAD_DIM
        k_end = jnp.where(lane == 64, masked, jnp.where(lane < 68, 1.0, 0.0))
        q_end = jnp.where(lane == 64, 1.0, 0.0)
        v_end = jnp.where(lane < 67, 1.0, 0.0)
        for k, (name, end) in enumerate((("QP", q_end), ("KP", k_end), ("VP", v_end))):
            for h in range(heads):
                unit = k * heads + h
                tile = y[:, unit // 2 * 128 : unit // 2 * 128 + 128]
                if unit % 2:
                    tile = pltpu.roll(tile, 64, 1)
                if k == 0:
                    tile = tile * SCALE
                r[name][s * heads + h, at, :] = jnp.where(real, tile, end).astype(BF16)

    early = [own0 + mine, (1 - c) * own + mine]
    late = [own0 + other, (1 - c) * own + other]

    local_x.wait()
    at_mine = pl.ds(own0 + mine, block)
    x_c = [send(xs.at[at_mine], xs.at[at_mine], "c")]
    for copy in local_b:
        copy.wait()
    project(x, early[0])
    x_c.pop().wait_recv()
    project(x, early[1])
    wa_h = []
    for k in range(2):
        arrived(wa_x[k])
        wa_h.append(weight_hop("wa", k, k + 1))
    wa_f = []
    for k in range(2):
        arrived(wa_h[k])
        wa_f += weight_far("wa", k, k + 1)
    x_x[0].wait_recv()
    at_other = [pl.ds(own0 + other + k * half, half) for k in range(2)]
    x_c.append(send(xs.at[at_other[0]], xs.at[at_other[0]], "c"))
    arrived(b_x)
    arrived(wa_f)
    project(ox, early[0])
    project(ox, early[1])
    x_x[1].wait_recv()
    x_c.append(send(xs.at[at_other[1]], xs.at[at_other[1]], "c"))
    project(x, late[0])
    project(ox, late[0])
    arrived(x_c)
    project(x, late[1])
    project(ox, late[1])
    for copy in local_w:
        copy.wait()

    def attend(s, first, last):
        @pl.loop(first, last)
        def _(i):
            at = pl.ds(pl.multiple_of(i * block, block), block)
            for h in range(heads):
                hs = s * heads + h
                q = r["QP"][hs, at, :]
                score = dnt(q, r["KP"][hs])
                top = jnp.max(score, -1, keepdims=True)
                expo = jnp.exp(score - top).astype(BF16)
                o = dn(expo, r["VP"][hs])
                total = o[:, HEAD_DIM : HEAD_DIM + 1]
                r["C"][s, at, h * HEAD_DIM : (h + 1) * HEAD_DIM] = (
                    o[:, :HEAD_DIM] / total
                ).astype(BF16)
                hi, mid, low = split3(-(top + jnp.log(total)))
                r["QP"][hs, at, :] = jnp.where(
                    lane == 65,
                    hi,
                    jnp.where(
                        lane == 66, mid, jnp.where(lane == 67, low, q.astype(F32))
                    ),
                ).astype(BF16)

    late_h, late_f = {}, {}
    attend(x, 0, 2)
    arrived(late_x["wu"])
    late_h["wu"] = weight_hop("wu")
    attend(x, 2, 4)
    attend(ox, 0, 2)
    arrived(late_h["wu"])
    late_f["wu"] = weight_far("wu")
    arrived(late_x["wd"])
    late_h["wd"] = weight_hop("wd")
    attend(ox, 2, 4)

    sbuf, rbuf = r["SB"], r["RB"]

    def exchange(partial):
        copies = []
        for i in range(2):
            sbuf[i] = partial(row(2 + i)).astype(BF16)
            copies.append(send(sbuf.at[i], rbuf.at[i], "c"))
        return copies

    def share(buf, i):
        at = pl.ds(row(i), block)
        return send(buf.at[at], buf.at[at], "c")

    sums = r["sums"]
    sums[...] = jnp.zeros_like(sums)

    def add_sum(k, v, n=None):
        n = v.shape[-1]
        sums[pl.ds(k, 1), :n] = sums[pl.ds(k, 1), :n] + v

    def attn_out(at0):
        at = pl.ds(at0, block)
        return sum(dn(r["C"][s, at, :hc], r["Wwa"][s, 3 * hc :, :]) for s in range(2))

    ex = exchange(attn_out)
    hb_c = []
    for i in range(2):
        a = attn_out(row(i)) + rep[0:1, :width]
        ex[i].wait_recv()
        z = xs[pl.ds(row(i), block), :].astype(F32) + a + rbuf[i].astype(F32)
        z = z - mean(z)
        inv = lax.rsqrt(mean(z * z) + EPS)
        n1 = z * inv
        at = pl.ds(i * block, block)
        r["N1"][at, :] = n1
        r["INV"][at, :] = jnp.broadcast_to(inv, (block, 128))
        r["HB"][pl.ds(row(i), block), :] = (n1 * rep[1:2, :width] + rep[2:3, :width]).astype(BF16)
        hb_c.append(share(r["HB"], i))
    done_send(ex)

    def up(s, first, last):
        @pl.loop(first, last)
        def _(i):
            at = pl.ds(row(i), block)
            u = dn(r["HB"][at, :], r["Wwu"][s]) + bias[s, 1:2, :ff]
            cdf = 0.5 * (1.0 + lax.erf(u * ROOT_HALF))
            r["G"][s, at, :] = (u * cdf).astype(BF16)
            r["SL"][s, at, :] = (cdf + u * (DENSITY * jnp.exp(-0.5 * u * u))).astype(BF16)

    up(x, 0, 2)
    arrived(hb_c)
    up(x, 2, 4)
    arrived(late_f["wu"])
    up(ox, 0, 4)

    def ffn_out(at0):
        at = pl.ds(at0, block)
        return dn(r["G"][0, at, :], r["Wwd"][0]) + dn(r["G"][1, at, :], r["Wwd"][1])

    arrived(late_h["wd"] + wd_far)
    ex = exchange(ffn_out)
    local_c.wait()
    c_x.wait_recv()
    df_c = []
    for i in range(2):
        at = pl.ds(i * block, block)
        hidden = r["N1"][at, :] * rep[1:2, :width] + rep[2:3, :width]
        f = ffn_out(row(i)) + rep[3:4, :width]
        ex[i].wait_recv()
        z = hidden + f + rbuf[i].astype(F32)
        z = z - mean(z)
        inv = lax.rsqrt(mean(z * z) + EPS)
        n2 = z * inv
        r["OB"][at, :] = (n2 * rep[4:5, :width] + rep[5:6, :width]).astype(BF16)
        dy = r["cot"][at, :].astype(F32)
        add_sum(4, col_sum(dy * n2))
        add_sum(5, col_sum(dy))
        e2 = dy * rep[4:5, :width]
        dz = inv * (e2 - mean(e2) - n2 * mean(e2 * n2))
        r["DZ"][at, :] = dz
        df = dz.astype(BF16)
        add_sum(3, col_sum(df.astype(F32)))
        r["DF"][pl.ds(row(i), block), :] = df
        df_c.append(share(r["DF"], i))
    done_send(ex)
    out_x = send(r["OB"].at[pl.ds(other, block)], r["out"].at[x], "x")
    out_l = local(r["OB"].at[pl.ds(mine, block)], r["out"].at[x])

    def adder(dst, d, row0, src, sd, n):
        size = chunk_of(n)

        @pl.loop(0, n // size)
        def _(i):
            at = pl.ds(mult(row0 + i * size), size)
            got = src[sd, pl.ds(mult(i * size), size), :].astype(F32)
            dst[d, at, :] = (dst[d, at, :].astype(F32) + got).astype(BF16)

    def stream(key):
        name, row0, n, order = plan.streams[key]
        grad, final = r["G_" + name], r["F_" + name]
        both, halved = True, []
        for k, (dim, _, n, halve) in enumerate(plan.steps(n, order)):
            got = r["S_%s_%d_%d" % (*key, k)]
            if dim == "x":
                copy = send(grad.at[ox, pl.ds(row0, n)], got.at[0], "x")
                both = False
            else:
                sent = row0
                if halve:
                    halved.append(dim)
                    sent = mult(row0 + (1 - bit[dim]) * n)
                    row0 = mult(row0 + bit[dim] * n)
                at = pl.ds(sent, n)
                copy = send(
                    grad.at[:, at] if both else grad.at[x, at], got if both else got.at[0], dim
                )
            yield
            copy.wait_recv()
            if dim != "x" and not halve:
                done_send([copy])
            if both:
                adder(grad, 0, row0, got, 0, n)
                adder(grad, 1, row0, got, 1, n)
            else:
                adder(grad, x, row0, got, 0, n)
        first = True
        keep = local(grad.at[x, pl.ds(row0, n)], final.at[pl.ds(row0, n)])
        for dim in reversed(halved):
            at = pl.ds(row0, n)
            copy = send(grad.at[x, at] if first else final.at[at], final.at[at], dim)
            first = False
            yield
            copy.wait_recv()
            if keep is not None:
                keep.wait()
                keep = None
            row0 = mult(row0 - bit[dim] * n)
            n *= 2
        if keep is not None:
            keep.wait()

    live = {}

    def advance(key):
        try:
            next(live[key])
        except StopIteration:
            del live[key]

    def begin(key):
        live[key] = sums_stream() if key == "sums" else stream(key)
        advance(key)

    def starts(*keys):
        for key in keys[:-1]:
            if (plan.streams[key][3][0] == "x") == (keys[-1] == "o"):
                begin(key)

    def step(name):
        for key in SCHEDULE.get(name, ()):
            if key in live:
                advance(key)

    def sums_stream():
        for k, who in enumerate(["c", "x"] + list(range(bits))):
            n = 8 if who == "c" else 16
            copy = send(sums.at[pl.ds(0, n)], r["SR"].at[k, pl.ds(0, n)], who)
            yield
            copy.wait_recv()
            done_send([copy])
            sums[0:n, :] = sums[0:n, :] + r["SR"][k, 0:n, :]
        r["vec"][...] = sums[...]

    def slope(first, last):
        @pl.loop(first, last)
        def _(i):
            at = pl.ds(row(i), block)
            for s in range(2):
                da = dnt(r["DF"][at, :], r["Wwd"][s])
                du = da * r["SL"][s, at, :].astype(F32)
                add_sum(8 + s, col_sum(du))
                r["SL"][s, at, :] = du.astype(BF16)

    def weight_grad(name, left, right):
        dst = r["G_" + name]
        n = dst.shape[1] // 2
        for s, tag in ((ox, "o"), (x, "s")):
            for j in range(2):
                at = slice(j * n, (j + 1) * n)
                dst[s, at, :] = dtn(left(s, at), right(s)).astype(BF16)
                starts((name, 2 * j), (name, 2 * j + 1), tag)
                step((name, tag, j))

    slope(0, 2)
    arrived(df_c)
    weight_grad("down", lambda s, at: r["G"][s, :, at], lambda s: r["DF"][...])
    slope(2, 4)
    step("slope")
    weight_grad("up", lambda s, at: r["HB"][:, at], lambda s: r["SL"][s])

    def hidden_back(at0):
        at = pl.ds(at0, block)
        return dnt(r["SL"][0, at, :], r["Wwu"][0]) + dnt(r["SL"][1, at, :], r["Wwu"][1])

    ex = exchange(hidden_back)
    step("hidden0")
    da_c = []
    for i in range(2):
        at = pl.ds(i * block, block)
        dh = r["DZ"][at, :] + hidden_back(row(i))
        ex[i].wait_recv()
        dh = dh + rbuf[i].astype(F32)
        n1 = r["N1"][at, :]
        add_sum(1, col_sum(dh * n1))
        add_sum(2, col_sum(dh))
        e1 = dh * rep[1:2, :width]
        dz = r["INV"][at, 0:1] * (e1 - mean(e1) - n1 * mean(e1 * n1))
        r["DZ"][at, :] = dz
        da = dz.astype(BF16)
        add_sum(0, col_sum(da.astype(F32)))
        r["DA"][pl.ds(row(i), block), :] = da
        da_c.append(share(r["DA"], i))
    done_send(ex)
    step("hidden1")

    rows_e = lax.broadcasted_iota(jnp.int32, (hc, heads * 128), 0)
    lanes_e = lax.broadcasted_iota(jnp.int32, (hc, heads * 128), 1)
    spot = lanes_e - lax.div(rows_e, HEAD_DIM) * 128
    r["E"][...] = jnp.where((spot >= 64) & (spot < 67), -1.0, 0.0).astype(BF16)

    def context_back(first, last):
        @pl.loop(first, last)
        def _(i):
            at = pl.ds(row(i), block)
            for s in range(2):
                dc = dnt(r["DA"][at, :], r["Wwa"][s, 3 * hc :, :]).astype(BF16).astype(F32)
                prod = dc * r["C"][s, at, :hc].astype(F32)
                prod_hi = prod.astype(BF16)
                prod_lo = (prod - prod_hi.astype(F32)).astype(BF16)
                ends = dn(prod_hi, r["E"][...]) + dn(prod_lo, r["E"][...])
                for h in range(heads):
                    end = ends[:, h * 128 : h * 128 + 128]
                    if 2 * h + 2 <= 2 * heads - heads % 2:
                        tile = dc[:, h // 2 * 128 : h // 2 * 128 + 128]
                        if h % 2:
                            tile = pltpu.roll(tile, 64, 1)
                    else:
                        tile = jnp.concatenate([dc[:, h * 64 :], end[:, 64:]], 1)
                    tile = jnp.where(lane < 64, tile, end)
                    hi, mid, low = split3(tile)
                    tile = jnp.where(lane == 65, mid, jnp.where(lane == 66, low, hi))
                    r["DC"][s * heads + h, at, :] = tile.astype(BF16)

    context_back(0, 2)
    step("ctx0")
    arrived(da_c)
    context_back(2, 4)
    step("ctx1")
    for s, tag in ((ox, "o"), (x, "s")):
        r["G_attn"][s, 3 * hc :, :] = dtn(r["C"][s], r["DA"][...])[:hc].astype(BF16)
        starts(("attn", 3), tag)
    step("gout")

    acc_k, acc_v = r["AK"], r["AV"]

    def head_back(s, h):
        hs = s * heads + h

        @pl.loop(0, 4)
        def _(i):
            at = pl.ds(pl.multiple_of(i * block, block), block)
            q = r["QP"][hs, at, :]
            dc = r["DC"][hs, at, :]
            p = jnp.exp(dnt(r["KP"][hs], q))
            ds = (p * dnt(r["VP"][hs], dc)).astype(BF16)
            dv = dn(p.astype(BF16), dc)
            dk = dn(ds, q)
            dq = dtn(ds, r["KP"][hs])
            r["D3"][s, at, h * HEAD_DIM : (h + 1) * HEAD_DIM] = (
                dq[:, :HEAD_DIM] * SCALE
            ).astype(BF16)

            @pl.when(i == 0)
            def _():
                acc_k[...] = dk
                acc_v[...] = dv

            @pl.when(i > 0)
            def _():
                acc_k[...] = acc_k[...] + dk
                acc_v[...] = acc_v[...] + dv

        lo = hc + h * HEAD_DIM
        r["D3"][s, :, lo : lo + HEAD_DIM] = acc_k[:, :HEAD_DIM].astype(BF16)
        lo += hc
        r["D3"][s, :, lo : lo + HEAD_DIM] = acc_v[:, :HEAD_DIM].astype(BF16)

    g_attn = r["G_attn"]
    for s, tag in ((ox, "o"), (x, "s")):
        for h in range(heads):
            head_back(s, h)
            step(("head", tag, h))
        add_sum(10 + s, col_sum(r["D3"][s].astype(F32)))
        g_attn[s, : 2 * hc, :] = dtn(r["D3"][s, :, : 2 * hc], xs[...]).astype(BF16)
        starts(("attn", 0), ("attn", 1), tag)
        step(("qk", tag))
        grad_v = dtn(r["D3"][s, :, 2 * hc :], xs[...])
        g_attn[s, 2 * hc : 3 * hc, :] = grad_v[:hc].astype(BF16)
        starts(("attn", 2), tag)
        step(("v", tag))

    def input_back(at0):
        at = pl.ds(at0, block)
        return sum(dn(r["D3"][s, at, :], r["Wwa"][s, : plan.qkv_cols, :]) for s in range(2))

    begin("sums")
    ex = exchange(input_back)
    step("dx0")
    for i in range(2):
        at = pl.ds(i * block, block)
        dx = r["DZ"][at, :] + input_back(row(i))
        ex[i].wait_recv()
        r["DZ"][at, :] = dx + rbuf[i].astype(F32)
    r["DXS"][...] = r["DZ"][pl.ds(other, block), :].astype(BF16)
    dx_x = send(r["DXS"], r["dx_far"], "x")
    dx_l = local(r["DZ"].at[pl.ds(mine, block)], r["dx_own"])

    step("dx1")
    step("tail")
    while live:
        for key in list(live):
            advance(key)
    out_x.wait_recv()
    dx_x.wait_recv()
    out_l.wait()
    dx_l.wait()
    done_send(list(pending))


def finish(*refs):
    f_down, f_up, dx_own, dx_far, out = refs[:5]
    g_down, g_up, dx, rows = refs[9:13]
    g_down[...] = f_down[...].astype(F32)
    g_up[...] = f_up[...].astype(F32)
    for src, dst in zip(refs[5:9], refs[13:]):
        dst[...] = src[...].astype(F32)
    own, far = dx_own[...], dx_far[...].astype(F32)
    first = lax.axis_index("tp") < 2
    dx[:, 0, :] = jnp.where(first, own, far)
    dx[:, 1, :] = jnp.where(first, far, own)
    rows[:, 0, :] = out[0]
    rows[:, 1, :] = out[1]


def local(
    inputs,
    lengths,
    w_query,
    b_query,
    w_key,
    w_value,
    b_value,
    w_out,
    b_out,
    norm1_gain,
    norm1_bias,
    w_up,
    b_up,
    w_down,
    b_down,
    norm2_gain,
    norm2_bias,
    cotangent,
):
    block, utts, width = inputs.shape
    dpn = lax.axis_size("dp")
    plan = Plan(block, width, w_query.shape[1], w_up.shape[1], dpn)
    hc, ff, wide = plan.head_cols, plan.ff, plan.wide
    slots, own, heads = plan.slots, plan.own, plan.heads

    xin = jnp.transpose(inputs, (1, 0, 2))
    cin = jnp.transpose(cotangent, (1, 0, 2))

    def rows_of(vectors):
        padded = [jnp.pad(v, (0, wide - v.shape[0])) for v in vectors]
        padded += [jnp.zeros((wide,), F32)] * (8 - len(padded))
        return jnp.stack(padded)

    b3 = jnp.concatenate([b_query, jnp.zeros_like(b_query), b_value])
    svec = rows_of([b3, b_up])
    rvec = rows_of([b_out, norm1_gain, norm1_bias, b_down, norm2_gain, norm2_bias])

    operands = [
        ("xin", xin),
        ("cin", cin),
        ("lens", lengths),
        ("wq", w_query.T),
        ("wk", w_key.T),
        ("wv", w_value.T),
        ("wo", w_out),
        ("wu", w_up),
        ("wd", w_down),
        ("svec", svec),
        ("rvec", rvec),
    ]
    shape_of = jax.ShapeDtypeStruct
    hbm = pl.BlockSpec(memory_space=pl.ANY)
    vmem = pl.BlockSpec(memory_space=pltpu.VMEM)
    smem = pl.BlockSpec(memory_space=pltpu.SMEM)
    outs = [
        ("out", shape_of((2, block, width), BF16), hbm),
        ("dx_own", shape_of((block, width), F32), hbm),
        ("dx_far", shape_of((block, width), BF16), hbm),
        ("vec", shape_of((16, wide), F32), vmem),
    ]
    grads = (
        ("down", ff, width),
        ("up", width, ff),
        ("attn", 4 * hc, width),
    )
    for name, rows, cols in grads:
        outs.append(("F_" + name, shape_of((rows, cols), BF16), vmem))

    def v(name, shape, dtype=BF16):
        return (name, pltpu.VMEM(shape, dtype))

    scratch = [
        v("X", (slots, width)),
        v("Wwa", (2, 4 * hc, width)),
        v("Wwu", (2, width, ff)),
        v("Wwd", (2, ff, width)),
        v("B", (2, 8, wide), F32),
        v("R", (8, wide), F32),
        v("cot", (own, width)),
        v("QP", (2 * heads, slots, 128)),
        v("KP", (2 * heads, slots, 128)),
        v("VP", (2 * heads, slots, 128)),
        v("DC", (2 * heads, slots, 128)),
        v("C", (2, slots, plan.out_cols)),
        v("E", (hc, heads * 128)),
        v("SB", (2, block, width)),
        v("RB", (2, block, width)),
        v("N1", (own, width), F32),
        v("INV", (own, 128), F32),
        v("HB", (slots, width)),
        v("G", (2, slots, ff)),
        v("SL", (2, slots, ff)),
        v("OB", (own, width)),
        v("DZ", (own, width), F32),
        v("DF", (slots, width)),
        v("DA", (slots, width)),
        v("D3", (2, slots, plan.qkv_cols)),
        v("AK", (slots, 128), F32),
        v("AV", (slots, 128), F32),
        v("DXS", (block, width)),
        v("sums", (16, wide), F32),
        v("SR", (2 + plan.bits, 16, wide), F32),
    ]
    for name, rows, cols in grads:
        scratch.append(v("G_" + name, (2, rows, cols)))
    widths = {name: cols for name, _, cols in grads}
    for key, (name, _, rows, order) in plan.streams.items():
        for k, (_, both, n, _) in enumerate(plan.steps(rows, order)):
            scratch.append(v("S_%s_%d_%d" % (*key, k), (both, n, widths[name])))
    scratch += [
        ("ssem", pltpu.SemaphoreType.DMA((192,))),
        ("rsem", pltpu.SemaphoreType.DMA((192,))),
        ("lsem", pltpu.SemaphoreType.DMA((24,))),
    ]
    names = [n for n, _ in operands] + [n for n, _, _ in outs] + [n for n, _ in scratch]
    results = pl.pallas_call(
        functools.partial(layer, plan, names),
        out_shape=[s for _, s, _ in outs],
        in_specs=[smem if n == "lens" else hbm for n, _ in operands],
        out_specs=[s for _, _, s in outs],
        scratch_shapes=[s for _, s in scratch],
        compiler_params=pltpu.CompilerParams(
            collective_id=0, has_side_effects=True, vmem_limit_bytes=63 * 2**20
        ),
        name="encoder_layer",
    )(*[a for _, a in operands])
    got = dict(zip([n for n, _, _ in outs], results))
    first = lax.axis_index("tp") < 2
    vec = got["vec"]
    grad_b_up = jnp.where(first, vec[8], vec[9])[:ff]
    grad_b3 = jnp.where(first, vec[10], vec[11])
    steps = 4

    def tiled(shape, axis=0):
        size = tuple(n // steps if d == axis else n for d, n in enumerate(shape))
        return pl.BlockSpec(size, lambda i: tuple(i if d == axis else 0 for d in range(len(shape))))

    ins = [got[n] for n in ("F_down", "F_up", "dx_own", "dx_far", "out")] + [got["F_attn"]] * 4
    in_specs = [tiled(a.shape, 1 if a.ndim == 3 else 0) for a in ins[:5]]
    in_specs += [
        pl.BlockSpec((hc // steps, width), lambda i, k=k: (k * steps + i, 0)) for k in range(4)
    ]
    out_shapes = [(ff, width), (width, ff)] + [(block, utts, width)] * 2 + [(hc, width)] * 4
    out_types = [F32, F32, F32, BF16] + [F32] * 4
    g_down, g_up, input_grad, outputs, g_query, g_key, g_value, g_out = pl.pallas_call(
        finish,
        grid=(steps,),
        in_specs=in_specs,
        out_specs=[tiled(n) for n in out_shapes],
        out_shape=[shape_of(n, t) for n, t in zip(out_shapes, out_types)],
        compiler_params=pltpu.CompilerParams(vmem_limit_bytes=40 * 2**20),
        name="finish",
    )(*ins)
    return (
        outputs,
        input_grad,
        g_query.T,
        grad_b3[:hc],
        g_key.T,
        g_value.T,
        grad_b3[2 * hc : 3 * hc],
        g_out,
        vec[0, :width],
        vec[1, :width],
        vec[2, :width],
        g_up,
        grad_b_up,
        g_down,
        vec[3, :width],
        vec[4, :width],
        vec[5, :width],
    )


def solution(mesh):
    whole = P()
    rows = P("tp", "dp", None)
    cols = P(None, "tp")
    down = P("tp", None)
    shard = P("tp")
    return jax.shard_map(
        local,
        mesh=mesh,
        in_specs=(
            rows,
            P("dp"),
            cols,
            shard,
            cols,
            cols,
            shard,
            down,
            whole,
            whole,
            whole,
            cols,
            shard,
            down,
            whole,
            whole,
            whole,
            rows,
        ),
        out_specs=(
            rows,
            rows,
            cols,
            shard,
            cols,
            cols,
            shard,
            down,
            whole,
            whole,
            whole,
            cols,
            shard,
            down,
            whole,
            whole,
            whole,
        ),
        check_vma=False,
    )
```

```python
import functools
import math

import jax
import jax.numpy as jnp
from jax import lax
from jax.experimental import pallas as pl
from jax.experimental.pallas import tpu as pltpu
from jax.sharding import PartitionSpec as P

HEAD_DIM = 64
EPS = 1e-05
ROOT_HALF = 0.7071067811865476
DENSITY = 0.3989422804014327
SCALE = 0.125
NEG = -1e30
F32 = jnp.float32
BF16 = jnp.bfloat16


def dn(a, b):
    return lax.dot_general(a, b, (((1,), (0,)), ((), ())), preferred_element_type=F32)


def dnt(a, b):
    return lax.dot_general(a, b, (((1,), (1,)), ((), ())), preferred_element_type=F32)


def dtn(a, b):
    return lax.dot_general(a, b, (((0,), (0,)), ((), ())), preferred_element_type=F32)


def split3(v):
    hi = v.astype(BF16).astype(F32)
    rest = v - hi
    mid = rest.astype(BF16).astype(F32)
    return hi, mid, rest - mid


def mean(v):
    return jnp.mean(v, -1, keepdims=True)


def col_sum(v):
    return jnp.sum(v, 0, keepdims=True)


def chunk_of(n):
    for c in (96, 64, 48, 32, 16):
        if n % c == 0:
            return c
    return n


ORDERS = {
    ('down', 0): [1, 0, 'x', 2],
    ('down', 1): [1, 0, 'x', 2],
    ('down', 2): ['x', 0, 1, 2],
    ('down', 3): [0, 1, 2, 'x'],
    ('up', 0): [0, 1, 'x', 2],
    ('up', 1): ['x', 0, 1, 2],
    ('up', 2): [0, 1, 'x', 2],
    ('up', 3): ['x', 0, 1, 2],
    ('attn', 0): ['x', 0, 1, 2],
    ('attn', 1): ['x', 1, 0, 2],
    ('attn', 2): ['x', 0, 1, 2],
    ('attn', 3): ['x', 0, 1, 2],
}
SCHEDULE = {
    'hidden0': [('down', 2), ('down', 0), ('down', 3)],
    'ctx0': [('up', 1), ('down', 1)],
    'ctx1': [('up', 0)],
    'gout': [('down', 3)],
    ('head', 'o', 0): [('up', 3), ('up', 0), ('up', 2)],
    ('head', 'o', 1): [('down', 2)],
    ('head', 'o', 2): [('attn', 3), ('down', 3), ('up', 0), ('up', 2), ('down', 0), ('down', 2)],
    ('qk', 'o'): [('up', 1)],
    ('v', 'o'): [('down', 3)],
    ('head', 's', 0): [('up', 2), ('down', 1), ('up', 0), ('down', 0), ('up', 1)],
    ('head', 's', 1): [('down', 3), ('up', 3), ('down', 2)],
    ('head', 's', 2): [('up', 0), ('attn', 3), ('up', 2)],
    ('qk', 's'): [('attn', 0), ('down', 0), ('down', 3), ('up', 3)],
    ('v', 's'): [('down', 2)],
    'dx0': [('up', 1), ('up', 0), ('attn', 1), ('attn', 3)],
    'dx1': [('up', 2), 'sums', ('attn', 0), ('up', 3), ('down', 0), ('up', 1)],
    "tail": [('attn', 2), ('down', 2), ('down', 1), ('attn', 1), ('attn', 3), ('up', 2), ('attn', 0), ('up', 3), ('up', 1), ('down', 0), ('attn', 2), 'sums', ('down', 1), ('attn', 1), ('attn', 3), ('attn', 0), ('up', 3), ('attn', 2), 'sums', ('down', 1), ('attn', 1), ('attn', 0), ('attn', 3), ('attn', 2), 'sums', ('attn', 1), ('down', 1), ('attn', 0), ('attn', 2), 'sums', ('attn', 1), ('attn', 2)],
}


class Plan:
    def __init__(self, block, width, head_cols, ff_local, dp):
        self.block = block
        self.slots = 4 * block
        self.own = 2 * block
        self.width = width
        self.head_cols = head_cols
        self.heads = head_cols // HEAD_DIM
        self.ff = ff_local
        self.dp = dp
        self.bits = dp.bit_length() - 1
        self.wide = max(width, ff_local, -(-3 * head_cols // 128) * 128)
        self.qkv_cols = -(-3 * head_cols // 128) * 128
        self.out_cols = -(-head_cols // 128) * 128
        self.streams = {}
        for name, rows in (("down", ff_local), ("up", width), ("attn", 4 * head_cols)):
            for k in range(4):
                n = rows // 4
                self.streams[(name, k)] = (name, k * n, n, self.order((name, k)))

    def order(self, key):
        order = [d for d in ORDERS[key] if d == "x" or d < self.bits]
        return order + list(range(3, self.bits))

    def steps(self, n, order):
        steps, both = [], 2
        for k, dim in enumerate(order):
            if dim == "x":
                both = 1
                steps.append((dim, both, n, False))
                continue
            last = both == 1 and k == len(order) - 1
            halve = not last and (n // 2) % 16 == 0
            if halve:
                n //= 2
            steps.append((dim, both, n, halve))
        return steps


def layer(plan, names, *refs):
    r = dict(zip(names, refs))
    block, slots, own, width = plan.block, plan.slots, plan.own, plan.width
    hc, heads, ff, dpn, bits = plan.head_cols, plan.heads, plan.ff, plan.dp, plan.bits
    dp = lax.axis_index("dp")
    tp = lax.axis_index("tp")
    x = lax.div(tp, 2)
    c = lax.rem(tp, 2)
    ox = 1 - x
    bit = [lax.rem(lax.div(dp, 1 << b), 2) for b in range(bits)]
    part = {b: (dp + (1 << b) * (1 - 2 * bit[b]), tp) for b in range(bits)}
    part["x"] = (dp, lax.rem(tp + 2, 4))
    part["c"] = (dp, tp + 1 - 2 * c)
    mesh_id = pl.DeviceIdType.MESH

    ssem, rsem, lsem = r["ssem"], r["rsem"], r["lsem"]
    count = {"r": 0, "l": 0}
    pending = []

    def send(src, dst, who):
        i = count["r"]
        count["r"] += 1
        copy = pltpu.make_async_remote_copy(
            src_ref=src,
            dst_ref=dst,
            send_sem=ssem.at[i],
            recv_sem=rsem.at[i],
            device_id=part[who],
            device_id_type=mesh_id,
        )
        copy.start()
        pending.append(copy)
        return copy

    def done_send(copies):
        for copy in copies:
            copy.wait_send()
            pending[:] = [p for p in pending if p is not copy]

    def local(src, dst):
        i = count["l"]
        count["l"] += 1
        copy = pltpu.make_async_copy(src, dst, lsem.at[i])
        copy.start()
        return copy

    def mult(v, m=16):
        return pl.multiple_of(v, math.gcd(m, 128))

    def row(i):
        return pl.multiple_of(lax.rem(c * own + i * block, slots), block)

    own0 = pl.multiple_of(c * own, own)
    mine = pl.multiple_of(x * block, block)
    other = pl.multiple_of(ox * block, block)

    xs = r["X"]
    local_a = []
    for k, name in enumerate(("wq", "wk", "wv", "wo")):
        local_a.append(local(r[name], r["Wwa"].at[x, pl.ds(k * hc, hc)]))
    local_x = local(r["inputs"], r["XI"])
    local_c = local(r["cot"], r["CI"])
    vectors = ("bq", "bv", "bu", "bo", "g1", "c1", "bd", "g2", "c2")
    local_v = [local(r[n], r["V" + n]) for n in vectors]
    barrier = pltpu.get_barrier_semaphore()
    for who in part.values():
        pl.semaphore_signal(barrier, inc=1, device_id=who, device_id_type=mesh_id)
    pl.semaphore_wait(barrier, len(part))

    gbits = min(2, bits)
    parts = 1 << gbits
    piece = lax.rem(dp, parts)

    def cut(name, k, of):
        if name == "wa":
            return k * hc, hc // parts, hc // parts
        n = r[name].shape[0] // parts
        return k * n // of, n // of, n

    def weight_x(name, k, of):
        start, size, step_rows = cut(name, k, of)
        src = r[("wq", "wk", "wv", "wo")[k]] if name == "wa" else r[name]
        off = mult(piece * step_rows, 16)
        from_at = pl.ds(off if name == "wa" else mult(off + start, 16), size)
        return send(src.at[from_at], r["W" + name].at[x, pl.ds(mult(off + start, 16), size)], "x")

    def weight_hop(name, k, of):
        start, size, step_rows = cut(name, k, of)
        at = pl.ds(mult(piece * step_rows + start, 16), size)
        dst = r["W" + name].at[ox, at]
        return [send(dst, dst, b) for b in range(gbits)]

    def weight_far(name, k, of):
        if gbits < 2:
            return []
        start, size, step_rows = cut(name, k, of)
        b = k % 2
        o = 1 - b
        from_piece = piece + (1 << o) * (1 - 2 * bit[o])
        at = pl.ds(mult(from_piece * step_rows + start, 16), size)
        dst = r["W" + name].at[ox, at]
        return [send(dst, dst, b)]

    def arrived(copies):
        for copy in copies:
            copy.wait_recv()

    half = block // 2
    wa_x = [weight_x("wa", k, 4) for k in range(4)]
    b_x = [send(r[n], r["O" + n], "x") for n in ("bq", "bv", "bu")]

    def divide(ref):
        even, odd = ref[:, 0, :], ref[:, 1, :]
        return jnp.where(x == 0, even, odd), jnp.where(x == 0, odd, even)

    local_x.wait()
    at_mine = pl.ds(own0 + mine, block)
    own_rows, far_rows = divide(r["XI"])
    r["XO"][...] = far_rows
    xs[at_mine, :] = own_rows
    x_x = []
    for k in range(2):
        src = r["XO"].at[pl.ds(k * half, half)]
        x_x.append(send(src, xs.at[pl.ds(own0 + mine + k * half, half)], "x"))
    late_x = {(name, k): weight_x(name, k, 2) for name in ("wu", "wd") for k in range(2)}
    x_c = [send(xs.at[at_mine], xs.at[at_mine], "c")]
    local_c.wait()
    own_rows, far_rows = divide(r["CI"])
    r["CO"][...] = far_rows
    r["CT"][pl.ds(mine, block), :] = own_rows
    c_x = send(r["CO"], r["CT"].at[pl.ds(mine, block)], "x")
    local_w = [local(r[name], r["W" + name].at[x]) for name in ("wu", "wd")]

    bias = r["B"]
    rep = r["R"]
    lane = lax.broadcasted_iota(jnp.int32, (block, 128), 1)
    valid = r["lens"][x]
    for copy in local_v:
        copy.wait()
    for k, name in enumerate(vectors[3:]):
        rep[k : k + 1, :width] = r["V" + name][...].reshape(1, width)

    def set_bias(s, q, v, u):
        bias[s, 0:1, :] = jnp.zeros((1, plan.wide), F32)
        bias[s, 0:1, :hc] = q[...].reshape(1, hc)
        bias[s, 0:1, 2 * hc : 3 * hc] = v[...].reshape(1, hc)
        bias[s, 1:2, :ff] = u[...].reshape(1, ff)

    set_bias(x, r["Vbq"], r["Vbv"], r["Vbu"])
    pad = plan.out_cols - hc
    if pad:
        for s in range(2):
            r["C"][s, :, hc:] = jnp.zeros((slots, pad), BF16)
    pad3 = plan.qkv_cols - 3 * hc
    if pad3:
        for s in range(2):
            r["D3"][s, :, 3 * hc :] = jnp.zeros((slots, pad3), BF16)

    def project(s, first):
        i = lax.div(first, block)
        at = pl.ds(pl.multiple_of(first, block), block)
        y = dnt(xs[at, :], r["Wwa"][s, : plan.qkv_cols, :]) + bias[s, 0:1, : plan.qkv_cols]
        slot0 = first + block * jnp.where(i == 1, 1, 0) - block * jnp.where(i == 2, 1, 0)
        slot = slot0 + lax.broadcasted_iota(jnp.int32, (block, 128), 0)
        masked = jnp.where(slot < valid, 0.0, NEG)
        real = lane < HEAD_DIM
        k_end = jnp.where(lane == 64, masked, jnp.where(lane < 68, 1.0, 0.0))
        q_end = jnp.where(lane == 64, 1.0, 0.0)
        v_end = jnp.where(lane < 67, 1.0, 0.0)
        for k, (name, end) in enumerate((("QP", q_end), ("KP", k_end), ("VP", v_end))):
            for h in range(heads):
                unit = k * heads + h
                tile = y[:, unit // 2 * 128 : unit // 2 * 128 + 128]
                if unit % 2:
                    tile = pltpu.roll(tile, 64, 1)
                if k == 0:
                    tile = tile * SCALE
                r[name][s * heads + h, at, :] = jnp.where(real, tile, end).astype(BF16)

    early = [own0 + mine, (1 - c) * own + mine]
    late = [own0 + other, (1 - c) * own + other]

    for copy in local_a:
        copy.wait()
    project(x, early[0])
    x_c.pop().wait_recv()
    project(x, early[1])
    wa_h, wa_f = [], []
    for k in range(4):
        wa_x[k].wait_recv()
        wa_h.append(weight_hop("wa", k, 4))
    for k in range(4):
        arrived(wa_h[k])
        wa_f += weight_far("wa", k, 4)
    arrived(b_x)
    set_bias(ox, r["Obq"], r["Obv"], r["Obu"])
    x_x[0].wait_recv()
    at_other = [pl.ds(own0 + other + k * half, half) for k in range(2)]
    x_c.append(send(xs.at[at_other[0]], xs.at[at_other[0]], "c"))
    arrived(wa_f)
    project(ox, early[0])
    project(ox, early[1])
    x_x[1].wait_recv()
    x_c.append(send(xs.at[at_other[1]], xs.at[at_other[1]], "c"))
    project(x, late[0])
    project(ox, late[0])
    arrived(x_c)
    project(x, late[1])
    project(ox, late[1])
    for copy in local_w:
        copy.wait()

    def attend(s, h):
        hs = s * heads + h
        tiles = [slice(i * block, (i + 1) * block) for i in range(4)]
        queries = [r["QP"][hs, at, :] for at in tiles]
        scores = [dnt(q, r["KP"][hs]) for q in queries]
        done = []
        for score in scores:
            top = jnp.max(score, -1, keepdims=True)
            done.append((dn(jnp.exp(score - top).astype(BF16), r["VP"][hs]), top))
        for at, q, (o, top) in zip(tiles, queries, done):
            total = o[:, HEAD_DIM : HEAD_DIM + 1]
            r["C"][s, at, h * HEAD_DIM : (h + 1) * HEAD_DIM] = (
                o[:, :HEAD_DIM] / total
            ).astype(BF16)
            hi, mid, low = split3(-(top + jnp.log(total)))
            ends = jnp.where(lane == 66, mid, jnp.where(lane == 67, low, q.astype(F32)))
            r["QP"][hs, at, :] = jnp.where(lane == 65, hi, ends).astype(BF16)

    late_h, late_f = {}, {}

    def hop(name, k):
        late_x[name, k].wait_recv()
        late_h[name, k] = weight_hop(name, k, 2)

    def far(name, k):
        arrived(late_h[name, k])
        late_f[name, k] = weight_far(name, k, 2)

    progress = {
        (0, heads - 2): [(hop, "wu", 1)],
        (0, heads - 1): [(far, "wu", 0)],
        (1, 0): [(hop, "wd", 0)],
        (1, heads - 2): [(far, "wu", 1)],
        (1, heads - 1): [(hop, "wd", 1)],
    }
    if heads < 3:
        progress = {(1, heads - 1): [(hop, "wu", 1), (far, "wu", 0), (hop, "wd", 0)]}
        progress[1, heads - 1] += [(far, "wu", 1), (hop, "wd", 1)]
    hop("wu", 0)
    for k, s in enumerate((x, ox)):
        for h in range(heads):
            attend(s, h)
            for move, name, chunk in progress.get((k, h), ()):
                move(name, chunk)

    sbuf, rbuf = r["SB"], r["RB"]

    def exchange(partial):
        copies = []
        for i in range(2):
            sbuf[i] = partial(row(2 + i)).astype(BF16)
            copies.append(send(sbuf.at[i], rbuf.at[i], "c"))
        return copies

    def share(buf, i):
        at = pl.ds(row(i), block)
        return send(buf.at[at], buf.at[at], "c")

    sums = r["sums"]
    sums[...] = jnp.zeros_like(sums)

    def add_sum(k, v, n=None):
        n = v.shape[-1]
        sums[pl.ds(k, 1), :n] = sums[pl.ds(k, 1), :n] + v

    def attn_out(at0):
        at = pl.ds(at0, block)
        return sum(dn(r["C"][s, at, :hc], r["Wwa"][s, 3 * hc :, :]) for s in range(2))

    ex = exchange(attn_out)
    hb_c = []
    for i in range(2):
        a = attn_out(row(i)) + rep[0:1, :width]
        ex[i].wait_recv()
        z = xs[pl.ds(row(i), block), :].astype(F32) + a + rbuf[i].astype(F32)
        z = z - mean(z)
        inv = lax.rsqrt(mean(z * z) + EPS)
        n1 = z * inv
        at = pl.ds(i * block, block)
        r["N1"][at, :] = n1
        r["INV"][at, :] = jnp.broadcast_to(inv, (block, 128))
        r["HB"][pl.ds(row(i), block), :] = (n1 * rep[1:2, :width] + rep[2:3, :width]).astype(BF16)
        hb_c.append(share(r["HB"], i))
    done_send(ex)

    def up(s, first, last):
        @pl.loop(first, last)
        def _(i):
            at = pl.ds(row(i), block)
            u = dn(r["HB"][at, :], r["Wwu"][s]) + bias[s, 1:2, :ff]
            cdf = 0.5 * (1.0 + lax.erf(u * ROOT_HALF))
            r["G"][s, at, :] = (u * cdf).astype(BF16)
            r["SL"][s, at, :] = (cdf + u * (DENSITY * jnp.exp(-0.5 * u * u))).astype(BF16)

    far("wd", 0)
    up(x, 0, 2)
    arrived(hb_c)
    far("wd", 1)
    up(x, 2, 4)
    arrived(late_f["wu", 0] + late_f["wu", 1])
    up(ox, 0, 4)

    def ffn_out(at0):
        at = pl.ds(at0, block)
        return dn(r["G"][0, at, :], r["Wwd"][0]) + dn(r["G"][1, at, :], r["Wwd"][1])

    arrived(late_f["wd", 0] + late_f["wd", 1])
    ex = exchange(ffn_out)
    c_x.wait_recv()
    df_c = []
    for i in range(2):
        at = pl.ds(i * block, block)
        hidden = r["N1"][at, :] * rep[1:2, :width] + rep[2:3, :width]
        f = ffn_out(row(i)) + rep[3:4, :width]
        ex[i].wait_recv()
        z = hidden + f + rbuf[i].astype(F32)
        z = z - mean(z)
        inv = lax.rsqrt(mean(z * z) + EPS)
        n2 = z * inv
        r["OB"][at, :] = (n2 * rep[4:5, :width] + rep[5:6, :width]).astype(BF16)
        dy = r["CT"][at, :].astype(F32)
        add_sum(4, col_sum(dy * n2))
        add_sum(5, col_sum(dy))
        e2 = dy * rep[4:5, :width]
        dz = inv * (e2 - mean(e2) - n2 * mean(e2 * n2))
        r["DZ"][at, :] = dz
        df = dz.astype(BF16)
        add_sum(3, col_sum(df.astype(F32)))
        r["DF"][pl.ds(row(i), block), :] = df
        df_c.append(share(r["DF"], i))
    done_send(ex)
    out_x = send(r["OB"].at[pl.ds(other, block)], r["out"].at[x], "x")
    out_l = local(r["OB"].at[pl.ds(mine, block)], r["out"].at[x])

    def adder(dst, d, row0, src, sd, n):
        size = chunk_of(n)

        @pl.loop(0, n // size)
        def _(i):
            at = pl.ds(mult(row0 + i * size), size)
            got = src[sd, pl.ds(mult(i * size), size), :].astype(F32)
            dst[d, at, :] = (dst[d, at, :].astype(F32) + got).astype(BF16)

    def stream(key):
        name, row0, n, order = plan.streams[key]
        grad, final = r["G_" + name], r["F_" + name]
        both, halved = True, []
        for k, (dim, _, n, halve) in enumerate(plan.steps(n, order)):
            got = r["S_%s_%d_%d" % (*key, k)]
            if dim == "x":
                copy = send(grad.at[ox, pl.ds(row0, n)], got.at[0], "x")
                both = False
            else:
                sent = row0
                if halve:
                    halved.append(dim)
                    sent = mult(row0 + (1 - bit[dim]) * n)
                    row0 = mult(row0 + bit[dim] * n)
                at = pl.ds(sent, n)
                copy = send(
                    grad.at[:, at] if both else grad.at[x, at], got if both else got.at[0], dim
                )
            yield
            copy.wait_recv()
            if dim != "x" and not halve:
                done_send([copy])
            if both:
                adder(grad, 0, row0, got, 0, n)
                adder(grad, 1, row0, got, 1, n)
            else:
                adder(grad, x, row0, got, 0, n)
        first = True
        keep = local(grad.at[x, pl.ds(row0, n)], final.at[pl.ds(row0, n)])
        for dim in reversed(halved):
            at = pl.ds(row0, n)
            copy = send(grad.at[x, at] if first else final.at[at], final.at[at], dim)
            first = False
            yield
            copy.wait_recv()
            if keep is not None:
                keep.wait()
                keep = None
            row0 = mult(row0 - bit[dim] * n)
            n *= 2
        if keep is not None:
            keep.wait()

    live = {}

    def advance(key):
        try:
            next(live[key])
        except StopIteration:
            del live[key]

    def begin(key):
        live[key] = sums_stream() if key == "sums" else stream(key)
        advance(key)

    def starts(*keys):
        for key in keys[:-1]:
            if (plan.streams[key][3][0] == "x") == (keys[-1] == "o"):
                begin(key)

    def step(name):
        for key in SCHEDULE.get(name, ()):
            if key in live:
                advance(key)

    def sums_stream():
        for k, who in enumerate(["c", "x"] + list(range(bits))):
            n = 8 if who == "c" else 16
            copy = send(sums.at[pl.ds(0, n)], r["SR"].at[k, pl.ds(0, n)], who)
            yield
            copy.wait_recv()
            done_send([copy])
            sums[0:n, :] = sums[0:n, :] + r["SR"][k, 0:n, :]
        r["vec"][...] = sums[...]

    def slope(first, last):
        @pl.loop(first, last)
        def _(i):
            at = pl.ds(row(i), block)
            for s in range(2):
                da = dnt(r["DF"][at, :], r["Wwd"][s])
                du = da * r["SL"][s, at, :].astype(F32)
                add_sum(8 + s, col_sum(du))
                r["SL"][s, at, :] = du.astype(BF16)

    def weight_grad(name, left, right):
        dst = r["G_" + name]
        n = dst.shape[1] // 2
        for s, tag in ((ox, "o"), (x, "s")):
            for j in range(2):
                at = slice(j * n, (j + 1) * n)
                dst[s, at, :] = dtn(left(s, at), right(s)).astype(BF16)
                starts((name, 2 * j), (name, 2 * j + 1), tag)
                step((name, tag, j))

    slope(0, 2)
    arrived(df_c)
    weight_grad("down", lambda s, at: r["G"][s, :, at], lambda s: r["DF"][...])
    slope(2, 4)
    step("slope")
    weight_grad("up", lambda s, at: r["HB"][:, at], lambda s: r["SL"][s])

    def hidden_back(at0):
        at = pl.ds(at0, block)
        return dnt(r["SL"][0, at, :], r["Wwu"][0]) + dnt(r["SL"][1, at, :], r["Wwu"][1])

    ex = exchange(hidden_back)
    step("hidden0")
    da_c = []
    for i in range(2):
        at = pl.ds(i * block, block)
        dh = r["DZ"][at, :] + hidden_back(row(i))
        ex[i].wait_recv()
        dh = dh + rbuf[i].astype(F32)
        n1 = r["N1"][at, :]
        add_sum(1, col_sum(dh * n1))
        add_sum(2, col_sum(dh))
        e1 = dh * rep[1:2, :width]
        dz = r["INV"][at, 0:1] * (e1 - mean(e1) - n1 * mean(e1 * n1))
        r["DZ"][at, :] = dz
        da = dz.astype(BF16)
        add_sum(0, col_sum(da.astype(F32)))
        r["DA"][pl.ds(row(i), block), :] = da
        da_c.append(share(r["DA"], i))
    done_send(ex)
    step("hidden1")

    rows_e = lax.broadcasted_iota(jnp.int32, (hc, heads * 128), 0)
    lanes_e = lax.broadcasted_iota(jnp.int32, (hc, heads * 128), 1)
    spot = lanes_e - lax.div(rows_e, HEAD_DIM) * 128
    r["E"][...] = jnp.where((spot >= 64) & (spot < 67), -1.0, 0.0).astype(BF16)

    def context_back(first, last):
        @pl.loop(first, last)
        def _(i):
            at = pl.ds(row(i), block)
            for s in range(2):
                dc = dnt(r["DA"][at, :], r["Wwa"][s, 3 * hc :, :]).astype(BF16).astype(F32)
                prod = dc * r["C"][s, at, :hc].astype(F32)
                prod_hi = prod.astype(BF16)
                prod_lo = (prod - prod_hi.astype(F32)).astype(BF16)
                ends = dn(prod_hi, r["E"][...]) + dn(prod_lo, r["E"][...])
                for h in range(heads):
                    end = ends[:, h * 128 : h * 128 + 128]
                    if 2 * h + 2 <= 2 * heads - heads % 2:
                        tile = dc[:, h // 2 * 128 : h // 2 * 128 + 128]
                        if h % 2:
                            tile = pltpu.roll(tile, 64, 1)
                    else:
                        tile = jnp.concatenate([dc[:, h * 64 :], end[:, 64:]], 1)
                    tile = jnp.where(lane < 64, tile, end)
                    hi, mid, low = split3(tile)
                    tile = jnp.where(lane == 65, mid, jnp.where(lane == 66, low, hi))
                    r["DC"][s * heads + h, at, :] = tile.astype(BF16)

    context_back(0, 2)
    step("ctx0")
    arrived(da_c)
    context_back(2, 4)
    step("ctx1")
    for s, tag in ((ox, "o"), (x, "s")):
        r["G_attn"][s, 3 * hc :, :] = dtn(r["C"][s], r["DA"][...])[:hc].astype(BF16)
        starts(("attn", 3), tag)
    step("gout")

    def head_back(s, h):
        hs = s * heads + h
        keys, values = r["KP"].at[hs], r["VP"].at[hs]
        r["KT"][...] = keys[...].T
        tiles = [slice(i * block, (i + 1) * block) for i in range(4)]
        queries = [r["QP"][hs, at, :] for at in tiles]
        tangents = [r["DC"][hs, at, :] for at in tiles]
        scores = [dnt(keys[...], q) for q in queries]
        centred = [dnt(values[...], dc) for dc in tangents]
        dk = dv = 0.0
        for at, q, dc, score, middle in zip(tiles, queries, tangents, scores, centred):
            p = jnp.exp(score)
            ds = (p * middle).astype(BF16)
            dv = dv + dn(p.astype(BF16), dc)
            dk = dk + dn(ds, q)
            dq = dn(r["KT"][...], ds).T
            r["D3"][s, at, h * HEAD_DIM : (h + 1) * HEAD_DIM] = (
                dq[:, :HEAD_DIM] * SCALE
            ).astype(BF16)
        lo = hc + h * HEAD_DIM
        r["D3"][s, :, lo : lo + HEAD_DIM] = dk[:, :HEAD_DIM].astype(BF16)
        lo += hc
        r["D3"][s, :, lo : lo + HEAD_DIM] = dv[:, :HEAD_DIM].astype(BF16)

    g_attn = r["G_attn"]
    for s, tag in ((ox, "o"), (x, "s")):
        for h in range(heads):
            head_back(s, h)
            step(("head", tag, h))
        add_sum(10 + s, col_sum(r["D3"][s].astype(F32)))
        g_attn[s, : 2 * hc, :] = dtn(r["D3"][s, :, : 2 * hc], xs[...]).astype(BF16)
        starts(("attn", 0), ("attn", 1), tag)
        step(("qk", tag))
        grad_v = dtn(r["D3"][s, :, 2 * hc :], xs[...])
        g_attn[s, 2 * hc : 3 * hc, :] = grad_v[:hc].astype(BF16)
        starts(("attn", 2), tag)
        step(("v", tag))

    def input_back(at0):
        at = pl.ds(at0, block)
        return sum(dn(r["D3"][s, at, :], r["Wwa"][s, : plan.qkv_cols, :]) for s in range(2))

    begin("sums")
    ex = exchange(input_back)
    step("dx0")
    for i in range(2):
        at = pl.ds(i * block, block)
        dx = r["DZ"][at, :] + input_back(row(i))
        ex[i].wait_recv()
        r["DZ"][at, :] = dx + rbuf[i].astype(F32)
    r["DXS"][...] = r["DZ"][pl.ds(other, block), :].astype(BF16)
    dx_x = send(r["DXS"], r["dx_far"], "x")
    dx_l = local(r["DZ"].at[pl.ds(mine, block)], r["dx_own"])

    step("dx1")
    step("tail")
    while live:
        for key in list(live):
            advance(key)
    out_x.wait_recv()
    dx_x.wait_recv()
    out_l.wait()
    dx_l.wait()
    done_send(list(pending))


def finish(names, *refs):
    r = dict(zip(names, refs))
    sem = r["sem"]
    used = []

    def copy(src, dst):
        made = pltpu.make_async_copy(src, dst, sem.at[len(used)])
        made.start()
        used.append(made)
        return made

    first = lax.axis_index("tp") < 2
    inner = ("out", "dx_own", "dx_far", "F_down", "F_up", "F_attn", "vec")
    got = {n: copy(r[n], r["i_" + n]) for n in inner}
    loads = len(used)
    got["out"].wait()
    for k in range(2):
        r["o_rows"][:, k, :] = r["i_out"][k]
    copy(r["o_rows"], r["rows"])
    got["dx_own"].wait()
    got["dx_far"].wait()
    own, far = r["i_dx_own"][...], r["i_dx_far"][...].astype(F32)
    r["o_dx"][:, 0, :] = jnp.where(first, own, far)
    r["o_dx"][:, 1, :] = jnp.where(first, far, own)
    copy(r["o_dx"], r["dx"])
    hc = r["g_query"].shape[0]
    targets = {"F_down": ["g_down"], "F_up": ["g_up"]}
    targets["F_attn"] = ["g_query", "g_key", "g_value", "g_out"]
    for n, outs in targets.items():
        got[n].wait()
        rows = r[n].shape[0] // 4
        for k in range(4):
            at = pl.ds(k * rows, rows)
            r["o_" + n][at, :] = r["i_" + n][at, :].astype(F32)
            target = r[outs[k]] if len(outs) > 1 else r[outs[0]].at[at]
            copy(r["o_" + n].at[at], target)
    got["vec"].wait()
    vec = r["i_vec"]
    width = r["s_bo"].shape[0]
    for k, n in enumerate(("bo", "g1", "c1", "bd", "g2", "c2")):
        r["s_" + n][...] = vec[k, :width]
    ff = r["s_bu"].shape[0]
    r["s_bu"][...] = jnp.where(first, vec[8, :ff], vec[9, :ff])
    b3 = jnp.where(first, vec[10:11, :], vec[11:12, :])
    r["s_bq"][...] = b3[:, :hc].reshape(hc)
    r["s_bv"][...] = b3[:, 2 * hc : 3 * hc].reshape(hc)
    for made in used[loads:]:
        made.wait()


def local(
    inputs,
    lengths,
    w_query,
    b_query,
    w_key,
    w_value,
    b_value,
    w_out,
    b_out,
    norm1_gain,
    norm1_bias,
    w_up,
    b_up,
    w_down,
    b_down,
    norm2_gain,
    norm2_bias,
    cotangent,
):
    block, utts, width = inputs.shape
    dpn = lax.axis_size("dp")
    plan = Plan(block, width, w_query.shape[1], w_up.shape[1], dpn)
    hc, ff, wide = plan.head_cols, plan.ff, plan.wide
    slots, own, heads = plan.slots, plan.own, plan.heads


    operands = [
        ("inputs", inputs),
        ("cot", cotangent),
        ("lens", lengths),
        ("wq", w_query.T),
        ("wk", w_key.T),
        ("wv", w_value.T),
        ("wo", w_out),
        ("wu", w_up),
        ("wd", w_down),
        ("bq", b_query),
        ("bv", b_value),
        ("bu", b_up),
        ("bo", b_out),
        ("g1", norm1_gain),
        ("c1", norm1_bias),
        ("bd", b_down),
        ("g2", norm2_gain),
        ("c2", norm2_bias),
    ]
    shape_of = jax.ShapeDtypeStruct
    hbm = pl.BlockSpec(memory_space=pl.ANY)
    vmem = pl.BlockSpec(memory_space=pltpu.VMEM)
    smem = pl.BlockSpec(memory_space=pltpu.SMEM)
    outs = [
        ("out", shape_of((2, block, width), BF16), hbm),
        ("dx_own", shape_of((block, width), F32), hbm),
        ("dx_far", shape_of((block, width), BF16), hbm),
        ("vec", shape_of((16, wide), F32), vmem),
    ]
    grads = (
        ("down", ff, width),
        ("up", width, ff),
        ("attn", 4 * hc, width),
    )
    for name, rows, cols in grads:
        outs.append(("F_" + name, shape_of((rows, cols), BF16), hbm))

    def v(name, shape, dtype=BF16):
        return (name, pltpu.VMEM(shape, dtype))

    scratch = [
        v("X", (slots, width)),
        v("Wwa", (2, 4 * hc, width)),
        v("Wwu", (2, width, ff)),
        v("Wwd", (2, ff, width)),
        v("B", (2, 8, wide), F32),
        *(v("V" + n, a.shape, F32) for n, a in operands[-9:]),
        v("Obq", (hc,), F32),
        v("Obv", (hc,), F32),
        v("Obu", (ff,), F32),
        v("R", (8, wide), F32),
        v("XI", (block, utts, width)),
        v("CI", (block, utts, width)),
        v("XO", (block, width)),
        v("CO", (block, width)),
        v("CT", (own, width)),
        v("QP", (2 * heads, slots, 128)),
        v("KP", (2 * heads, slots, 128)),
        v("VP", (2 * heads, slots, 128)),
        v("DC", (2 * heads, slots, 128)),
        v("C", (2, slots, plan.out_cols)),
        v("E", (hc, heads * 128)),
        v("SB", (2, block, width)),
        v("RB", (2, block, width)),
        v("N1", (own, width), F32),
        v("INV", (own, 128), F32),
        v("HB", (slots, width)),
        v("G", (2, slots, ff)),
        v("SL", (2, slots, ff)),
        v("OB", (own, width)),
        v("DZ", (own, width), F32),
        v("DF", (slots, width)),
        v("DA", (slots, width)),
        v("D3", (2, slots, plan.qkv_cols)),
        v("KT", (128, slots)),
        v("DXS", (block, width)),
        v("sums", (16, wide), F32),
        v("SR", (2 + plan.bits, 16, wide), F32),
    ]
    for name, rows, cols in grads:
        scratch.append(v("G_" + name, (2, rows, cols)))
    widths = {name: cols for name, _, cols in grads}
    for key, (name, _, rows, order) in plan.streams.items():
        for k, (_, both, n, _) in enumerate(plan.steps(rows, order)):
            scratch.append(v("S_%s_%d_%d" % (*key, k), (both, n, widths[name])))
    scratch += [
        ("ssem", pltpu.SemaphoreType.DMA((192,))),
        ("rsem", pltpu.SemaphoreType.DMA((192,))),
        ("lsem", pltpu.SemaphoreType.DMA((48,))),
    ]
    names = [n for n, _ in operands] + [n for n, _, _ in outs] + [n for n, _ in scratch]
    results = pl.pallas_call(
        functools.partial(layer, plan, names),
        out_shape=[s for _, s, _ in outs],
        in_specs=[smem if n == "lens" else hbm for n, _ in operands],
        out_specs=[s for _, _, s in outs],
        scratch_shapes=[s for _, s in scratch],
        compiler_params=pltpu.CompilerParams(
            collective_id=0, has_side_effects=True, vmem_limit_bytes=63 * 2**20
        ),
        name="encoder_layer",
    )(*[a for _, a in operands])
    got = dict(zip([n for n, _, _ in outs], results))
    inner = [got[n] for n in ("out", "dx_own", "dx_far", "F_down", "F_up", "F_attn", "vec")]
    inner_names = ["out", "dx_own", "dx_far", "F_down", "F_up", "F_attn", "vec"]
    frames = (block, utts, width)
    final = [("g_down", (ff, width), F32), ("g_up", (width, ff), F32)]
    final += [("dx", frames, F32), ("rows", frames, BF16)]
    final += [(n, (hc, width), F32) for n in ("g_query", "g_key", "g_value", "g_out")]
    small = [("s_" + n, (width,)) for n in ("bo", "g1", "c1", "bd", "g2", "c2")]
    small += [("s_bu", (ff,)), ("s_bq", (hc,)), ("s_bv", (hc,))]
    buffers = [("i_" + n, a.shape, a.dtype) for n, a in zip(inner_names, inner)]
    buffers += [("o_rows", frames, BF16), ("o_dx", frames, F32)]
    buffers += [("o_" + n, got[n].shape, F32) for n in ("F_down", "F_up", "F_attn")]
    labels = inner_names + [n for n, _, _ in final] + [n for n, _ in small]
    labels += [n for n, _, _ in buffers] + ["sem"]
    results = pl.pallas_call(
        functools.partial(finish, labels),
        in_specs=[hbm] * len(inner),
        out_specs=[hbm] * len(final) + [vmem] * len(small),
        out_shape=[shape_of(n, t) for _, n, t in final] + [shape_of(n, F32) for _, n in small],
        scratch_shapes=[pltpu.VMEM(n, t) for _, n, t in buffers]
        + [pltpu.SemaphoreType.DMA((32,))],
        compiler_params=pltpu.CompilerParams(vmem_limit_bytes=60 * 2**20),
        name="finish",
    )(*inner)
    g_down, g_up, input_grad, outputs, g_query, g_key, g_value, g_out = results[:8]
    g_bo, g_g1, g_c1, g_bd, g_g2, g_c2, g_bu, g_bq, g_bv = results[8:]
    return (
        outputs,
        input_grad,
        g_query.T,
        g_bq,
        g_key.T,
        g_value.T,
        g_bv,
        g_out,
        g_bo,
        g_g1,
        g_c1,
        g_up,
        g_bu,
        g_down,
        g_bd,
        g_g2,
        g_c2,
    )


def solution(mesh):
    whole = P()
    rows = P("tp", "dp", None)
    cols = P(None, "tp")
    down = P("tp", None)
    shard = P("tp")
    return jax.shard_map(
        local,
        mesh=mesh,
        in_specs=(
            rows,
            P("dp"),
            cols,
            shard,
            cols,
            cols,
            shard,
            down,
            whole,
            whole,
            whole,
            cols,
            shard,
            down,
            whole,
            whole,
            whole,
            rows,
        ),
        out_specs=(
            rows,
            rows,
            cols,
            shard,
            cols,
            cols,
            shard,
            down,
            whole,
            whole,
            whole,
            cols,
            shard,
            down,
            whole,
            whole,
            whole,
        ),
        check_vma=False,
    )
```

```python
import functools
import math

import jax
import jax.numpy as jnp
from jax import lax
from jax.experimental import pallas as pl
from jax.experimental.pallas import tpu as pltpu
from jax.sharding import PartitionSpec as P

HEAD_DIM = 64
EPS = 1e-05
ROOT_HALF = 0.7071067811865476
DENSITY = 0.3989422804014327
SCALE = 0.125
NEG = -1e30
F32 = jnp.float32
BF16 = jnp.bfloat16


def dn(a, b):
    return lax.dot_general(a, b, (((1,), (0,)), ((), ())), preferred_element_type=F32)


def dnt(a, b):
    return lax.dot_general(a, b, (((1,), (1,)), ((), ())), preferred_element_type=F32)


def dtn(a, b):
    return lax.dot_general(a, b, (((0,), (0,)), ((), ())), preferred_element_type=F32)


def split3(v):
    hi = v.astype(BF16).astype(F32)
    rest = v - hi
    mid = rest.astype(BF16).astype(F32)
    return hi, mid, rest - mid


def mean(v):
    return jnp.mean(v, -1, keepdims=True)


def col_sum(v):
    return jnp.sum(v, 0, keepdims=True)


def chunk_of(n):
    for c in (96, 64, 48, 32, 16):
        if n % c == 0:
            return c
    return n


ORDERS = {
    ('down', 0): [0, 1, 2, 'x'],
    ('down', 1): [1, 0, 'x', 2],
    ('down', 2): [1, 0, 'x', 2],
    ('down', 3): ['x', 0, 1, 2],
    ('up', 0): [0, 1, 'x', 2],
    ('up', 1): [0, 'x', 1, 2],
    ('up', 2): ['x', 0, 1, 2],
    ('up', 3): ['x', 0, 1, 2],
    ('attn', 0): ['x', 0, 1, 2],
    ('attn', 1): ['x', 0, 1, 2],
    ('attn', 2): ['x', 0, 1, 2],
    ('attn', 3): [1, 0, 'x', 2],
}
SCHEDULE = {
    'hidden0': [('down', 1), ('down', 0)],
    'hidden1': [('down', 3)],
    'ctx0': [('up', 0), ('down', 2)],
    'ctx1': [('down', 0), ('up', 2)],
    ('head', 'o', 0): [('up', 0), ('up', 1)],
    ('head', 'o', 1): [('up', 0), ('up', 3), ('down', 1), ('down', 3), ('down', 0)],
    ('head', 'o', 2): [('down', 2), ('up', 1), ('down', 1), ('attn', 3)],
    ('qk', 'o'): [('up', 0), ('down', 3), ('down', 2), ('up', 2), ('down', 0), ('up', 1)],
    ('head', 's', 0): [('up', 0), ('up', 3), ('down', 1)],
    ('head', 's', 1): [('down', 3), ('attn', 3)],
    ('head', 's', 2): [('up', 0), ('down', 2), ('up', 2), ('down', 1), ('down', 0)],
    ('qk', 's'): [('up', 3), ('attn', 1), ('up', 1), ('down', 2), ('down', 3), ('attn', 0)],
    'dx0': [('up', 2), ('down', 0)],
    'dx1': [('attn', 1), ('up', 3), ('attn', 2), ('down', 1), ('attn', 3), ('up', 1), 'sums'],
    "tail": [('down', 3), ('down', 2), ('attn', 0), ('up', 2), ('attn', 1), ('attn', 2), ('up', 3), 'sums', ('attn', 3), ('up', 1), ('attn', 0), ('attn', 1), ('up', 2), ('attn', 2), ('attn', 0), ('up', 3), ('attn', 1), 'sums', ('attn', 2), ('attn', 3), ('attn', 0), 'sums', ('attn', 1), ('attn', 2), ('attn', 0), ('attn', 3), 'sums', ('attn', 2)],
}


class Plan:
    def __init__(self, block, width, head_cols, ff_local, dp):
        self.block = block
        self.slots = 4 * block
        self.own = 2 * block
        self.width = width
        self.head_cols = head_cols
        self.heads = head_cols // HEAD_DIM
        self.ff = ff_local
        self.dp = dp
        self.bits = dp.bit_length() - 1
        self.wide = max(width, ff_local, -(-3 * head_cols // 128) * 128)
        self.qkv_cols = -(-3 * head_cols // 128) * 128
        self.out_cols = -(-head_cols // 128) * 128
        self.streams = {}
        for name, rows in (("down", ff_local), ("up", width), ("attn", 4 * head_cols)):
            for k in range(4):
                n = rows // 4
                self.streams[(name, k)] = (name, k * n, n, self.order((name, k)))

    def order(self, key):
        order = [d for d in ORDERS[key] if d == "x" or d < self.bits]
        return order + list(range(3, self.bits))

    def steps(self, n, order):
        steps, both = [], 2
        for k, dim in enumerate(order):
            if dim == "x":
                both = 1
                steps.append((dim, both, n, False))
                continue
            last = both == 1 and k == len(order) - 1
            halve = not last and (n // 2) % 16 == 0
            if halve:
                n //= 2
            steps.append((dim, both, n, halve))
        return steps


    def x_first(self, key):
        return self.streams[key][3][0] == "x"

    def moves(self):
        events = []

        def point(name, *keys, tags="os"):
            events.append((name, [k for k in keys if ("o" if self.x_first(k) else "s") in tags]))

        for name in ("down", "up"):
            for j in range(2):
                for tag in "os":
                    point((name, tag, j), (name, 2 * j), (name, 2 * j + 1), tags=tag)
            if name == "down":
                point("slope")
        for name in ("hidden0", "hidden1", "ctx0", "ctx1"):
            point(name)
        point("gout", ("attn", 3))
        for tag in "os":
            for h in range(self.heads):
                point(("head", tag, h))
            point(("qk", tag), ("attn", 0), ("attn", 1), tags=tag)
            point(("v", tag), ("attn", 2), tags=tag)
        events += [("dx0", ["sums"]), ("dx1", []), ("tail", [])]
        total = {"sums": 3 + self.bits}
        for key, (_, _, n, order) in self.streams.items():
            steps = self.steps(n, order)
            total[key] = 1 + len(steps) + sum(halve for _, _, _, halve in steps)
        at, moves = {}, {}
        for name, begun in events:
            moves[name] = [(key, 0) for key in begun]
            at.update({key: 1 for key in begun})
            for key in SCHEDULE.get(name, ()):
                if key in at and at[key] < total[key]:
                    moves[name].append((key, at[key]))
                    at[key] += 1
        while any(at[key] < total[key] for key in at):
            for key in at:
                if at[key] < total[key]:
                    moves["tail"].append((key, at[key]))
                    at[key] += 1
        return moves


def layer(plan, names, *refs):
    r = dict(zip(names, refs))
    block, slots, own, width = plan.block, plan.slots, plan.own, plan.width
    hc, heads, ff, dpn, bits = plan.head_cols, plan.heads, plan.ff, plan.dp, plan.bits
    dp = lax.axis_index("dp")
    tp = lax.axis_index("tp")
    x = lax.div(tp, 2)
    c = lax.rem(tp, 2)
    ox = 1 - x
    bit = [lax.rem(lax.div(dp, 1 << b), 2) for b in range(bits)]
    part = {b: (dp + (1 << b) * (1 - 2 * bit[b]), tp) for b in range(bits)}
    part["x"] = (dp, lax.rem(tp + 2, 4))
    part["c"] = (dp, tp + 1 - 2 * c)
    mesh_id = pl.DeviceIdType.MESH

    ssem, rsem, lsem = r["ssem"], r["rsem"], r["lsem"]
    count = {"r": 0, "l": 0}
    pending = []

    def take(n):
        count["r"] += n
        return count["r"] - n

    def remote(src, dst, i, who):
        return pltpu.make_async_remote_copy(
            src_ref=src,
            dst_ref=dst,
            send_sem=ssem.at[i],
            recv_sem=rsem.at[i],
            device_id=part[who],
            device_id_type=mesh_id,
        )

    def prepare(src, dst, who, keep=True):
        copy = remote(src, dst, take(1), who)
        if keep:
            pending.append(copy)
        return copy

    def send(src, dst, who):
        copy = prepare(src, dst, who)
        copy.start()
        return copy

    def local_prepare(src, dst):
        i = count["l"]
        count["l"] += 1
        return pltpu.make_async_copy(src, dst, lsem.at[i])

    def local(src, dst):
        copy = local_prepare(src, dst)
        copy.start()
        return copy

    def mult(v, m=16):
        return pl.multiple_of(v, math.gcd(m, 128))

    def row(i):
        return pl.multiple_of(lax.rem(c * own + i * block, slots), block)

    own0 = pl.multiple_of(c * own, own)
    mine = pl.multiple_of(x * block, block)
    other = pl.multiple_of(ox * block, block)

    xs = r["X"]
    local_a = []
    for k, name in enumerate(("wq", "wk", "wv", "wo")):
        local_a.append(local(r[name], r["Wwa"].at[x, pl.ds(k * hc, hc)]))
    local_x = local(r["inputs"], r["XI"])
    local_c = local(r["cot"], r["CI"])
    vectors = ("bq", "bv", "bu", "bo", "g1", "c1", "bd", "g2", "c2")
    local_v = [local(r[n], r["V" + n]) for n in vectors]
    barrier = pltpu.get_barrier_semaphore()
    for who in part.values():
        pl.semaphore_signal(barrier, inc=1, device_id=who, device_id_type=mesh_id)
    pl.semaphore_wait(barrier, len(part))

    gbits = min(2, bits)
    parts = 1 << gbits
    piece = lax.rem(dp, parts)

    def cut(name, k, of):
        if name == "wa":
            return k * hc, hc // parts, hc // parts
        n = r[name].shape[0] // parts
        return k * n // of, n // of, n

    def weight_x(name, k, of):
        start, size, step_rows = cut(name, k, of)
        src = r[("wq", "wk", "wv", "wo")[k]] if name == "wa" else r[name]
        off = mult(piece * step_rows, 16)
        from_at = pl.ds(off if name == "wa" else mult(off + start, 16), size)
        return send(src.at[from_at], r["W" + name].at[x, pl.ds(mult(off + start, 16), size)], "x")

    def weight_hop(name, k, of):
        start, size, step_rows = cut(name, k, of)
        at = pl.ds(mult(piece * step_rows + start, 16), size)
        dst = r["W" + name].at[ox, at]
        return [prepare(dst, dst, b) for b in range(gbits)]

    def weight_far(name, k, of):
        if gbits < 2:
            return []
        start, size, step_rows = cut(name, k, of)
        b = k % 2
        o = 1 - b
        from_piece = piece + (1 << o) * (1 - 2 * bit[o])
        at = pl.ds(mult(from_piece * step_rows + start, 16), size)
        dst = r["W" + name].at[ox, at]
        return [prepare(dst, dst, b)]

    def arrived(copies):
        for copy in copies:
            copy.wait_recv()

    half = block // 2
    wa_x = [weight_x("wa", k, 4) for k in range(4)]
    b_x = [send(r[n], r["O" + n], "x") for n in ("bq", "bv", "bu")]

    def divide(ref):
        even, odd = ref[:, 0, :], ref[:, 1, :]
        return jnp.where(x == 0, even, odd), jnp.where(x == 0, odd, even)

    local_x.wait()
    at_mine = pl.ds(own0 + mine, block)
    own_rows, far_rows = divide(r["XI"])
    r["XO"][...] = far_rows
    xs[at_mine, :] = own_rows
    x_x = []
    for k in range(2):
        src = r["XO"].at[pl.ds(k * half, half)]
        x_x.append(send(src, xs.at[pl.ds(own0 + mine + k * half, half)], "x"))
    late_x = {(name, k): weight_x(name, k, 2) for name in ("wu", "wd") for k in range(2)}
    x_c = [send(xs.at[at_mine], xs.at[at_mine], "c")]
    local_c.wait()
    own_rows, far_rows = divide(r["CI"])
    r["CO"][...] = far_rows
    r["CT"][pl.ds(mine, block), :] = own_rows
    c_x = send(r["CO"], r["CT"].at[pl.ds(mine, block)], "x")
    local_w = [local(r[name], r["W" + name].at[x]) for name in ("wu", "wd")]

    bias = r["B"]
    rep = r["R"]
    lane = lax.broadcasted_iota(jnp.int32, (block, 128), 1)
    valid = r["lens"][x]
    for copy in local_v:
        copy.wait()
    for k, name in enumerate(vectors[3:]):
        rep[k : k + 1, :width] = r["V" + name][...].reshape(1, width)

    def set_bias(s, q, v, u):
        bias[s, 0:1, :] = jnp.zeros((1, plan.wide), F32)
        bias[s, 0:1, :hc] = q[...].reshape(1, hc)
        bias[s, 0:1, 2 * hc : 3 * hc] = v[...].reshape(1, hc)
        bias[s, 1:2, :ff] = u[...].reshape(1, ff)

    set_bias(x, r["Vbq"], r["Vbv"], r["Vbu"])
    def project(s, first):
        i = lax.div(first, block)
        at = pl.ds(pl.multiple_of(first, block), block)
        y = dnt(xs[at, :], r["Wwa"][s, : plan.qkv_cols, :]) + bias[s, 0:1, : plan.qkv_cols]
        slot0 = first + block * jnp.where(i == 1, 1, 0) - block * jnp.where(i == 2, 1, 0)
        slot = slot0 + lax.broadcasted_iota(jnp.int32, (block, 128), 0)
        masked = jnp.where(slot < valid, 0.0, NEG)
        real = lane < HEAD_DIM
        k_end = jnp.where(lane == 64, masked, jnp.where(lane < 68, 1.0, 0.0))
        q_end = jnp.where(lane == 64, 1.0, 0.0)
        v_end = jnp.where(lane < 67, 1.0, 0.0)
        for k, (name, end) in enumerate((("QP", q_end), ("KP", k_end), ("VP", v_end))):
            for h in range(heads):
                unit = k * heads + h
                tile = y[:, unit // 2 * 128 : unit // 2 * 128 + 128]
                if unit % 2:
                    tile = pltpu.roll(tile, 64, 1)
                if k == 0:
                    tile = tile * SCALE
                r[name][s * heads + h, at, :] = jnp.where(real, tile, end).astype(BF16)

    def started(copies):
        for copy in copies:
            copy.start()
        return copies

    def frames_at(k, offset):
        return lax.rem(own0 + k * own, slots) + offset

    for copy in local_a:
        copy.wait()
    wa_h, wa_f = [], []
    for k in range(4):
        wa_x[k].wait_recv()
        wa_h.append(started(weight_hop("wa", k, 4)))
    for k in range(4):
        arrived(wa_h[k])
        wa_f += started(weight_far("wa", k, 4))
    arrived(b_x)
    set_bias(ox, r["Obq"], r["Obv"], r["Obu"])
    x_x[0].wait_recv()
    at_other = [pl.ds(own0 + other + k * half, half) for k in range(2)]
    x_c.append(send(xs.at[at_other[0]], xs.at[at_other[0]], "c"))
    x_c.pop(0).wait_recv()
    arrived(wa_f)

    @pl.loop(0, 4)
    def _(i):
        project(lax.rem(i, 2), frames_at(lax.div(i, 2), mine))

    x_x[1].wait_recv()
    x_c.append(send(xs.at[at_other[1]], xs.at[at_other[1]], "c"))
    for k in range(2):
        if k:
            arrived(x_c)

        @pl.loop(0, 2)
        def _(s, k=k):
            project(s, frames_at(k, other))

    for copy in local_w:
        copy.wait()

    row_tiles = [slice(i * block, (i + 1) * block) for i in range(4)]

    def attend(hs):
        queries = [r["QP"][hs, at, :] for at in row_tiles]
        scores = [dnt(q, r["KP"][hs]) for q in queries]
        done = []
        for score in scores:
            top = jnp.max(score, -1, keepdims=True)
            done.append((dn(jnp.exp(score - top).astype(BF16), r["VP"][hs]), top))
        for at, q, (o, top) in zip(row_tiles, queries, done):
            total = o[:, HEAD_DIM : HEAD_DIM + 1]
            r["DC"][hs, at, :] = (o / total).astype(BF16)
            hi, mid, low = split3(-(top + jnp.log(total)))
            ends = jnp.where(lane == 66, mid, jnp.where(lane == 67, low, q.astype(F32)))
            r["QP"][hs, at, :] = jnp.where(lane == 65, hi, ends).astype(BF16)

    chunks = [(name, k) for name in ("wu", "wd") for k in range(2)]
    late_h = {key: weight_hop(*key, 2) for key in chunks}
    late_f = {key: weight_far(*key, 2) for key in chunks}

    def hop(name, k):
        late_x[name, k].wait_recv()
        started(late_h[name, k])

    def far(name, k):
        arrived(late_h[name, k])
        started(late_f[name, k])

    progress = [(1, hop, "wu", 1), (2, far, "wu", 0), (3, hop, "wd", 0)]
    progress += [(4, far, "wu", 1), (5, hop, "wd", 1)]
    hop("wu", 0)

    @pl.loop(0, 2 * heads)
    def _(i):
        attend(lax.rem(x * heads + i, 2 * heads))
        for when, move, name, k in progress:

            @pl.when(i == min(when, 2 * heads - 1))
            def _(move=move, name=name, k=k):
                move(name, k)

    def join(dst, s, parts, first, last):
        @pl.loop(first, last)
        def _(i):
            at = pl.ds(pl.multiple_of(i * block, block), block)
            for t in range(0, len(parts), 2):
                ref, h = parts[t]
                tile = ref[s * heads + h, at, :].astype(F32)
                odd = jnp.zeros_like(tile)
                if t + 1 < len(parts):
                    ref, h = parts[t + 1]
                    odd = pltpu.roll(ref[s * heads + h, at, :].astype(F32), 64, 1)
                tile = jnp.where(lane < HEAD_DIM, tile, odd)
                dst[s, at, t * 64 : t * 64 + 128] = tile.astype(BF16)

    @pl.loop(0, 2)
    def _(s):
        join(r["C"], s, [(r["DC"], h) for h in range(heads)], 0, 4)

    sbuf, rbuf = r["SB"], r["RB"]

    def exchange(partial):
        base = take(2)

        @pl.loop(0, 2)
        def _(i):
            sbuf[i] = partial(row(2 + i)).astype(BF16)
            remote(sbuf.at[i], rbuf.at[i], base + i, "c").start()

        return base

    def received(base, i):
        remote(sbuf.at[i], rbuf.at[i], base + i, "c").wait_recv()
        return rbuf[i].astype(F32)

    def left(base):
        for i in range(2):
            remote(sbuf.at[i], rbuf.at[i], base + i, "c").wait_send()

    def share(buf, base, i):
        at = pl.ds(row(i), block)
        return remote(buf.at[at], buf.at[at], base + i, "c")

    def shared(buf):
        base = take(2)
        copies = [share(buf, base, i) for i in range(2)]
        pending.extend(copies)
        return base, copies

    sums = r["sums"]
    sums[...] = jnp.zeros_like(sums)

    def add_sum(k, v, n=None):
        n = v.shape[-1]
        sums[pl.ds(k, 1), :n] = sums[pl.ds(k, 1), :n] + v

    def attn_out(at0):
        at = pl.ds(at0, block)
        return sum(dn(r["C"][s, at, :hc], r["Wwa"][s, 3 * hc :, :]) for s in range(2))

    ex = exchange(attn_out)
    hb_base, hb_c = shared(r["HB"])

    @pl.loop(0, 2)
    def _(i):
        a = attn_out(row(i)) + rep[0:1, :width]
        z = xs[pl.ds(row(i), block), :].astype(F32) + a + received(ex, i)
        z = z - mean(z)
        inv = lax.rsqrt(mean(z * z) + EPS)
        n1 = z * inv
        at = pl.ds(pl.multiple_of(i * block, block), block)
        r["N1"][at, :] = n1
        r["INV"][at, :] = jnp.broadcast_to(inv, (block, 128))
        r["HB"][pl.ds(row(i), block), :] = (n1 * rep[1:2, :width] + rep[2:3, :width]).astype(BF16)
        share(r["HB"], hb_base, i).start()
    left(ex)

    def up(s, first, last):
        @pl.loop(first, last)
        def _(i):
            at = pl.ds(row(i), block)
            u = dn(r["HB"][at, :], r["Wwu"][s]) + bias[s, 1:2, :ff]
            cdf = 0.5 * (1.0 + lax.erf(u * ROOT_HALF))
            r["G"][s, at, :] = (u * cdf).astype(BF16)
            r["SL"][s, at, :] = u.astype(BF16)

    far("wd", 0)
    up(x, 0, 2)
    arrived(hb_c)
    far("wd", 1)
    up(x, 2, 4)
    arrived(late_f["wu", 0] + late_f["wu", 1])
    up(ox, 0, 4)

    def ffn_out(at0):
        at = pl.ds(at0, block)
        return dn(r["G"][0, at, :], r["Wwd"][0]) + dn(r["G"][1, at, :], r["Wwd"][1])

    arrived(late_f["wd", 0] + late_f["wd", 1])
    ex = exchange(ffn_out)
    df_base, df_c = shared(r["DF"])
    c_x.wait_recv()

    @pl.loop(0, 2)
    def _(i):
        at = pl.ds(pl.multiple_of(i * block, block), block)
        hidden = r["N1"][at, :] * rep[1:2, :width] + rep[2:3, :width]
        f = ffn_out(row(i)) + rep[3:4, :width]
        z = hidden + f + received(ex, i)
        z = z - mean(z)
        inv = lax.rsqrt(mean(z * z) + EPS)
        n2 = z * inv
        r["OB"][at, :] = (n2 * rep[4:5, :width] + rep[5:6, :width]).astype(BF16)
        dy = r["CT"][at, :].astype(F32)
        add_sum(4, col_sum(dy * n2))
        add_sum(5, col_sum(dy))
        e2 = dy * rep[4:5, :width]
        dz = inv * (e2 - mean(e2) - n2 * mean(e2 * n2))
        r["DZ"][at, :] = dz
        df = dz.astype(BF16)
        add_sum(3, col_sum(df.astype(F32)))
        r["DF"][pl.ds(row(i), block), :] = df
        share(r["DF"], df_base, i).start()
    left(ex)
    out_x = send(r["OB"].at[pl.ds(other, block)], r["out"].at[x], "x")
    out_l = local(r["OB"].at[pl.ds(mine, block)], r["out"].at[x])

    def adder(dst, d, row0, src, sd, n):
        size = chunk_of(n)

        @pl.loop(0, n // size)
        def _(i):
            at = pl.ds(mult(row0 + i * size), size)
            got = src[sd, pl.ds(mult(i * size), size), :].astype(F32)
            dst[d, at, :] = (dst[d, at, :].astype(F32) + got).astype(BF16)

    def stream(key):
        name, row0, n, order = plan.streams[key]
        grad, final = r["G_" + name], r["F_" + name]
        both, halved, copies, then = True, [], [], []
        for k, (dim, _, n, halve) in enumerate(plan.steps(n, order)):
            got = r["S_%s_%d_%d" % (*key, k)]
            if dim == "x":
                copies.append(prepare(grad.at[ox, pl.ds(row0, n)], got.at[0], "x"))
                both = False
            else:
                sent = row0
                if halve:
                    halved.append(dim)
                    sent = mult(row0 + (1 - bit[dim]) * n)
                    row0 = mult(row0 + bit[dim] * n)
                at = pl.ds(sent, n)
                src = grad.at[:, at] if both else grad.at[x, at]
                copies.append(prepare(src, got if both else got.at[0], dim, halve))

            def add(copy=copies[-1], got=got, row0=row0, n=n, both=both, wait=dim != "x" and not halve):
                if wait:
                    copy.wait_send()
                if both:
                    adder(grad, 0, row0, got, 0, n)
                    adder(grad, 1, row0, got, 1, n)
                else:
                    adder(grad, x, row0, got, 0, n)

            then.append([add])
        keep = local_prepare(grad.at[x, pl.ds(row0, n)], final.at[pl.ds(row0, n)])
        then[-1].append(keep.start)
        src = grad.at[x, pl.ds(row0, n)]
        for dim in reversed(halved):
            at = pl.ds(row0, n)
            copies.append(prepare(src, final.at[at], dim))
            then.append([])
            row0 = mult(row0 - bit[dim] * n)
            n *= 2
            src = final.at[pl.ds(row0, n)]
        then[len(plan.steps(plan.streams[key][2], order)) if halved else -1].append(keep.wait)
        return chain(copies, then)

    def chain(copies, then):
        def move(k):
            if k:
                copies[k - 1].wait_recv()
                for act in then[k - 1]:
                    act()
            if k < len(copies):
                copies[k].start()

        return move

    def sums_stream():
        copies, then = [], []
        for k, who in enumerate(["c", "x"] + list(range(bits))):
            n = 8 if who == "c" else 16
            copy = prepare(sums.at[pl.ds(0, n)], r["SR"].at[k, pl.ds(0, n)], who, False)

            def add(copy=copy, k=k, n=n):
                copy.wait_send()
                sums[0:n, :] = sums[0:n, :] + r["SR"][k, 0:n, :]

            copies.append(copy)
            then.append([add])
        return chain(copies, then)

    movers = {key: stream(key) for key in plan.streams}
    movers["sums"] = sums_stream()
    moves = plan.moves()

    def step(name, when=None):
        if not moves[name]:
            return

        def make():
            for key, k in moves[name]:
                movers[key](k)

        if when is None:
            make()
        else:
            pl.when(when)(make)

    def slope(first, last):
        @pl.loop(first, last)
        def _(i):
            at = pl.ds(row(i), block)
            for s in range(2):
                da = dnt(r["DF"][at, :], r["Wwd"][s])
                u = r["SL"][s, at, :].astype(F32)
                cdf = 0.5 * (1.0 + lax.erf(u * ROOT_HALF))
                du = da * (cdf + u * (DENSITY * jnp.exp(-0.5 * u * u)))
                add_sum(8 + s, col_sum(du))
                r["SL"][s, at, :] = du.astype(BF16)

    def weight_grad(name, lhs, rhs):
        dst = r["G_" + name]
        n = dst.shape[1] // 2

        @pl.loop(0, 4)
        def _(q):
            s, j = lax.rem(ox + q, 2), lax.div(q, 2)
            at = pl.ds(pl.multiple_of(j * n, n), n)
            dst[s, at, :] = dtn(lhs(s, at), rhs(s)).astype(BF16)
            for k in range(4):
                step((name, "os"[k % 2], k // 2), q == k)

    slope(0, 2)
    arrived(df_c)
    weight_grad("down", lambda s, at: r["G"][s, :, at], lambda s: r["DF"][...])
    slope(2, 4)
    step("slope")
    weight_grad("up", lambda s, at: r["HB"][:, at], lambda s: r["SL"][s])

    def hidden_back(at0):
        at = pl.ds(at0, block)
        return dnt(r["SL"][0, at, :], r["Wwu"][0]) + dnt(r["SL"][1, at, :], r["Wwu"][1])

    ex = exchange(hidden_back)
    da_base, da_c = shared(r["DA"])
    step("hidden0")

    @pl.loop(0, 2)
    def _(i):
        at = pl.ds(pl.multiple_of(i * block, block), block)
        dh = r["DZ"][at, :] + hidden_back(row(i))
        dh = dh + received(ex, i)
        n1 = r["N1"][at, :]
        add_sum(1, col_sum(dh * n1))
        add_sum(2, col_sum(dh))
        e1 = dh * rep[1:2, :width]
        dz = r["INV"][at, 0:1] * (e1 - mean(e1) - n1 * mean(e1 * n1))
        r["DZ"][at, :] = dz
        da = dz.astype(BF16)
        add_sum(0, col_sum(da.astype(F32)))
        r["DA"][pl.ds(row(i), block), :] = da
        share(r["DA"], da_base, i).start()
    left(ex)
    step("hidden1")

    rows_e = lax.broadcasted_iota(jnp.int32, (hc, heads * 128), 0)
    lanes_e = lax.broadcasted_iota(jnp.int32, (hc, heads * 128), 1)
    spot = lanes_e - lax.div(rows_e, HEAD_DIM) * 128
    r["E"][...] = jnp.where((spot >= 64) & (spot < 67), -1.0, 0.0).astype(BF16)

    def context_back(first, last):
        @pl.loop(first, last)
        def _(i):
            at = pl.ds(row(i), block)
            for s in range(2):
                dc = dnt(r["DA"][at, :], r["Wwa"][s, 3 * hc :, :]).astype(BF16).astype(F32)
                prod = dc * r["C"][s, at, :hc].astype(F32)
                prod_hi = prod.astype(BF16)
                prod_lo = (prod - prod_hi.astype(F32)).astype(BF16)
                ends = dn(prod_hi, r["E"][...]) + dn(prod_lo, r["E"][...])
                for h in range(heads):
                    end = ends[:, h * 128 : h * 128 + 128]
                    if 2 * h + 2 <= 2 * heads - heads % 2:
                        tile = dc[:, h // 2 * 128 : h // 2 * 128 + 128]
                        if h % 2:
                            tile = pltpu.roll(tile, 64, 1)
                    else:
                        tile = jnp.concatenate([dc[:, h * 64 :], end[:, 64:]], 1)
                    tile = jnp.where(lane < 64, tile, end)
                    hi, mid, low = split3(tile)
                    tile = jnp.where(lane == 65, mid, jnp.where(lane == 66, low, hi))
                    r["DC"][s * heads + h, at, :] = tile.astype(BF16)

    context_back(0, 2)
    step("ctx0")
    arrived(da_c)
    context_back(2, 4)
    step("ctx1")
    @pl.loop(0, 2)
    def _(s):
        r["G_attn"][s, 3 * hc :, :] = dtn(r["C"][s], r["DA"][...])[:hc].astype(BF16)

    step("gout")

    def head_back(hs):
        keys, values = r["KP"].at[hs], r["VP"].at[hs]
        r["KT"][...] = keys[...].T
        queries = [r["QP"][hs, at, :] for at in row_tiles]
        tangents = [r["DC"][hs, at, :] for at in row_tiles]
        scores = [dnt(keys[...], q) for q in queries]
        centred = [dnt(values[...], dc) for dc in tangents]
        dk = dv = 0.0
        dq = []
        for q, dc, score, middle in zip(queries, tangents, scores, centred):
            p = jnp.exp(score)
            ds = (p * middle).astype(BF16)
            dv = dv + dn(p.astype(BF16), dc)
            dk = dk + dn(ds, q)
            dq.append(dn(r["KT"][...], ds).T)
        for at, d in zip(row_tiles, dq):
            r["QP"][hs, at, :] = (d * SCALE).astype(BF16)
        r["KP"][hs] = dk.astype(BF16)
        r["VP"][hs] = dv.astype(BF16)

    g_attn = r["G_attn"]

    @pl.loop(0, 2)
    def _(i):
        s = lax.rem(ox + i, 2)

        @pl.loop(0, heads)
        def _(h):
            head_back(s * heads + h)
            for k in range(2 * heads):
                step(("head", "os"[k // heads], k % heads), i * heads + h == k)

        join(r["D3"], s, [(r[n], h) for n in ("QP", "KP", "VP") for h in range(heads)], 0, 4)
        add_sum(10 + s, col_sum(r["D3"][s].astype(F32)))
        g_attn[s, : 2 * hc, :] = dtn(r["D3"][s, :, : 2 * hc], xs[...]).astype(BF16)
        for k in range(2):
            step(("qk", "os"[k]), i == k)
        grad_v = dtn(r["D3"][s, :, 2 * hc :], xs[...])
        g_attn[s, 2 * hc : 3 * hc, :] = grad_v[:hc].astype(BF16)
        for k in range(2):
            step(("v", "os"[k]), i == k)

    def input_back(at0):
        at = pl.ds(at0, block)
        return sum(dn(r["D3"][s, at, :], r["Wwa"][s, : plan.qkv_cols, :]) for s in range(2))

    ex = exchange(input_back)
    step("dx0")

    @pl.loop(0, 2)
    def _(i):
        at = pl.ds(pl.multiple_of(i * block, block), block)
        dx = r["DZ"][at, :] + input_back(row(i))
        r["DZ"][at, :] = dx + received(ex, i)

    left(ex)
    r["DXS"][...] = r["DZ"][pl.ds(other, block), :].astype(BF16)
    dx_x = send(r["DXS"], r["dx_far"], "x")
    dx_l = local(r["DZ"].at[pl.ds(mine, block)], r["dx_own"])

    step("dx1")
    step("tail")
    r["vec"][...] = sums[...]
    out_x.wait_recv()
    dx_x.wait_recv()
    out_l.wait()
    dx_l.wait()
    for copy in pending:
        copy.wait_send()


def finish(names, *refs):
    r = dict(zip(names, refs))
    sem = r["sem"]
    used = []

    def copy(src, dst):
        made = pltpu.make_async_copy(src, dst, sem.at[len(used)])
        made.start()
        used.append(made)
        return made

    first = lax.axis_index("tp") < 2
    hc = r["g_query"].shape[0]
    targets = {"F_down": ["g_down"], "F_up": ["g_up"]}
    targets["F_attn"] = ["g_query", "g_key", "g_value", "g_out"]
    got = {}
    for n in targets:
        rows = r[n].shape[0] // 4
        for k in range(4):
            at = pl.ds(k * rows, rows)
            got[n, k] = copy(r[n].at[at], r["i_" + n].at[at])
    for n in ("dx_own", "dx_far", "out", "vec"):
        got[n] = copy(r[n], r["i_" + n])
    loads = len(used)
    for n, outs in targets.items():
        rows = r[n].shape[0] // 4
        if len(outs) > 1:
            for k in range(4):
                got[n, k].wait()
        for k in range(4):
            at = pl.ds(k * rows, rows)
            if len(outs) == 1:
                got[n, k].wait()
            r["o_" + n][at, :] = r["i_" + n][at, :].astype(F32)
            target = r[outs[k]] if len(outs) > 1 else r[outs[0]].at[at]
            copy(r["o_" + n].at[at], target)
    got["dx_own"].wait()
    got["dx_far"].wait()
    own, far = r["i_dx_own"][...], r["i_dx_far"][...].astype(F32)
    r["o_dx"][:, 0, :] = jnp.where(first, own, far)
    r["o_dx"][:, 1, :] = jnp.where(first, far, own)
    copy(r["o_dx"], r["dx"])
    got["out"].wait()
    for k in range(2):
        r["o_rows"][:, k, :] = r["i_out"][k]
    copy(r["o_rows"], r["rows"])
    got["vec"].wait()
    vec = r["i_vec"]
    width = r["s_bo"].shape[0]
    for k, n in enumerate(("bo", "g1", "c1", "bd", "g2", "c2")):
        r["s_" + n][...] = vec[k, :width]
    ff = r["s_bu"].shape[0]
    r["s_bu"][...] = jnp.where(first, vec[8, :ff], vec[9, :ff])
    b3 = jnp.where(first, vec[10:11, :], vec[11:12, :])
    r["s_bq"][...] = b3[:, :hc].reshape(hc)
    r["s_bv"][...] = b3[:, 2 * hc : 3 * hc].reshape(hc)
    for made in used[loads:]:
        made.wait()


def local(
    inputs,
    lengths,
    w_query,
    b_query,
    w_key,
    w_value,
    b_value,
    w_out,
    b_out,
    norm1_gain,
    norm1_bias,
    w_up,
    b_up,
    w_down,
    b_down,
    norm2_gain,
    norm2_bias,
    cotangent,
):
    block, utts, width = inputs.shape
    dpn = lax.axis_size("dp")
    plan = Plan(block, width, w_query.shape[1], w_up.shape[1], dpn)
    hc, ff, wide = plan.head_cols, plan.ff, plan.wide
    slots, own, heads = plan.slots, plan.own, plan.heads


    operands = [
        ("inputs", inputs),
        ("cot", cotangent),
        ("lens", lengths),
        ("wq", w_query.T),
        ("wk", w_key.T),
        ("wv", w_value.T),
        ("wo", w_out),
        ("wu", w_up),
        ("wd", w_down),
        ("bq", b_query),
        ("bv", b_value),
        ("bu", b_up),
        ("bo", b_out),
        ("g1", norm1_gain),
        ("c1", norm1_bias),
        ("bd", b_down),
        ("g2", norm2_gain),
        ("c2", norm2_bias),
    ]
    shape_of = jax.ShapeDtypeStruct
    hbm = pl.BlockSpec(memory_space=pl.ANY)
    vmem = pl.BlockSpec(memory_space=pltpu.VMEM)
    smem = pl.BlockSpec(memory_space=pltpu.SMEM)
    outs = [
        ("out", shape_of((2, block, width), BF16), hbm),
        ("dx_own", shape_of((block, width), F32), hbm),
        ("dx_far", shape_of((block, width), BF16), hbm),
        ("vec", shape_of((16, wide), F32), vmem),
    ]
    grads = (
        ("down", ff, width),
        ("up", width, ff),
        ("attn", 4 * hc, width),
    )
    for name, rows, cols in grads:
        outs.append(("F_" + name, shape_of((rows, cols), BF16), hbm))

    def v(name, shape, dtype=BF16):
        return (name, pltpu.VMEM(shape, dtype))

    scratch = [
        v("X", (slots, width)),
        v("Wwa", (2, 4 * hc, width)),
        v("Wwu", (2, width, ff)),
        v("Wwd", (2, ff, width)),
        v("B", (2, 8, wide), F32),
        *(v("V" + n, a.shape, F32) for n, a in operands[-9:]),
        v("Obq", (hc,), F32),
        v("Obv", (hc,), F32),
        v("Obu", (ff,), F32),
        v("R", (8, wide), F32),
        v("XI", (block, utts, width)),
        v("CI", (block, utts, width)),
        v("XO", (block, width)),
        v("CO", (block, width)),
        v("CT", (own, width)),
        v("QP", (2 * heads, slots, 128)),
        v("KP", (2 * heads, slots, 128)),
        v("VP", (2 * heads, slots, 128)),
        v("DC", (2 * heads, slots, 128)),
        v("C", (2, slots, plan.out_cols)),
        v("E", (hc, heads * 128)),
        v("SB", (2, block, width)),
        v("RB", (2, block, width)),
        v("N1", (own, width), F32),
        v("INV", (own, 128), F32),
        v("HB", (slots, width)),
        v("G", (2, slots, ff)),
        v("SL", (2, slots, ff)),
        v("OB", (own, width)),
        v("DZ", (own, width), F32),
        v("DF", (slots, width)),
        v("DA", (slots, width)),
        v("D3", (2, slots, plan.qkv_cols)),
        v("KT", (128, slots)),
        v("DXS", (block, width)),
        v("sums", (16, wide), F32),
        v("SR", (2 + plan.bits, 16, wide), F32),
    ]
    for name, rows, cols in grads:
        scratch.append(v("G_" + name, (2, rows, cols)))
    widths = {name: cols for name, _, cols in grads}
    for key, (name, _, rows, order) in plan.streams.items():
        for k, (_, both, n, _) in enumerate(plan.steps(rows, order)):
            scratch.append(v("S_%s_%d_%d" % (*key, k), (both, n, widths[name])))
    scratch += [
        ("ssem", pltpu.SemaphoreType.DMA((192,))),
        ("rsem", pltpu.SemaphoreType.DMA((192,))),
        ("lsem", pltpu.SemaphoreType.DMA((48,))),
    ]
    names = [n for n, _ in operands] + [n for n, _, _ in outs] + [n for n, _ in scratch]
    results = pl.pallas_call(
        functools.partial(layer, plan, names),
        out_shape=[s for _, s, _ in outs],
        in_specs=[smem if n == "lens" else hbm for n, _ in operands],
        out_specs=[s for _, _, s in outs],
        scratch_shapes=[s for _, s in scratch],
        compiler_params=pltpu.CompilerParams(
            collective_id=0, has_side_effects=True, vmem_limit_bytes=63 * 2**20
        ),
        name="encoder_layer",
    )(*[a for _, a in operands])
    got = dict(zip([n for n, _, _ in outs], results))
    inner = [got[n] for n in ("out", "dx_own", "dx_far", "F_down", "F_up", "F_attn", "vec")]
    inner_names = ["out", "dx_own", "dx_far", "F_down", "F_up", "F_attn", "vec"]
    frames = (block, utts, width)
    final = [("g_down", (ff, width), F32), ("g_up", (width, ff), F32)]
    final += [("dx", frames, F32), ("rows", frames, BF16)]
    final += [(n, (hc, width), F32) for n in ("g_query", "g_key", "g_value", "g_out")]
    small = [("s_" + n, (width,)) for n in ("bo", "g1", "c1", "bd", "g2", "c2")]
    small += [("s_bu", (ff,)), ("s_bq", (hc,)), ("s_bv", (hc,))]
    buffers = [("i_" + n, a.shape, a.dtype) for n, a in zip(inner_names, inner)]
    buffers += [("o_rows", frames, BF16), ("o_dx", frames, F32)]
    buffers += [("o_" + n, got[n].shape, F32) for n in ("F_down", "F_up", "F_attn")]
    labels = inner_names + [n for n, _, _ in final] + [n for n, _ in small]
    labels += [n for n, _, _ in buffers] + ["sem"]
    results = pl.pallas_call(
        functools.partial(finish, labels),
        in_specs=[hbm] * len(inner),
        out_specs=[hbm] * len(final) + [vmem] * len(small),
        out_shape=[shape_of(n, t) for _, n, t in final] + [shape_of(n, F32) for _, n in small],
        scratch_shapes=[pltpu.VMEM(n, t) for _, n, t in buffers]
        + [pltpu.SemaphoreType.DMA((32,))],
        compiler_params=pltpu.CompilerParams(vmem_limit_bytes=60 * 2**20),
        name="finish",
    )(*inner)
    g_down, g_up, input_grad, outputs, g_query, g_key, g_value, g_out = results[:8]
    g_bo, g_g1, g_c1, g_bd, g_g2, g_c2, g_bu, g_bq, g_bv = results[8:]
    return (
        outputs,
        input_grad,
        g_query.T,
        g_bq,
        g_key.T,
        g_value.T,
        g_bv,
        g_out,
        g_bo,
        g_g1,
        g_c1,
        g_up,
        g_bu,
        g_down,
        g_bd,
        g_g2,
        g_c2,
    )


def solution(mesh):
    whole = P()
    rows = P("tp", "dp", None)
    cols = P(None, "tp")
    down = P("tp", None)
    shard = P("tp")
    return jax.shard_map(
        local,
        mesh=mesh,
        in_specs=(
            rows,
            P("dp"),
            cols,
            shard,
            cols,
            cols,
            shard,
            down,
            whole,
            whole,
            whole,
            cols,
            shard,
            down,
            whole,
            whole,
            whole,
            rows,
        ),
        out_specs=(
            rows,
            rows,
            cols,
            shard,
            cols,
            cols,
            shard,
            down,
            whole,
            whole,
            whole,
            cols,
            shard,
            down,
            whole,
            whole,
            whole,
        ),
        check_vma=False,
    )
```

```python
import functools
import math

import jax
import jax.numpy as jnp
from jax import lax
from jax.experimental import pallas as pl
from jax.experimental.pallas import tpu as pltpu
from jax.sharding import PartitionSpec as P

HEAD_DIM = 64
EPS = 1e-05
ROOT_HALF = 0.7071067811865476
DENSITY = 0.3989422804014327
SCALE = 0.125
NEG = -1e30
F32 = jnp.float32
BF16 = jnp.bfloat16


def dn(a, b):
    return lax.dot_general(a, b, (((1,), (0,)), ((), ())), preferred_element_type=F32)


def dnt(a, b):
    return lax.dot_general(a, b, (((1,), (1,)), ((), ())), preferred_element_type=F32)


def dtn(a, b):
    return lax.dot_general(a, b, (((0,), (0,)), ((), ())), preferred_element_type=F32)


def split3(v):
    hi = v.astype(BF16).astype(F32)
    rest = v - hi
    mid = rest.astype(BF16).astype(F32)
    return hi, mid, rest - mid


def mean(v):
    return jnp.mean(v, -1, keepdims=True)


def col_sum(v):
    return jnp.sum(v, 0, keepdims=True)


def chunk_of(n):
    for c in (96, 64, 48, 32, 16):
        if n % c == 0:
            return c
    return n


ORDERS = {
    ('down', 0): [0, 1, 2, 'x'],
    ('down', 1): [1, 0, 'x', 2],
    ('down', 2): [1, 0, 'x', 2],
    ('down', 3): ['x', 0, 1, 2],
    ('up', 0): [0, 1, 'x', 2],
    ('up', 1): [0, 'x', 1, 2],
    ('up', 2): ['x', 0, 1, 2],
    ('up', 3): ['x', 0, 1, 2],
    ('attn', 0): ['x', 0, 1, 2],
    ('attn', 1): ['x', 0, 1, 2],
    ('attn', 2): ['x', 0, 1, 2],
    ('attn', 3): [1, 0, 'x', 2],
}
SCHEDULE = {
    'hidden0': [('down', 1), ('down', 0)],
    'hidden1': [('down', 3)],
    'ctx0': [('up', 0), ('down', 2)],
    'ctx1': [('down', 0), ('up', 2)],
    ('head', 'o', 0): [('up', 0), ('up', 1)],
    ('head', 'o', 1): [('up', 0), ('up', 3), ('down', 1), ('down', 3), ('down', 0)],
    ('head', 'o', 2): [('down', 2), ('up', 1), ('down', 1), ('attn', 3)],
    ('qk', 'o'): [('up', 0), ('down', 3), ('down', 2), ('up', 2), ('down', 0), ('up', 1)],
    ('head', 's', 0): [('up', 0), ('up', 3), ('down', 1)],
    ('head', 's', 1): [('down', 3), ('attn', 3)],
    ('head', 's', 2): [('up', 0), ('down', 2), ('up', 2), ('down', 1), ('down', 0)],
    ('qk', 's'): [('up', 3), ('attn', 1), ('up', 1), ('down', 2), ('down', 3), ('attn', 0)],
    'dx0': [('up', 2), ('down', 0)],
    'dx1': [('attn', 1), ('up', 3), ('attn', 2), ('down', 1), ('attn', 3), ('up', 1), 'sums'],
    "tail": [('down', 3), ('down', 2), ('attn', 0), ('up', 2), ('attn', 1), ('attn', 2), ('up', 3), 'sums', ('attn', 3), ('up', 1), ('attn', 0), ('attn', 1), ('up', 2), ('attn', 2), ('attn', 0), ('up', 3), ('attn', 1), 'sums', ('attn', 2), ('attn', 3), ('attn', 0), 'sums', ('attn', 1), ('attn', 2), ('attn', 0), ('attn', 3), 'sums', ('attn', 2)],
}


class Plan:
    def __init__(self, block, width, head_cols, ff_local, dp):
        self.block = block
        self.slots = 4 * block
        self.own = 2 * block
        self.width = width
        self.head_cols = head_cols
        self.heads = head_cols // HEAD_DIM
        self.ff = ff_local
        self.dp = dp
        self.bits = dp.bit_length() - 1
        self.wide = max(width, ff_local, -(-3 * head_cols // 128) * 128)
        self.qkv_cols = -(-3 * head_cols // 128) * 128
        self.out_cols = -(-head_cols // 128) * 128
        self.streams = {}
        for name, rows in (("down", ff_local), ("up", width), ("attn", 4 * head_cols)):
            for k in range(4):
                n = rows // 4
                self.streams[(name, k)] = (name, k * n, n, self.order((name, k)))

    def order(self, key):
        order = [d for d in ORDERS[key] if d == "x" or d < self.bits]
        return order + list(range(3, self.bits))

    def steps(self, n, order):
        steps, both = [], 2
        for k, dim in enumerate(order):
            if dim == "x":
                both = 1
                steps.append((dim, both, n, False))
                continue
            last = both == 1 and k == len(order) - 1
            halve = not last and (n // 2) % 16 == 0
            if halve:
                n //= 2
            steps.append((dim, both, n, halve))
        return steps


    def x_first(self, key):
        return self.streams[key][3][0] == "x"

    def moves(self):
        events = []

        def point(name, *keys, tags="os"):
            events.append((name, [k for k in keys if ("o" if self.x_first(k) else "s") in tags]))

        for name in ("down", "up"):
            for j in range(2):
                for tag in "os":
                    point((name, tag, j), (name, 2 * j), (name, 2 * j + 1), tags=tag)
            if name == "down":
                point("slope")
        for name in ("hidden0", "hidden1", "ctx0", "ctx1"):
            point(name)
        point("gout", ("attn", 3))
        for tag in "os":
            for h in range(self.heads):
                point(("head", tag, h))
            point(("qk", tag), ("attn", 0), ("attn", 1), tags=tag)
            point(("v", tag), ("attn", 2), tags=tag)
        events += [("dx0", ["sums"]), ("dx1", []), ("tail", [])]
        total = {"sums": 3 + self.bits}
        for key, (_, _, n, order) in self.streams.items():
            steps = self.steps(n, order)
            total[key] = 1 + len(steps) + sum(halve for _, _, _, halve in steps)
        at, moves = {}, {}
        for name, begun in events:
            moves[name] = [(key, 0) for key in begun]
            at.update({key: 1 for key in begun})
            for key in SCHEDULE.get(name, ()):
                if key in at and at[key] < total[key]:
                    moves[name].append((key, at[key]))
                    at[key] += 1
        while any(at[key] < total[key] for key in at):
            for key in at:
                if at[key] < total[key]:
                    moves["tail"].append((key, at[key]))
                    at[key] += 1
        return moves


def layer(plan, names, *refs):
    r = dict(zip(names, refs))
    block, slots, own, width = plan.block, plan.slots, plan.own, plan.width
    hc, heads, ff, dpn, bits = plan.head_cols, plan.heads, plan.ff, plan.dp, plan.bits
    dp = lax.axis_index("dp")
    tp = lax.axis_index("tp")
    x = lax.div(tp, 2)
    c = lax.rem(tp, 2)
    ox = 1 - x
    bit = [lax.rem(lax.div(dp, 1 << b), 2) for b in range(bits)]
    part = {b: (dp + (1 << b) * (1 - 2 * bit[b]), tp) for b in range(bits)}
    part["x"] = (dp, lax.rem(tp + 2, 4))
    part["c"] = (dp, tp + 1 - 2 * c)
    mesh_id = pl.DeviceIdType.MESH

    ssem, rsem, lsem = r["ssem"], r["rsem"], r["lsem"]
    count = {"r": 0, "l": 0}
    pending = []

    def take(n):
        count["r"] += n
        return count["r"] - n

    def remote(src, dst, i, who):
        return pltpu.make_async_remote_copy(
            src_ref=src,
            dst_ref=dst,
            send_sem=ssem.at[i],
            recv_sem=rsem.at[i],
            device_id=part[who],
            device_id_type=mesh_id,
        )

    def prepare(src, dst, who, keep=True):
        copy = remote(src, dst, take(1), who)
        if keep:
            pending.append(copy)
        return copy

    def send(src, dst, who):
        copy = prepare(src, dst, who)
        copy.start()
        return copy

    def local_prepare(src, dst):
        i = count["l"]
        count["l"] += 1
        return pltpu.make_async_copy(src, dst, lsem.at[i])

    def local(src, dst):
        copy = local_prepare(src, dst)
        copy.start()
        return copy

    def mult(v, m=16):
        return pl.multiple_of(v, math.gcd(m, 128))

    def row(i):
        return pl.multiple_of(lax.rem(c * own + i * block, slots), block)

    own0 = pl.multiple_of(c * own, own)
    mine = pl.multiple_of(x * block, block)
    other = pl.multiple_of(ox * block, block)

    xs = r["X"]
    local_a = []
    for k, name in enumerate(("wq", "wk", "wv", "wo")):
        local_a.append(local(r[name], r["Wwa"].at[x, pl.ds(k * hc, hc)]))
    local_x = local(r["inputs"], r["XI"])
    local_c = local(r["cot"], r["CI"])
    vectors = ("bq", "bv", "bu", "bo", "g1", "c1", "bd", "g2", "c2")
    local_v = [local(r[n], r["V" + n]) for n in vectors]
    barrier = pltpu.get_barrier_semaphore()
    for who in part.values():
        pl.semaphore_signal(barrier, inc=1, device_id=who, device_id_type=mesh_id)
    pl.semaphore_wait(barrier, len(part))

    gbits = min(2, bits)
    parts = 1 << gbits
    piece = lax.rem(dp, parts)

    def cut(name, k, of):
        if name == "wa":
            return k * hc, hc // parts, hc // parts
        n = r[name].shape[0] // parts
        return k * n // of, n // of, n

    def weight_x(name, k, of, piece=piece):
        start, size, step_rows = cut(name, k, of)
        src = r[("wq", "wk", "wv", "wo")[k]] if name == "wa" else r[name]
        off = mult(piece * step_rows, 16)
        from_at = pl.ds(off if name == "wa" else mult(off + start, 16), size)
        return send(src.at[from_at], r["W" + name].at[x, pl.ds(mult(off + start, 16), size)], "x")

    def weight_hop(name, k, of):
        start, size, step_rows = cut(name, k, of)
        at = pl.ds(mult(piece * step_rows + start, 16), size)
        dst = r["W" + name].at[ox, at]
        return [prepare(dst, dst, b) for b in range(gbits)]

    def weight_far(name, k, of):
        if gbits < 2:
            return []
        start, size, step_rows = cut(name, k, of)
        if name == "wd" and k == 1:
            return []
        ways = [(k % 2, start, size)]
        if name == "wd":
            low = size // 2 // 16 * 16
            ways = [(0, start, low), (1, start + low, size - low)]
        copies = []
        for b, start, size in ways:
            o = 1 - b
            from_piece = piece + (1 << o) * (1 - 2 * bit[o])
            at = pl.ds(mult(from_piece * step_rows + start, 16), size)
            dst = r["W" + name].at[ox, at]
            if size:
                copies.append(prepare(dst, dst, b))
        return copies

    def arrived(copies):
        for copy in copies:
            copy.wait_recv()

    half = block // 2
    wa_x = [weight_x("wa", k, 4) for k in range(3)]
    b_x = [send(r[n], r["O" + n], "x") for n in ("bq", "bv", "bu")]

    def divide(ref):
        even, odd = ref[:, 0, :], ref[:, 1, :]
        return jnp.where(x == 0, even, odd), jnp.where(x == 0, odd, even)

    local_x.wait()
    at_mine = pl.ds(own0 + mine, block)
    own_rows, far_rows = divide(r["XI"])
    r["XO"][...] = far_rows
    xs[at_mine, :] = own_rows
    x_x = []
    for k in range(2):
        src = r["XO"].at[pl.ds(k * half, half)]
        x_x.append(send(src, xs.at[pl.ds(own0 + mine + k * half, half)], "x"))
    wa_x.append(weight_x("wa", 3, 4))
    late_x = {(name, k): weight_x(name, k, 2) for name in ("wu", "wd") for k in range(2)}
    wd_far = [weight_x("wd", 1, 2, parts - 1 - piece)] if gbits == 2 else []
    x_c = [send(xs.at[at_mine], xs.at[at_mine], "c")]
    local_c.wait()
    own_rows, far_rows = divide(r["CI"])
    r["CO"][...] = far_rows
    r["CT"][pl.ds(mine, block), :] = own_rows
    c_x = send(r["CO"], r["CT"].at[pl.ds(mine, block)], "x")
    local_w = [local(r[name], r["W" + name].at[x]) for name in ("wu", "wd")]

    bias = r["B"]
    rep = r["R"]
    lane = lax.broadcasted_iota(jnp.int32, (block, 128), 1)
    valid = r["lens"][x]
    for copy in local_v:
        copy.wait()
    for k, name in enumerate(vectors[3:]):
        rep[k : k + 1, :width] = r["V" + name][...].reshape(1, width)

    def set_bias(s, q, v, u):
        bias[s, 0:1, :] = jnp.zeros((1, plan.wide), F32)
        bias[s, 0:1, :hc] = q[...].reshape(1, hc)
        bias[s, 0:1, 2 * hc : 3 * hc] = v[...].reshape(1, hc)
        bias[s, 1:2, :ff] = u[...].reshape(1, ff)

    set_bias(x, r["Vbq"], r["Vbv"], r["Vbu"])
    def project(s, first):
        i = lax.div(first, block)
        at = pl.ds(pl.multiple_of(first, block), block)
        y = dnt(xs[at, :], r["Wwa"][s, : 3 * hc, :]) + bias[s, 0:1, : 3 * hc]
        slot0 = first + block * jnp.where(i == 1, 1, 0) - block * jnp.where(i == 2, 1, 0)
        slot = slot0 + lax.broadcasted_iota(jnp.int32, (block, 128), 0)
        masked = jnp.where(slot < valid, 0.0, NEG)
        real = lane < HEAD_DIM
        k_end = jnp.where(lane == 64, masked, jnp.where(lane < 68, 1.0, 0.0))
        q_end = jnp.where(lane == 64, 1.0, 0.0)
        v_end = jnp.where(lane < 67, 1.0, 0.0)
        for k, (name, end) in enumerate((("QP", q_end), ("KP", k_end), ("VP", v_end))):
            for h in range(heads):
                unit = k * heads + h
                tile = y[:, unit // 2 * 128 : unit // 2 * 128 + 128]
                if unit % 2:
                    tile = pltpu.roll(tile, 64, 1)
                elif unit + 1 == 3 * heads:
                    tile = jnp.concatenate([tile, end[:, HEAD_DIM:]], 1)
                if k == 0:
                    tile = tile * SCALE
                r[name][s * heads + h, at, :] = jnp.where(real, tile, end).astype(BF16)

    def started(copies):
        for copy in copies:
            copy.start()
        return copies

    def frames_at(k, offset):
        return lax.rem(own0 + k * own, slots) + offset

    for copy in local_a:
        copy.wait()
    wa_h, wa_f = [], []
    project(x, frames_at(0, mine))
    for k in range(3):
        wa_x[k].wait_recv()
        wa_h.append(started(weight_hop("wa", k, 4)))
    x_c.pop(0).wait_recv()
    project(x, frames_at(1, mine))
    for k in range(3):
        arrived(wa_h[k])
        wa_f += started(weight_far("wa", k, 4))
    arrived(b_x)
    set_bias(ox, r["Obq"], r["Obv"], r["Obu"])
    for k in range(2):
        x_x[k].wait_recv()
        at_other = pl.ds(own0 + other + k * half, half)
        x_c.append(send(xs.at[at_other], xs.at[at_other], "c"))
    arrived(wa_f)
    for copy in local_w:
        copy.wait()

    @pl.loop(0, 2)
    def _(i):
        project(ox, frames_at(i, mine))

    for k in range(2):
        if k:
            arrived(x_c)

        @pl.loop(0, 2)
        def _(s, k=k):
            project(s, frames_at(k, other))

    wa_x[3].wait_recv()
    wo_h = started(weight_hop("wa", 3, 4))
    wo_f = weight_far("wa", 3, 4)

    row_tiles = [slice(i * block, (i + 1) * block) for i in range(4)]

    def attend(hs):
        queries = [r["QP"][hs, at, :] for at in row_tiles]
        scores = [dnt(q, r["KP"][hs]) for q in queries]
        done = []
        for score in scores:
            top = jnp.max(score, -1, keepdims=True)
            done.append((dn(jnp.exp(score - top).astype(BF16), r["VP"][hs]), top))
        for at, q, (o, top) in zip(row_tiles, queries, done):
            total = o[:, HEAD_DIM : HEAD_DIM + 1]
            r["DC"][hs, at, :] = (o / total).astype(BF16)
            hi, mid, low = split3(-(top + jnp.log(total)))
            ends = jnp.where(lane == 66, mid, jnp.where(lane == 67, low, q.astype(F32)))
            r["QP"][hs, at, :] = jnp.where(lane == 65, hi, ends).astype(BF16)

    chunks = [(name, k) for name in ("wu", "wd") for k in range(2)]
    late_h = {key: weight_hop(*key, 2) for key in chunks}
    late_f = {key: weight_far(*key, 2) for key in chunks}

    def hop(name, k):
        late_x[name, k].wait_recv()
        started(late_h[name, k])

    def far(name, k):
        arrived(late_h[name, k])
        started(late_f[name, k])

    def far_out(name, k):
        arrived(wo_h)
        started(wo_f)

    progress = [(1, far_out, "wa", 3), (1, hop, "wu", 1), (2, far, "wu", 0), (3, hop, "wd", 0)]
    progress += [(4, far, "wu", 1), (5, hop, "wd", 1)]
    hop("wu", 0)

    @pl.loop(0, 2 * heads)
    def _(i):
        attend(lax.rem(x * heads + i, 2 * heads))
        for when, move, name, k in progress:

            @pl.when(i == min(when, 2 * heads - 1))
            def _(move=move, name=name, k=k):
                move(name, k)

    def join(dst, s, parts, first, last):
        @pl.loop(first, last)
        def _(i):
            at = pl.ds(pl.multiple_of(i * block, block), block)
            for t in range(0, len(parts), 2):
                ref, h = parts[t]
                tile = ref[s * heads + h, at, :].astype(F32)
                odd = jnp.zeros_like(tile)
                if t + 1 < len(parts):
                    ref, h = parts[t + 1]
                    odd = pltpu.roll(ref[s * heads + h, at, :].astype(F32), 64, 1)
                tile = jnp.where(lane < HEAD_DIM, tile, odd)
                dst[s, at, t * 64 : t * 64 + 128] = tile.astype(BF16)

    @pl.loop(0, 2)
    def _(s):
        join(r["C"], s, [(r["DC"], h) for h in range(heads)], 0, 4)

    sbuf, rbuf = r["SB"], r["RB"]

    def exchange(partial):
        base = take(2)

        @pl.loop(0, 2)
        def _(i):
            sbuf[i] = partial(row(2 + i)).astype(BF16)
            remote(sbuf.at[i], rbuf.at[i], base + i, "c").start()

        return base

    def received(base, i):
        remote(sbuf.at[i], rbuf.at[i], base + i, "c").wait_recv()
        return rbuf[i].astype(F32)

    def left(base):
        for i in range(2):
            remote(sbuf.at[i], rbuf.at[i], base + i, "c").wait_send()

    def share(buf, base, i):
        at = pl.ds(row(i), block)
        return remote(buf.at[at], buf.at[at], base + i, "c")

    def shared(buf):
        base = take(2)
        copies = [share(buf, base, i) for i in range(2)]
        pending.extend(copies)
        return base, copies

    sums = r["sums"]
    sums[...] = jnp.zeros_like(sums)

    def add_sum(k, v, n=None):
        n = v.shape[-1]
        sums[pl.ds(k, 1), :n] = sums[pl.ds(k, 1), :n] + v

    def attn_out(at0):
        at = pl.ds(at0, block)
        return sum(dn(r["C"][s, at, :hc], r["Wwa"][s, 3 * hc :, :]) for s in range(2))

    arrived(wo_f)
    ex = exchange(attn_out)
    hb_base, hb_c = shared(r["HB"])

    @pl.loop(0, 2)
    def _(i):
        a = attn_out(row(i)) + rep[0:1, :width]
        z = xs[pl.ds(row(i), block), :].astype(F32) + a + received(ex, i)
        z = z - mean(z)
        inv = lax.rsqrt(mean(z * z) + EPS)
        n1 = z * inv
        at = pl.ds(pl.multiple_of(i * block, block), block)
        r["N1"][at, :] = n1
        r["INV"][at, :] = jnp.broadcast_to(inv, (block, 128))
        r["HB"][pl.ds(row(i), block), :] = (n1 * rep[1:2, :width] + rep[2:3, :width]).astype(BF16)
        share(r["HB"], hb_base, i).start()
    left(ex)

    def up(s, first, last):
        @pl.loop(first, last)
        def _(i):
            at = pl.ds(row(i), block)
            u = dn(r["HB"][at, :], r["Wwu"][s]) + bias[s, 1:2, :ff]
            cdf = 0.5 * (1.0 + lax.erf(u * ROOT_HALF))
            r["G"][s, at, :] = (u * cdf).astype(BF16)
            r["SL"][s, at, :] = u.astype(BF16)

    up(x, 0, 2)
    far("wd", 0)
    arrived(hb_c)
    up(x, 2, 4)
    arrived(late_f["wu", 0] + late_f["wu", 1])
    up(ox, 0, 4)

    def ffn_out(at0):
        at = pl.ds(at0, block)
        return dn(r["G"][0, at, :], r["Wwd"][0]) + dn(r["G"][1, at, :], r["Wwd"][1])

    arrived(late_h["wd", 1] + late_f["wd", 0] + wd_far)
    ex = exchange(ffn_out)
    df_base, df_c = shared(r["DF"])
    c_x.wait_recv()

    @pl.loop(0, 2)
    def _(i):
        at = pl.ds(pl.multiple_of(i * block, block), block)
        hidden = r["N1"][at, :] * rep[1:2, :width] + rep[2:3, :width]
        f = ffn_out(row(i)) + rep[3:4, :width]
        z = hidden + f + received(ex, i)
        z = z - mean(z)
        inv = lax.rsqrt(mean(z * z) + EPS)
        n2 = z * inv
        r["OB"][at, :] = (n2 * rep[4:5, :width] + rep[5:6, :width]).astype(BF16)
        dy = r["CT"][at, :].astype(F32)
        add_sum(4, col_sum(dy * n2))
        add_sum(5, col_sum(dy))
        e2 = dy * rep[4:5, :width]
        dz = inv * (e2 - mean(e2) - n2 * mean(e2 * n2))
        r["DZ"][at, :] = dz
        df = dz.astype(BF16)
        add_sum(3, col_sum(df.astype(F32)))
        r["DF"][pl.ds(row(i), block), :] = df
        share(r["DF"], df_base, i).start()
    left(ex)
    out_x = send(r["OB"].at[pl.ds(other, block)], r["out"].at[x], "x")
    out_l = local(r["OB"].at[pl.ds(mine, block)], r["out"].at[x])

    def adder(dst, d, row0, src, sd, n):
        size = chunk_of(n)

        @pl.loop(0, n // size)
        def _(i):
            at = pl.ds(mult(row0 + i * size), size)
            dst[d, at, :] = dst[d, at, :] + src[sd, pl.ds(mult(i * size), size), :]

    def stream(key):
        name, row0, n, order = plan.streams[key]
        grad, final = r["G_" + name], r["F_" + name]
        both, halved, copies, then = True, [], [], []
        for k, (dim, _, n, halve) in enumerate(plan.steps(n, order)):
            got = r["S_%s_%d_%d" % (*key, k)]
            if dim == "x":
                copies.append(prepare(grad.at[ox, pl.ds(row0, n)], got.at[0], "x"))
                both = False
            else:
                sent = row0
                if halve:
                    halved.append(dim)
                    sent = mult(row0 + (1 - bit[dim]) * n)
                    row0 = mult(row0 + bit[dim] * n)
                at = pl.ds(sent, n)
                src = grad.at[:, at] if both else grad.at[x, at]
                copies.append(prepare(src, got if both else got.at[0], dim, halve))

            def add(copy=copies[-1], got=got, row0=row0, n=n, both=both, wait=dim != "x" and not halve):
                if wait:
                    copy.wait_send()
                if both:
                    adder(grad, 0, row0, got, 0, n)
                    adder(grad, 1, row0, got, 1, n)
                else:
                    adder(grad, x, row0, got, 0, n)

            then.append([add])
        keep = local_prepare(grad.at[x, pl.ds(row0, n)], final.at[pl.ds(row0, n)])
        then[-1].append(keep.start)
        src = grad.at[x, pl.ds(row0, n)]
        for dim in reversed(halved):
            at = pl.ds(row0, n)
            copies.append(prepare(src, final.at[at], dim))
            then.append([])
            row0 = mult(row0 - bit[dim] * n)
            n *= 2
            src = final.at[pl.ds(row0, n)]
        then[len(plan.steps(plan.streams[key][2], order)) if halved else -1].append(keep.wait)
        return chain(copies, then)

    def chain(copies, then):
        def move(k):
            if k:
                copies[k - 1].wait_recv()
                for act in then[k - 1]:
                    act()
            if k < len(copies):
                copies[k].start()

        return move

    def sums_stream():
        copies, then = [], []
        for k, who in enumerate(["c", "x"] + list(range(bits))):
            n = 8 if who == "c" else 16
            copy = prepare(sums.at[pl.ds(0, n)], r["SR"].at[k, pl.ds(0, n)], who, False)

            def add(copy=copy, k=k, n=n):
                copy.wait_send()
                sums[0:n, :] = sums[0:n, :] + r["SR"][k, 0:n, :]

            copies.append(copy)
            then.append([add])
        return chain(copies, then)

    movers = {key: stream(key) for key in plan.streams}
    movers["sums"] = sums_stream()
    moves = plan.moves()

    def step(name, when=None):
        if not moves[name]:
            return

        def make():
            for key, k in moves[name]:
                movers[key](k)

        if when is None:
            make()
        else:
            pl.when(when)(make)

    def slope(first, last):
        @pl.loop(first, last)
        def _(i):
            at = pl.ds(row(i), block)
            for s in range(2):
                da = dnt(r["DF"][at, :], r["Wwd"][s])
                u = r["SL"][s, at, :].astype(F32)
                cdf = 0.5 * (1.0 + lax.erf(u * ROOT_HALF))
                du = da * (cdf + u * (DENSITY * jnp.exp(-0.5 * u * u)))
                add_sum(8 + s, col_sum(du))
                r["SL"][s, at, :] = du.astype(BF16)

    def weight_grad(name, lhs, rhs):
        dst = r["G_" + name]
        n = dst.shape[1] // 2

        @pl.loop(0, 4)
        def _(q):
            s, j = lax.rem(ox + q, 2), lax.div(q, 2)
            at = pl.ds(pl.multiple_of(j * n, n), n)
            dst[s, at, :] = dtn(lhs(s, at), rhs(s)).astype(BF16)
            for k in range(4):
                step((name, "os"[k % 2], k // 2), q == k)

    slope(0, 2)
    arrived(df_c)
    weight_grad("down", lambda s, at: r["G"][s, :, at], lambda s: r["DF"][...])
    slope(2, 4)
    step("slope")
    weight_grad("up", lambda s, at: r["HB"][:, at], lambda s: r["SL"][s])

    def hidden_back(at0):
        at = pl.ds(at0, block)
        return dnt(r["SL"][0, at, :], r["Wwu"][0]) + dnt(r["SL"][1, at, :], r["Wwu"][1])

    ex = exchange(hidden_back)
    da_base, da_c = shared(r["DA"])
    step("hidden0")

    @pl.loop(0, 2)
    def _(i):
        at = pl.ds(pl.multiple_of(i * block, block), block)
        dh = r["DZ"][at, :] + hidden_back(row(i))
        dh = dh + received(ex, i)
        n1 = r["N1"][at, :]
        add_sum(1, col_sum(dh * n1))
        add_sum(2, col_sum(dh))
        e1 = dh * rep[1:2, :width]
        dz = r["INV"][at, 0:1] * (e1 - mean(e1) - n1 * mean(e1 * n1))
        r["DZ"][at, :] = dz
        da = dz.astype(BF16)
        add_sum(0, col_sum(da.astype(F32)))
        r["DA"][pl.ds(row(i), block), :] = da
        share(r["DA"], da_base, i).start()
    left(ex)
    step("hidden1")

    rows_e = lax.broadcasted_iota(jnp.int32, (hc, heads * 128), 0)
    lanes_e = lax.broadcasted_iota(jnp.int32, (hc, heads * 128), 1)
    spot = lanes_e - lax.div(rows_e, HEAD_DIM) * 128
    r["E"][...] = jnp.where((spot >= 64) & (spot < 67), -1.0, 0.0).astype(BF16)

    def context_back(first, last):
        @pl.loop(first, last)
        def _(i):
            at = pl.ds(row(i), block)
            for s in range(2):
                dc = dnt(r["DA"][at, :], r["Wwa"][s, 3 * hc :, :]).astype(BF16).astype(F32)
                prod = dc * r["C"][s, at, :hc].astype(F32)
                prod_hi = prod.astype(BF16)
                prod_lo = (prod - prod_hi.astype(F32)).astype(BF16)
                ends = dn(prod_hi, r["E"][...]) + dn(prod_lo, r["E"][...])
                for h in range(heads):
                    end = ends[:, h * 128 : h * 128 + 128]
                    if 2 * h + 2 <= 2 * heads - heads % 2:
                        tile = dc[:, h // 2 * 128 : h // 2 * 128 + 128]
                        if h % 2:
                            tile = pltpu.roll(tile, 64, 1)
                    else:
                        tile = jnp.concatenate([dc[:, h * 64 :], end[:, 64:]], 1)
                    tile = jnp.where(lane < 64, tile, end)
                    hi, mid, low = split3(tile)
                    tile = jnp.where(lane == 65, mid, jnp.where(lane == 66, low, hi))
                    r["DC"][s * heads + h, at, :] = tile.astype(BF16)

    context_back(0, 2)
    step("ctx0")
    arrived(da_c)
    context_back(2, 4)
    step("ctx1")
    @pl.loop(0, 2)
    def _(s):
        r["G_attn"][s, 3 * hc :, :] = dtn(r["C"][s], r["DA"][...])[:hc].astype(BF16)

    step("gout")

    def head_back(hs):
        keys, values = r["KP"].at[hs], r["VP"].at[hs]
        r["KT"][...] = keys[...].T
        queries = [r["QP"][hs, at, :] for at in row_tiles]
        tangents = [r["DC"][hs, at, :] for at in row_tiles]
        scores = [dnt(keys[...], q) for q in queries]
        centred = [dnt(values[...], dc) for dc in tangents]
        dk = dv = 0.0
        dq = []
        for q, dc, score, middle in zip(queries, tangents, scores, centred):
            p = jnp.exp(score)
            ds = (p * middle).astype(BF16)
            dv = dv + dn(p.astype(BF16), dc)
            dk = dk + dn(ds, q)
            dq.append(dn(r["KT"][...], ds).T)
        for at, d in zip(row_tiles, dq):
            r["QP"][hs, at, :] = (d * SCALE).astype(BF16)
        r["KP"][hs] = dk.astype(BF16)
        r["VP"][hs] = dv.astype(BF16)

    g_attn = r["G_attn"]

    @pl.loop(0, 2)
    def _(i):
        s = lax.rem(ox + i, 2)

        @pl.loop(0, heads)
        def _(h):
            head_back(s * heads + h)
            for k in range(2 * heads):
                step(("head", "os"[k // heads], k % heads), i * heads + h == k)

        join(r["D3"], s, [(r[n], h) for n in ("QP", "KP", "VP") for h in range(heads)], 0, 4)
        add_sum(10 + s, col_sum(r["D3"][s].astype(F32)))
        g_attn[s, : 2 * hc, :] = dtn(r["D3"][s, :, : 2 * hc], xs[...]).astype(BF16)
        for k in range(2):
            step(("qk", "os"[k]), i == k)
        grad_v = dtn(r["D3"][s, :, 2 * hc :], xs[...])
        g_attn[s, 2 * hc : 3 * hc, :] = grad_v[:hc].astype(BF16)
        for k in range(2):
            step(("v", "os"[k]), i == k)

    def input_back(at0):
        at = pl.ds(at0, block)
        return sum(dn(r["D3"][s, at, :], r["Wwa"][s, : plan.qkv_cols, :]) for s in range(2))

    ex = exchange(input_back)
    step("dx0")

    @pl.loop(0, 2)
    def _(i):
        at = pl.ds(pl.multiple_of(i * block, block), block)
        dx = r["DZ"][at, :] + input_back(row(i))
        r["DZ"][at, :] = dx + received(ex, i)

    left(ex)
    r["DXS"][...] = r["DZ"][pl.ds(other, block), :].astype(BF16)
    dx_x = send(r["DXS"], r["dx_far"], "x")
    dx_l = local(r["DZ"].at[pl.ds(mine, block)], r["dx_own"])

    step("dx1")
    step("tail")
    r["vec"][...] = sums[...]
    out_x.wait_recv()
    dx_x.wait_recv()
    out_l.wait()
    dx_l.wait()
    for copy in pending:
        copy.wait_send()


def finish(names, *refs):
    r = dict(zip(names, refs))
    sem = r["sem"]
    used = []

    def copy(src, dst):
        made = pltpu.make_async_copy(src, dst, sem.at[len(used)])
        made.start()
        used.append(made)
        return made

    first = lax.axis_index("tp") < 2
    hc = r["g_query"].shape[0]
    targets = {"F_down": ["g_down"], "F_up": ["g_up"]}
    targets["F_attn"] = ["g_query", "g_key", "g_value", "g_out"]
    got = {}
    for n in targets:
        rows = r[n].shape[0] // 4
        for k in range(4):
            at = pl.ds(k * rows, rows)
            got[n, k] = copy(r[n].at[at], r["i_" + n].at[at])
    for n in ("dx_own", "dx_far", "out", "vec"):
        got[n] = copy(r[n], r["i_" + n])
    loads = len(used)
    for n, outs in targets.items():
        rows = r[n].shape[0] // 4
        if len(outs) > 1:
            for k in range(4):
                got[n, k].wait()
        for k in range(4):
            at = pl.ds(k * rows, rows)
            if len(outs) == 1:
                got[n, k].wait()
            r["o_" + n][at, :] = r["i_" + n][at, :].astype(F32)
            target = r[outs[k]] if len(outs) > 1 else r[outs[0]].at[at]
            copy(r["o_" + n].at[at], target)
    got["dx_own"].wait()
    got["dx_far"].wait()
    own, far = r["i_dx_own"][...], r["i_dx_far"][...].astype(F32)
    r["o_dx"][:, 0, :] = jnp.where(first, own, far)
    r["o_dx"][:, 1, :] = jnp.where(first, far, own)
    copy(r["o_dx"], r["dx"])
    got["out"].wait()
    for k in range(2):
        r["o_rows"][:, k, :] = r["i_out"][k]
    copy(r["o_rows"], r["rows"])
    got["vec"].wait()
    vec = r["i_vec"]
    width = r["s_bo"].shape[0]
    for k, n in enumerate(("bo", "g1", "c1", "bd", "g2", "c2")):
        r["s_" + n][...] = vec[k, :width]
    ff = r["s_bu"].shape[0]
    r["s_bu"][...] = jnp.where(first, vec[8, :ff], vec[9, :ff])
    b3 = jnp.where(first, vec[10:11, :], vec[11:12, :])
    r["s_bq"][...] = b3[:, :hc].reshape(hc)
    r["s_bv"][...] = b3[:, 2 * hc : 3 * hc].reshape(hc)
    for made in used[loads:]:
        made.wait()


def local(
    inputs,
    lengths,
    w_query,
    b_query,
    w_key,
    w_value,
    b_value,
    w_out,
    b_out,
    norm1_gain,
    norm1_bias,
    w_up,
    b_up,
    w_down,
    b_down,
    norm2_gain,
    norm2_bias,
    cotangent,
):
    block, utts, width = inputs.shape
    dpn = lax.axis_size("dp")
    plan = Plan(block, width, w_query.shape[1], w_up.shape[1], dpn)
    hc, ff, wide = plan.head_cols, plan.ff, plan.wide
    slots, own, heads = plan.slots, plan.own, plan.heads


    operands = [
        ("inputs", inputs),
        ("cot", cotangent),
        ("lens", lengths),
        ("wq", w_query.T),
        ("wk", w_key.T),
        ("wv", w_value.T),
        ("wo", w_out),
        ("wu", w_up),
        ("wd", w_down),
        ("bq", b_query),
        ("bv", b_value),
        ("bu", b_up),
        ("bo", b_out),
        ("g1", norm1_gain),
        ("c1", norm1_bias),
        ("bd", b_down),
        ("g2", norm2_gain),
        ("c2", norm2_bias),
    ]
    shape_of = jax.ShapeDtypeStruct
    hbm = pl.BlockSpec(memory_space=pl.ANY)
    vmem = pl.BlockSpec(memory_space=pltpu.VMEM)
    smem = pl.BlockSpec(memory_space=pltpu.SMEM)
    outs = [
        ("out", shape_of((2, block, width), BF16), hbm),
        ("dx_own", shape_of((block, width), F32), hbm),
        ("dx_far", shape_of((block, width), BF16), hbm),
        ("vec", shape_of((16, wide), F32), vmem),
    ]
    grads = (
        ("down", ff, width),
        ("up", width, ff),
        ("attn", 4 * hc, width),
    )
    for name, rows, cols in grads:
        outs.append(("F_" + name, shape_of((rows, cols), BF16), hbm))

    def v(name, shape, dtype=BF16):
        return (name, pltpu.VMEM(shape, dtype))

    scratch = [
        v("X", (slots, width)),
        v("Wwa", (2, 4 * hc, width)),
        v("Wwu", (2, width, ff)),
        v("Wwd", (2, ff, width)),
        v("B", (2, 8, wide), F32),
        *(v("V" + n, a.shape, F32) for n, a in operands[-9:]),
        v("Obq", (hc,), F32),
        v("Obv", (hc,), F32),
        v("Obu", (ff,), F32),
        v("R", (8, wide), F32),
        v("XI", (block, utts, width)),
        v("CI", (block, utts, width)),
        v("XO", (block, width)),
        v("CO", (block, width)),
        v("CT", (own, width)),
        v("QP", (2 * heads, slots, 128)),
        v("KP", (2 * heads, slots, 128)),
        v("VP", (2 * heads, slots, 128)),
        v("DC", (2 * heads, slots, 128)),
        v("C", (2, slots, plan.out_cols)),
        v("E", (hc, heads * 128)),
        v("SB", (2, block, width)),
        v("RB", (2, block, width)),
        v("N1", (own, width), F32),
        v("INV", (own, 128), F32),
        v("HB", (slots, width)),
        v("G", (2, slots, ff)),
        v("SL", (2, slots, ff)),
        v("OB", (own, width)),
        v("DZ", (own, width), F32),
        v("DF", (slots, width)),
        v("DA", (slots, width)),
        v("D3", (2, slots, plan.qkv_cols)),
        v("KT", (128, slots)),
        v("DXS", (block, width)),
        v("sums", (16, wide), F32),
        v("SR", (2 + plan.bits, 16, wide), F32),
    ]
    for name, rows, cols in grads:
        scratch.append(v("G_" + name, (2, rows, cols)))
    widths = {name: cols for name, _, cols in grads}
    for key, (name, _, rows, order) in plan.streams.items():
        for k, (_, both, n, _) in enumerate(plan.steps(rows, order)):
            scratch.append(v("S_%s_%d_%d" % (*key, k), (both, n, widths[name])))
    scratch += [
        ("ssem", pltpu.SemaphoreType.DMA((192,))),
        ("rsem", pltpu.SemaphoreType.DMA((192,))),
        ("lsem", pltpu.SemaphoreType.DMA((48,))),
    ]
    names = [n for n, _ in operands] + [n for n, _, _ in outs] + [n for n, _ in scratch]
    results = pl.pallas_call(
        functools.partial(layer, plan, names),
        out_shape=[s for _, s, _ in outs],
        in_specs=[smem if n == "lens" else hbm for n, _ in operands],
        out_specs=[s for _, _, s in outs],
        scratch_shapes=[s for _, s in scratch],
        compiler_params=pltpu.CompilerParams(
            collective_id=0, has_side_effects=True, vmem_limit_bytes=63 * 2**20
        ),
        name="encoder_layer",
    )(*[a for _, a in operands])
    got = dict(zip([n for n, _, _ in outs], results))
    inner = [got[n] for n in ("out", "dx_own", "dx_far", "F_down", "F_up", "F_attn", "vec")]
    inner_names = ["out", "dx_own", "dx_far", "F_down", "F_up", "F_attn", "vec"]
    frames = (block, utts, width)
    final = [("g_down", (ff, width), F32), ("g_up", (width, ff), F32)]
    final += [("dx", frames, F32), ("rows", frames, BF16)]
    final += [(n, (hc, width), F32) for n in ("g_query", "g_key", "g_value", "g_out")]
    small = [("s_" + n, (width,)) for n in ("bo", "g1", "c1", "bd", "g2", "c2")]
    small += [("s_bu", (ff,)), ("s_bq", (hc,)), ("s_bv", (hc,))]
    buffers = [("i_" + n, a.shape, a.dtype) for n, a in zip(inner_names, inner)]
    buffers += [("o_rows", frames, BF16), ("o_dx", frames, F32)]
    buffers += [("o_" + n, got[n].shape, F32) for n in ("F_down", "F_up", "F_attn")]
    labels = inner_names + [n for n, _, _ in final] + [n for n, _ in small]
    labels += [n for n, _, _ in buffers] + ["sem"]
    results = pl.pallas_call(
        functools.partial(finish, labels),
        in_specs=[hbm] * len(inner),
        out_specs=[hbm] * len(final) + [vmem] * len(small),
        out_shape=[shape_of(n, t) for _, n, t in final] + [shape_of(n, F32) for _, n in small],
        scratch_shapes=[pltpu.VMEM(n, t) for _, n, t in buffers]
        + [pltpu.SemaphoreType.DMA((32,))],
        compiler_params=pltpu.CompilerParams(vmem_limit_bytes=60 * 2**20),
        name="finish",
    )(*inner)
    g_down, g_up, input_grad, outputs, g_query, g_key, g_value, g_out = results[:8]
    g_bo, g_g1, g_c1, g_bd, g_g2, g_c2, g_bu, g_bq, g_bv = results[8:]
    return (
        outputs,
        input_grad,
        g_query.T,
        g_bq,
        g_key.T,
        g_value.T,
        g_bv,
        g_out,
        g_bo,
        g_g1,
        g_c1,
        g_up,
        g_bu,
        g_down,
        g_bd,
        g_g2,
        g_c2,
    )


def solution(mesh):
    whole = P()
    rows = P("tp", "dp", None)
    cols = P(None, "tp")
    down = P("tp", None)
    shard = P("tp")
    return jax.shard_map(
        local,
        mesh=mesh,
        in_specs=(
            rows,
            P("dp"),
            cols,
            shard,
            cols,
            cols,
            shard,
            down,
            whole,
            whole,
            whole,
            cols,
            shard,
            down,
            whole,
            whole,
            whole,
            rows,
        ),
        out_specs=(
            rows,
            rows,
            cols,
            shard,
            cols,
            cols,
            shard,
            down,
            whole,
            whole,
            whole,
            cols,
            shard,
            down,
            whole,
            whole,
            whole,
        ),
        check_vma=False,
    )
```

```python
import functools
import math

import jax
import jax.numpy as jnp
from jax import lax
from jax.experimental import pallas as pl
from jax.experimental.pallas import tpu as pltpu
from jax.sharding import PartitionSpec as P

HEAD_DIM = 64
EPS = 1e-05
ROOT_HALF = 0.7071067811865476
DENSITY = 0.3989422804014327
SCALE = 0.125
NEG = -1e30
F32 = jnp.float32
BF16 = jnp.bfloat16


def dn(a, b):
    return lax.dot_general(a, b, (((1,), (0,)), ((), ())), preferred_element_type=F32)


def dnt(a, b):
    return lax.dot_general(a, b, (((1,), (1,)), ((), ())), preferred_element_type=F32)


def dtn(a, b):
    return lax.dot_general(a, b, (((0,), (0,)), ((), ())), preferred_element_type=F32)


def split3(v):
    hi = v.astype(BF16).astype(F32)
    rest = v - hi
    mid = rest.astype(BF16).astype(F32)
    return hi, mid, rest - mid


def mean(v):
    return jnp.mean(v, -1, keepdims=True)


def col_sum(v):
    return jnp.sum(v, 0, keepdims=True)


def chunk_of(n):
    for c in (96, 64, 48, 32, 16):
        if n % c == 0:
            return c
    return n


ORDERS = {
    ('down', 0): [0, 1, 2, 'x'],
    ('down', 1): [1, 0, 'x', 2],
    ('down', 2): [1, 0, 'x', 2],
    ('down', 3): ['x', 0, 1, 2],
    ('up', 0): [0, 1, 'x', 2],
    ('up', 1): [0, 'x', 1, 2],
    ('up', 2): ['x', 0, 1, 2],
    ('up', 3): ['x', 0, 1, 2],
    ('attn', 0): ['x', 0, 1, 2],
    ('attn', 1): ['x', 0, 1, 2],
    ('attn', 2): ['x', 0, 1, 2],
    ('attn', 3): [1, 0, 'x', 2],
}
SCHEDULE = {
    'hidden0': [('down', 1), ('down', 0)],
    'hidden1': [('down', 3)],
    'ctx0': [('up', 0), ('down', 2)],
    'ctx1': [('down', 0), ('up', 2)],
    ('head', 'o', 0): [('up', 0), ('up', 1)],
    ('head', 'o', 1): [('up', 0), ('up', 3), ('down', 1), ('down', 3), ('down', 0)],
    ('head', 'o', 2): [('down', 2), ('up', 1), ('down', 1), ('attn', 3)],
    ('qk', 'o'): [('up', 0), ('down', 3), ('down', 2), ('up', 2), ('down', 0), ('up', 1)],
    ('head', 's', 0): [('up', 0), ('up', 3), ('down', 1)],
    ('head', 's', 1): [('down', 3), ('attn', 3)],
    ('head', 's', 2): [('up', 0), ('down', 2), ('up', 2), ('down', 1), ('down', 0)],
    ('qk', 's'): [('up', 3), ('attn', 1), ('up', 1), ('down', 2), ('down', 3), ('attn', 0)],
    'dx0': [('up', 2), ('down', 0)],
    'dx1': [('attn', 1), ('up', 3), ('attn', 2), ('down', 1), ('attn', 3), ('up', 1), 'sums'],
    "tail": [('down', 3), ('down', 2), ('attn', 0), ('up', 2), ('attn', 1), ('attn', 2), ('up', 3), 'sums', ('attn', 3), ('up', 1), ('attn', 0), ('attn', 1), ('up', 2), ('attn', 2), ('attn', 0), ('up', 3), ('attn', 1), 'sums', ('attn', 2), ('attn', 3), ('attn', 0), 'sums', ('attn', 1), ('attn', 2), ('attn', 0), ('attn', 3), 'sums', ('attn', 2)],
}


class Plan:
    def __init__(self, block, width, head_cols, ff_local, dp):
        self.block = block
        self.slots = 4 * block
        self.own = 2 * block
        self.width = width
        self.head_cols = head_cols
        self.heads = head_cols // HEAD_DIM
        self.ff = ff_local
        self.dp = dp
        self.bits = dp.bit_length() - 1
        self.wide = max(width, ff_local, -(-3 * head_cols // 128) * 128)
        self.qkv_cols = -(-3 * head_cols // 128) * 128
        self.out_cols = -(-head_cols // 128) * 128
        self.streams = {}
        for name, rows in (("down", ff_local), ("up", width), ("attn", 4 * head_cols)):
            for k in range(4):
                n = rows // 4
                self.streams[(name, k)] = (name, k * n, n, self.order((name, k)))

    def order(self, key):
        order = [d for d in ORDERS[key] if d == "x" or d < self.bits]
        return order + list(range(3, self.bits))

    def steps(self, n, order):
        steps, both = [], 2
        for k, dim in enumerate(order):
            if dim == "x":
                both = 1
                steps.append((dim, both, n, False))
                continue
            last = both == 1 and k == len(order) - 1
            halve = not last and (n // 2) % 16 == 0
            if halve:
                n //= 2
            steps.append((dim, both, n, halve))
        return steps


    def x_first(self, key):
        return self.streams[key][3][0] == "x"

    def moves(self):
        events = []

        def point(name, *keys, tags="os"):
            events.append((name, [k for k in keys if ("o" if self.x_first(k) else "s") in tags]))

        for name in ("down", "up"):
            for j in range(2):
                for tag in "os":
                    point((name, tag, j), (name, 2 * j), (name, 2 * j + 1), tags=tag)
            if name == "down":
                point("slope")
        for name in ("hidden0", "hidden1", "ctx0", "ctx1"):
            point(name)
        point("gout", ("attn", 3))
        for tag in "os":
            for h in range(self.heads):
                point(("head", tag, h))
            point(("qk", tag), ("attn", 0), ("attn", 1), tags=tag)
            point(("v", tag), ("attn", 2), tags=tag)
        events += [("dx0", ["sums"]), ("dx1", []), ("tail", [])]
        total = {"sums": 3 + self.bits}
        for key, (_, _, n, order) in self.streams.items():
            steps = self.steps(n, order)
            total[key] = 1 + len(steps) + sum(halve for _, _, _, halve in steps)
        at, moves = {}, {}
        for name, begun in events:
            moves[name] = [(key, 0) for key in begun]
            at.update({key: 1 for key in begun})
            for key in SCHEDULE.get(name, ()):
                if key in at and at[key] < total[key]:
                    moves[name].append((key, at[key]))
                    at[key] += 1
        while any(at[key] < total[key] for key in at):
            for key in at:
                if at[key] < total[key]:
                    moves["tail"].append((key, at[key]))
                    at[key] += 1
        return moves


def layer(plan, names, *refs):
    r = dict(zip(names, refs))
    block, slots, own, width = plan.block, plan.slots, plan.own, plan.width
    hc, heads, ff, dpn, bits = plan.head_cols, plan.heads, plan.ff, plan.dp, plan.bits
    dp = lax.axis_index("dp")
    tp = lax.axis_index("tp")
    x = lax.div(tp, 2)
    c = lax.rem(tp, 2)
    ox = 1 - x
    bit = [lax.rem(lax.div(dp, 1 << b), 2) for b in range(bits)]
    part = {b: (dp + (1 << b) * (1 - 2 * bit[b]), tp) for b in range(bits)}
    part["x"] = (dp, lax.rem(tp + 2, 4))
    part["c"] = (dp, tp + 1 - 2 * c)
    mesh_id = pl.DeviceIdType.MESH

    ssem, rsem, lsem = r["ssem"], r["rsem"], r["lsem"]
    count = {"r": 0, "l": 0}
    pending = []

    def take(n):
        count["r"] += n
        return count["r"] - n

    def remote(src, dst, i, who):
        return pltpu.make_async_remote_copy(
            src_ref=src,
            dst_ref=dst,
            send_sem=ssem.at[i],
            recv_sem=rsem.at[i],
            device_id=part[who],
            device_id_type=mesh_id,
        )

    def prepare(src, dst, who, keep=True):
        copy = remote(src, dst, take(1), who)
        if keep:
            pending.append(copy)
        return copy

    def send(src, dst, who):
        copy = prepare(src, dst, who)
        copy.start()
        return copy

    def local_prepare(src, dst):
        i = count["l"]
        count["l"] += 1
        return pltpu.make_async_copy(src, dst, lsem.at[i])

    def local(src, dst):
        copy = local_prepare(src, dst)
        copy.start()
        return copy

    def mult(v, m=16):
        return pl.multiple_of(v, math.gcd(m, 128))

    def row(i):
        return pl.multiple_of(lax.rem(c * own + i * block, slots), block)

    own0 = pl.multiple_of(c * own, own)
    mine = pl.multiple_of(x * block, block)
    other = pl.multiple_of(ox * block, block)

    xs = r["X"]
    local_a = []
    for k, name in enumerate(("wq", "wk", "wv", "wo")):
        local_a.append(local(r[name], r["Wwa"].at[x, pl.ds(k * hc, hc)]))
    local_x = local(r["inputs"], r["XI"])
    local_c = local(r["cot"], r["CI"])
    vectors = ("bq", "bv", "bu", "bo", "g1", "c1", "bd", "g2", "c2")
    local_v = [local(r[n], r["V" + n]) for n in vectors]
    barrier = pltpu.get_barrier_semaphore()
    for who in part.values():
        pl.semaphore_signal(barrier, inc=1, device_id=who, device_id_type=mesh_id)
    pl.semaphore_wait(barrier, len(part))

    gbits = min(2, bits)
    parts = 1 << gbits
    piece = lax.rem(dp, parts)

    def cut(name, k, of):
        if name == "wa":
            return k * hc, hc // parts, hc // parts
        n = r[name].shape[0] // parts
        return k * n // of, n // of, n

    def weight_x(name, k, of, piece=piece):
        start, size, step_rows = cut(name, k, of)
        src = r[("wq", "wk", "wv", "wo")[k]] if name == "wa" else r[name]
        off = mult(piece * step_rows, 16)
        from_at = pl.ds(off if name == "wa" else mult(off + start, 16), size)
        return send(src.at[from_at], r["W" + name].at[x, pl.ds(mult(off + start, 16), size)], "x")

    def weight_hop(name, k, of):
        start, size, step_rows = cut(name, k, of)
        at = pl.ds(mult(piece * step_rows + start, 16), size)
        dst = r["W" + name].at[ox, at]
        return [prepare(dst, dst, b) for b in range(gbits)]

    def weight_far(name, k, of):
        if gbits < 2:
            return []
        start, size, step_rows = cut(name, k, of)
        if name == "wd" and k == 1:
            return []
        ways = [(k % 2, start, size)]
        if name == "wd":
            low = size // 2 // 16 * 16
            ways = [(0, start, low), (1, start + low, size - low)]
        copies = []
        for b, start, size in ways:
            o = 1 - b
            from_piece = piece + (1 << o) * (1 - 2 * bit[o])
            at = pl.ds(mult(from_piece * step_rows + start, 16), size)
            dst = r["W" + name].at[ox, at]
            if size:
                copies.append(prepare(dst, dst, b))
        return copies

    def arrived(copies):
        for copy in copies:
            copy.wait_recv()

    half = block // 2
    wa_x = [weight_x("wa", k, 4) for k in range(3)]
    b_x = [send(r[n], r["O" + n], "x") for n in ("bq", "bv", "bu")]

    def divide(ref):
        even, odd = ref[:, 0, :], ref[:, 1, :]
        return jnp.where(x == 0, even, odd), jnp.where(x == 0, odd, even)

    local_x.wait()
    at_mine = pl.ds(own0 + mine, block)
    own_rows, far_rows = divide(r["XI"])
    r["XO"][...] = far_rows
    xs[at_mine, :] = own_rows
    x_x = []
    for k in range(2):
        src = r["XO"].at[pl.ds(k * half, half)]
        x_x.append(send(src, xs.at[pl.ds(own0 + mine + k * half, half)], "x"))
    wa_x.append(weight_x("wa", 3, 4))
    late_x = {(name, k): weight_x(name, k, 2) for name in ("wu", "wd") for k in range(2)}
    wd_far = [weight_x("wd", 1, 2, parts - 1 - piece)] if gbits == 2 else []
    x_c = [send(xs.at[at_mine], xs.at[at_mine], "c")]
    local_c.wait()
    own_rows, far_rows = divide(r["CI"])
    r["CO"][...] = far_rows
    r["CT"][pl.ds(mine, block), :] = own_rows
    c_x = send(r["CO"], r["CT"].at[pl.ds(mine, block)], "x")
    local_w = [local(r[name], r["W" + name].at[x]) for name in ("wu", "wd")]

    bias = r["B"]
    rep = r["R"]
    lane = lax.broadcasted_iota(jnp.int32, (block, 128), 1)
    valid = r["lens"][x]
    for copy in local_v:
        copy.wait()
    for k, name in enumerate(vectors[3:]):
        rep[k : k + 1, :width] = r["V" + name][...].reshape(1, width)

    def set_bias(s, q, v, u):
        bias[s, 0:1, :] = jnp.zeros((1, plan.wide), F32)
        bias[s, 0:1, :hc] = q[...].reshape(1, hc)
        bias[s, 0:1, 2 * hc : 3 * hc] = v[...].reshape(1, hc)
        bias[s, 1:2, :ff] = u[...].reshape(1, ff)

    set_bias(x, r["Vbq"], r["Vbv"], r["Vbu"])
    def project(s, first):
        i = lax.div(first, block)
        at = pl.ds(pl.multiple_of(first, block), block)
        y = dnt(xs[at, :], r["Wwa"][s, : 3 * hc, :]) + bias[s, 0:1, : 3 * hc]
        slot0 = first + block * jnp.where(i == 1, 1, 0) - block * jnp.where(i == 2, 1, 0)
        slot = slot0 + lax.broadcasted_iota(jnp.int32, (block, 128), 0)
        masked = jnp.where(slot < valid, 0.0, NEG)
        real = lane < HEAD_DIM
        k_end = jnp.where(lane == 64, masked, jnp.where(lane < 68, 1.0, 0.0))
        q_end = jnp.where(lane == 64, 1.0, 0.0)
        v_end = jnp.where(lane < 67, 1.0, 0.0)
        for k, (name, end) in enumerate((("QP", q_end), ("KP", k_end), ("VP", v_end))):
            for h in range(heads):
                unit = k * heads + h
                tile = y[:, unit // 2 * 128 : unit // 2 * 128 + 128]
                if unit % 2:
                    tile = pltpu.roll(tile, 64, 1)
                elif unit + 1 == 3 * heads:
                    tile = jnp.concatenate([tile, end[:, HEAD_DIM:]], 1)
                if k == 0:
                    tile = tile * SCALE
                r[name][s * heads + h, at, :] = jnp.where(real, tile, end).astype(BF16)

    def started(copies):
        for copy in copies:
            copy.start()
        return copies

    def frames_at(k, offset):
        return lax.rem(own0 + k * own, slots) + offset

    for copy in local_a:
        copy.wait()
    wa_h, wa_f = [], []
    project(x, frames_at(0, mine))
    for k in range(3):
        wa_x[k].wait_recv()
        wa_h.append(started(weight_hop("wa", k, 4)))
    x_c.pop(0).wait_recv()
    project(x, frames_at(1, mine))
    for k in range(3):
        arrived(wa_h[k])
        wa_f += started(weight_far("wa", k, 4))
    arrived(b_x)
    set_bias(ox, r["Obq"], r["Obv"], r["Obu"])
    for k in range(2):
        x_x[k].wait_recv()
        at_other = pl.ds(own0 + other + k * half, half)
        x_c.append(send(xs.at[at_other], xs.at[at_other], "c"))
    arrived(wa_f)
    for copy in local_w:
        copy.wait()

    @pl.loop(0, 2)
    def _(i):
        project(ox, frames_at(i, mine))

    for k in range(2):
        if k:
            arrived(x_c)

        @pl.loop(0, 2)
        def _(s, k=k):
            project(s, frames_at(k, other))

    wa_x[3].wait_recv()
    wo_h = started(weight_hop("wa", 3, 4))
    wo_f = weight_far("wa", 3, 4)

    row_tiles = [slice(i * block, (i + 1) * block) for i in range(4)]

    def attend(hs):
        queries = [r["QP"][hs, at, :] for at in row_tiles]
        scores = [dnt(q, r["KP"][hs]) for q in queries]
        done = []
        for score in scores:
            top = jnp.max(score, -1, keepdims=True)
            done.append((dn(jnp.exp(score - top).astype(BF16), r["VP"][hs]), top))
        for at, q, (o, top) in zip(row_tiles, queries, done):
            total = o[:, HEAD_DIM : HEAD_DIM + 1]
            r["DC"][hs, at, :] = (o / total).astype(BF16)
            hi, mid, low = split3(-(top + jnp.log(total)))
            ends = jnp.where(lane == 66, mid, jnp.where(lane == 67, low, q.astype(F32)))
            r["QP"][hs, at, :] = jnp.where(lane == 65, hi, ends).astype(BF16)

    chunks = [(name, k) for name in ("wu", "wd") for k in range(2)]
    late_h = {key: weight_hop(*key, 2) for key in chunks}
    late_f = {key: weight_far(*key, 2) for key in chunks}

    def hop(name, k):
        late_x[name, k].wait_recv()
        started(late_h[name, k])

    def far(name, k):
        arrived(late_h[name, k])
        started(late_f[name, k])

    def far_out(name, k):
        arrived(wo_h)
        started(wo_f)

    progress = [(1, far_out, "wa", 3), (1, hop, "wu", 1), (2, far, "wu", 0), (3, hop, "wd", 0)]
    progress += [(4, far, "wu", 1), (5, hop, "wd", 1)]
    hop("wu", 0)

    @pl.loop(0, 2 * heads)
    def _(i):
        attend(lax.rem(x * heads + i, 2 * heads))
        for when, move, name, k in progress:

            @pl.when(i == min(when, 2 * heads - 1))
            def _(move=move, name=name, k=k):
                move(name, k)

    def join(dst, s, parts, first, last):
        @pl.loop(first, last)
        def _(i):
            at = pl.ds(pl.multiple_of(i * block, block), block)
            for t in range(0, len(parts), 2):
                ref, h = parts[t]
                tile = ref[s * heads + h, at, :].astype(F32)
                odd = jnp.zeros_like(tile)
                if t + 1 < len(parts):
                    ref, h = parts[t + 1]
                    odd = pltpu.roll(ref[s * heads + h, at, :].astype(F32), 64, 1)
                tile = jnp.where(lane < HEAD_DIM, tile, odd)
                dst[s, at, t * 64 : t * 64 + 128] = tile.astype(BF16)

    @pl.loop(0, 2)
    def _(s):
        join(r["C"], s, [(r["DC"], h) for h in range(heads)], 0, 4)

    sbuf, rbuf = r["SB"], r["RB"]

    def exchange(partial):
        base = take(2)

        @pl.loop(0, 2)
        def _(i):
            sbuf[i] = partial(row(2 + i)).astype(BF16)
            remote(sbuf.at[i], rbuf.at[i], base + i, "c").start()

        return base

    def received(base, i):
        remote(sbuf.at[i], rbuf.at[i], base + i, "c").wait_recv()
        return rbuf[i].astype(F32)

    def left(base):
        for i in range(2):
            remote(sbuf.at[i], rbuf.at[i], base + i, "c").wait_send()

    def share(buf, base, i):
        at = pl.ds(row(i), block)
        return remote(buf.at[at], buf.at[at], base + i, "c")

    def shared(buf):
        base = take(2)
        copies = [share(buf, base, i) for i in range(2)]
        pending.extend(copies)
        return base, copies

    sums = r["sums"]
    sums[...] = jnp.zeros_like(sums)

    def add_sum(k, v, n=None):
        n = v.shape[-1]
        sums[pl.ds(k, 1), :n] = sums[pl.ds(k, 1), :n] + v

    def attn_out(at0):
        at = pl.ds(at0, block)
        return sum(dn(r["C"][s, at, :hc], r["Wwa"][s, 3 * hc :, :]) for s in range(2))

    arrived(wo_f)
    ex = exchange(attn_out)
    hb_base, hb_c = shared(r["HB"])

    @pl.loop(0, 2)
    def _(i):
        a = attn_out(row(i)) + rep[0:1, :width]
        z = xs[pl.ds(row(i), block), :].astype(F32) + a + received(ex, i)
        z = z - mean(z)
        inv = lax.rsqrt(mean(z * z) + EPS)
        n1 = z * inv
        at = pl.ds(pl.multiple_of(i * block, block), block)
        r["N1"][at, :] = n1
        r["INV"][at, :] = jnp.broadcast_to(inv, (block, 128))
        r["HB"][pl.ds(row(i), block), :] = (n1 * rep[1:2, :width] + rep[2:3, :width]).astype(BF16)
        share(r["HB"], hb_base, i).start()
    left(ex)

    def up(s, first, last):
        @pl.loop(first // 2, last // 2)
        def _(i):
            at = pl.ds(pl.multiple_of(row(2 * i), own), own)
            u = dn(r["HB"][at, :], r["Wwu"][s]) + bias[s, 1:2, :ff]
            cdf = 0.5 * (1.0 + lax.erf(u * ROOT_HALF))
            r["G"][s, at, :] = (u * cdf).astype(BF16)
            r["SL"][s, at, :] = u.astype(BF16)

    up(x, 0, 2)
    far("wd", 0)
    arrived(hb_c)
    up(x, 2, 4)
    arrived(late_f["wu", 0] + late_f["wu", 1])
    up(ox, 0, 4)

    def ffn_out(at0):
        at = pl.ds(at0, block)
        return dn(r["G"][0, at, :], r["Wwd"][0]) + dn(r["G"][1, at, :], r["Wwd"][1])

    arrived(late_h["wd", 1] + late_f["wd", 0] + wd_far)
    ex = exchange(ffn_out)
    df_base, df_c = shared(r["DF"])
    c_x.wait_recv()

    @pl.loop(0, 2)
    def _(i):
        at = pl.ds(pl.multiple_of(i * block, block), block)
        hidden = r["N1"][at, :] * rep[1:2, :width] + rep[2:3, :width]
        f = ffn_out(row(i)) + rep[3:4, :width]
        z = hidden + f + received(ex, i)
        z = z - mean(z)
        inv = lax.rsqrt(mean(z * z) + EPS)
        n2 = z * inv
        r["OB"][at, :] = (n2 * rep[4:5, :width] + rep[5:6, :width]).astype(BF16)
        dy = r["CT"][at, :].astype(F32)
        add_sum(4, col_sum(dy * n2))
        add_sum(5, col_sum(dy))
        e2 = dy * rep[4:5, :width]
        dz = inv * (e2 - mean(e2) - n2 * mean(e2 * n2))
        r["DZ"][at, :] = dz
        df = dz.astype(BF16)
        add_sum(3, col_sum(df.astype(F32)))
        r["DF"][pl.ds(row(i), block), :] = df
        share(r["DF"], df_base, i).start()
    left(ex)
    out_x = send(r["OB"].at[pl.ds(other, block)], r["out"].at[x], "x")
    out_l = local(r["OB"].at[pl.ds(mine, block)], r["out"].at[x])

    def adder(dst, d, row0, src, sd, n):
        size = chunk_of(n)

        @pl.loop(0, n // size)
        def _(i):
            at = pl.ds(mult(row0 + i * size), size)
            dst[d, at, :] = dst[d, at, :] + src[sd, pl.ds(mult(i * size), size), :]

    def stream(key):
        name, row0, n, order = plan.streams[key]
        grad, final = r["G_" + name], r["F_" + name]
        both, halved, copies, then = True, [], [], []
        for k, (dim, _, n, halve) in enumerate(plan.steps(n, order)):
            got = r["S_%s_%d_%d" % (*key, k)]
            if dim == "x":
                copies.append(prepare(grad.at[ox, pl.ds(row0, n)], got.at[0], "x"))
                both = False
            else:
                sent = row0
                if halve:
                    halved.append(dim)
                    sent = mult(row0 + (1 - bit[dim]) * n)
                    row0 = mult(row0 + bit[dim] * n)
                at = pl.ds(sent, n)
                src = grad.at[:, at] if both else grad.at[x, at]
                copies.append(prepare(src, got if both else got.at[0], dim, halve))

            def add(copy=copies[-1], got=got, row0=row0, n=n, both=both, wait=dim != "x" and not halve):
                if wait:
                    copy.wait_send()
                if both:
                    adder(grad, 0, row0, got, 0, n)
                    adder(grad, 1, row0, got, 1, n)
                else:
                    adder(grad, x, row0, got, 0, n)

            then.append([add])
        keep = local_prepare(grad.at[x, pl.ds(row0, n)], final.at[pl.ds(row0, n)])
        then[-1].append(keep.start)
        src = grad.at[x, pl.ds(row0, n)]
        for dim in reversed(halved):
            at = pl.ds(row0, n)
            copies.append(prepare(src, final.at[at], dim))
            then.append([])
            row0 = mult(row0 - bit[dim] * n)
            n *= 2
            src = final.at[pl.ds(row0, n)]
        then[len(plan.steps(plan.streams[key][2], order)) if halved else -1].append(keep.wait)
        return chain(copies, then)

    def chain(copies, then):
        def move(k):
            if k:
                copies[k - 1].wait_recv()
                for act in then[k - 1]:
                    act()
            if k < len(copies):
                copies[k].start()

        return move

    def sums_stream():
        copies, then = [], []
        for k, who in enumerate(["c", "x"] + list(range(bits))):
            n = 8 if who == "c" else 16
            copy = prepare(sums.at[pl.ds(0, n)], r["SR"].at[k, pl.ds(0, n)], who, False)

            def add(copy=copy, k=k, n=n):
                copy.wait_send()
                sums[0:n, :] = sums[0:n, :] + r["SR"][k, 0:n, :]

            copies.append(copy)
            then.append([add])
        return chain(copies, then)

    movers = {key: stream(key) for key in plan.streams}
    movers["sums"] = sums_stream()
    moves = plan.moves()

    def step(name, when=None):
        if not moves[name]:
            return

        def make():
            for key, k in moves[name]:
                movers[key](k)

        if when is None:
            make()
        else:
            pl.when(when)(make)

    def slope(first, last):
        @pl.loop(first, last)
        def _(i):
            at = pl.ds(row(i), block)
            grads = [dnt(r["DF"][at, :], r["Wwd"][s]) for s in range(2)]
            ups = [r["SL"][s, at, :].astype(F32) for s in range(2)]
            for s, (da, u) in enumerate(zip(grads, ups)):
                cdf = 0.5 * (1.0 + lax.erf(u * ROOT_HALF))
                du = da * (cdf + u * (DENSITY * jnp.exp(-0.5 * u * u)))
                add_sum(8 + s, col_sum(du))
                r["SL"][s, at, :] = du.astype(BF16)

    def weight_grad(name, lhs, rhs):
        dst = r["G_" + name]
        n = dst.shape[1] // 2

        @pl.loop(0, 4)
        def _(q):
            s, j = lax.rem(ox + q, 2), lax.div(q, 2)
            at = pl.ds(pl.multiple_of(j * n, n), n)
            dst[s, at, :] = dtn(lhs(s, at), rhs(s)).astype(BF16)
            for k in range(4):
                step((name, "os"[k % 2], k // 2), q == k)

    slope(0, 1)
    arrived(df_c)
    weight_grad("down", lambda s, at: r["G"][s, :, at], lambda s: r["DF"][...])
    slope(1, 4)
    step("slope")
    weight_grad("up", lambda s, at: r["HB"][:, at], lambda s: r["SL"][s])

    def hidden_back(at0):
        at = pl.ds(at0, block)
        return dnt(r["SL"][0, at, :], r["Wwu"][0]) + dnt(r["SL"][1, at, :], r["Wwu"][1])

    ex = exchange(hidden_back)
    da_base, da_c = shared(r["DA"])
    step("hidden0")

    @pl.loop(0, 2)
    def _(i):
        at = pl.ds(pl.multiple_of(i * block, block), block)
        dh = r["DZ"][at, :] + hidden_back(row(i))
        dh = dh + received(ex, i)
        n1 = r["N1"][at, :]
        add_sum(1, col_sum(dh * n1))
        add_sum(2, col_sum(dh))
        e1 = dh * rep[1:2, :width]
        dz = r["INV"][at, 0:1] * (e1 - mean(e1) - n1 * mean(e1 * n1))
        r["DZ"][at, :] = dz
        da = dz.astype(BF16)
        add_sum(0, col_sum(da.astype(F32)))
        r["DA"][pl.ds(row(i), block), :] = da
        share(r["DA"], da_base, i).start()
    left(ex)
    step("hidden1")

    rows_e = lax.broadcasted_iota(jnp.int32, (hc, heads * 128), 0)
    lanes_e = lax.broadcasted_iota(jnp.int32, (hc, heads * 128), 1)
    spot = lanes_e - lax.div(rows_e, HEAD_DIM) * 128
    r["E"][...] = jnp.where((spot >= 64) & (spot < 67), -1.0, 0.0).astype(BF16)

    def context_back(first, last):
        @pl.loop(first, last)
        def _(i):
            at = pl.ds(row(i), block)
            for s in range(2):
                dc = dnt(r["DA"][at, :], r["Wwa"][s, 3 * hc :, :]).astype(BF16).astype(F32)
                prod = dc * r["C"][s, at, :hc].astype(F32)
                prod_hi = prod.astype(BF16)
                prod_lo = (prod - prod_hi.astype(F32)).astype(BF16)
                ends = dn(prod_hi, r["E"][...]) + dn(prod_lo, r["E"][...])
                for h in range(heads):
                    end = ends[:, h * 128 : h * 128 + 128]
                    if 2 * h + 2 <= 2 * heads - heads % 2:
                        tile = dc[:, h // 2 * 128 : h // 2 * 128 + 128]
                        if h % 2:
                            tile = pltpu.roll(tile, 64, 1)
                    else:
                        tile = jnp.concatenate([dc[:, h * 64 :], end[:, 64:]], 1)
                    tile = jnp.where(lane < 64, tile, end)
                    hi, mid, low = split3(tile)
                    tile = jnp.where(lane == 65, mid, jnp.where(lane == 66, low, hi))
                    r["DC"][s * heads + h, at, :] = tile.astype(BF16)

    context_back(0, 2)
    step("ctx0")
    arrived(da_c)
    context_back(2, 4)
    step("ctx1")
    @pl.loop(0, 2)
    def _(s):
        r["G_attn"][s, 3 * hc :, :] = dtn(r["C"][s], r["DA"][...])[:hc].astype(BF16)

    step("gout")

    def head_back(hs):
        keys, values = r["KP"].at[hs], r["VP"].at[hs]
        r["KT"][...] = keys[...].T
        queries = [r["QP"][hs, at, :] for at in row_tiles]
        tangents = [r["DC"][hs, at, :] for at in row_tiles]
        scores = [dnt(keys[...], q) for q in queries]
        centred = [dnt(values[...], dc) for dc in tangents]
        dk = dv = 0.0
        dq = []
        for q, dc, score, middle in zip(queries, tangents, scores, centred):
            p = jnp.exp(score)
            ds = (p * middle).astype(BF16)
            dv = dv + dn(p.astype(BF16), dc)
            dk = dk + dn(ds, q)
            dq.append(dn(r["KT"][...], ds).T)
        for at, d in zip(row_tiles, dq):
            r["QP"][hs, at, :] = (d * SCALE).astype(BF16)
        r["KP"][hs] = dk.astype(BF16)
        r["VP"][hs] = dv.astype(BF16)

    g_attn = r["G_attn"]

    @pl.loop(0, 2)
    def _(i):
        s = lax.rem(ox + i, 2)

        @pl.loop(0, heads)
        def _(h):
            head_back(s * heads + h)
            for k in range(2 * heads):
                step(("head", "os"[k // heads], k % heads), i * heads + h == k)

        join(r["D3"], s, [(r[n], h) for n in ("QP", "KP", "VP") for h in range(heads)], 0, 4)
        add_sum(10 + s, col_sum(r["D3"][s].astype(F32)))
        g_attn[s, : 2 * hc, :] = dtn(r["D3"][s, :, : 2 * hc], xs[...]).astype(BF16)
        for k in range(2):
            step(("qk", "os"[k]), i == k)
        grad_v = dtn(r["D3"][s, :, 2 * hc :], xs[...])
        g_attn[s, 2 * hc : 3 * hc, :] = grad_v[:hc].astype(BF16)
        for k in range(2):
            step(("v", "os"[k]), i == k)

    def input_back(at0):
        at = pl.ds(at0, block)
        return sum(dn(r["D3"][s, at, :], r["Wwa"][s, : plan.qkv_cols, :]) for s in range(2))

    ex = exchange(input_back)
    step("dx0")

    @pl.loop(0, 2)
    def _(i):
        at = pl.ds(pl.multiple_of(i * block, block), block)
        dx = r["DZ"][at, :] + input_back(row(i))
        r["DZ"][at, :] = dx + received(ex, i)

    left(ex)
    r["DXS"][...] = r["DZ"][pl.ds(other, block), :].astype(BF16)
    dx_x = send(r["DXS"], r["dx_far"], "x")
    dx_l = local(r["DZ"].at[pl.ds(mine, block)], r["dx_own"])

    step("dx1")
    step("tail")
    vec_l = local(sums, r["vec"])
    out_x.wait_recv()
    dx_x.wait_recv()
    out_l.wait()
    vec_l.wait()
    dx_l.wait()
    for copy in pending:
        copy.wait_send()


def finish(names, *refs):
    r = dict(zip(names, refs))
    sem = r["sem"]
    used = []

    def copy(src, dst):
        made = pltpu.make_async_copy(src, dst, sem.at[len(used)])
        made.start()
        used.append(made)
        return made

    first = lax.axis_index("tp") < 2
    hc = r["g_query"].shape[0]
    targets = {"F_down": ["g_down"], "F_up": ["g_up"]}
    targets["F_attn"] = ["g_query", "g_key", "g_value", "g_out"]
    got = {"vec": copy(r["vec"], r["i_vec"])}
    for n in targets:
        rows = r[n].shape[0] // 4
        for k in range(4):
            at = pl.ds(k * rows, rows)
            got[n, k] = copy(r[n].at[at], r["i_" + n].at[at])
    for n in ("dx_own", "dx_far", "out"):
        got[n] = copy(r[n], r["i_" + n])
    loads = len(used)

    def vectors():
        vec = r["i_vec"]
        width, ff = r["s_bo"].shape[0], r["s_bu"].shape[0]
        got["vec"].wait()
        for k, n in enumerate(("bo", "g1", "c1", "bd", "g2", "c2")):
            r["t_" + n][...] = vec[k, :width]
        r["t_bu"][...] = jnp.where(first, vec[8, :ff], vec[9, :ff])
        b3 = jnp.where(first, vec[10:11, :], vec[11:12, :])
        r["t_bq"][...] = b3[:, :hc].reshape(hc)
        r["t_bv"][...] = b3[:, 2 * hc : 3 * hc].reshape(hc)
        for n in ("bo", "g1", "c1", "bd", "g2", "c2", "bu", "bq", "bv"):
            copy(r["t_" + n], r["s_" + n])

    for n, outs in targets.items():
        if n == "F_up":
            vectors()
        rows = r[n].shape[0] // 4
        if len(outs) > 1:
            for k in range(4):
                got[n, k].wait()
        for k in range(4):
            at = pl.ds(k * rows, rows)
            if len(outs) == 1:
                got[n, k].wait()
            r["o_" + n][at, :] = r["i_" + n][at, :].astype(F32)
            target = r[outs[k]] if len(outs) > 1 else r[outs[0]].at[at]
            copy(r["o_" + n].at[at], target)
    got["dx_own"].wait()
    got["dx_far"].wait()
    own, far = r["i_dx_own"][...], r["i_dx_far"][...].astype(F32)
    r["o_dx"][:, 0, :] = jnp.where(first, own, far)
    r["o_dx"][:, 1, :] = jnp.where(first, far, own)
    copy(r["o_dx"], r["dx"])
    got["out"].wait()
    for k in range(2):
        r["o_rows"][:, k, :] = r["i_out"][k]
    copy(r["o_rows"], r["rows"])
    for made in used[loads:]:
        made.wait()


def local(
    inputs,
    lengths,
    w_query,
    b_query,
    w_key,
    w_value,
    b_value,
    w_out,
    b_out,
    norm1_gain,
    norm1_bias,
    w_up,
    b_up,
    w_down,
    b_down,
    norm2_gain,
    norm2_bias,
    cotangent,
):
    block, utts, width = inputs.shape
    dpn = lax.axis_size("dp")
    plan = Plan(block, width, w_query.shape[1], w_up.shape[1], dpn)
    hc, ff, wide = plan.head_cols, plan.ff, plan.wide
    slots, own, heads = plan.slots, plan.own, plan.heads


    operands = [
        ("inputs", inputs),
        ("cot", cotangent),
        ("lens", lengths),
        ("wq", w_query.T),
        ("wk", w_key.T),
        ("wv", w_value.T),
        ("wo", w_out),
        ("wu", w_up),
        ("wd", w_down),
        ("bq", b_query),
        ("bv", b_value),
        ("bu", b_up),
        ("bo", b_out),
        ("g1", norm1_gain),
        ("c1", norm1_bias),
        ("bd", b_down),
        ("g2", norm2_gain),
        ("c2", norm2_bias),
    ]
    shape_of = jax.ShapeDtypeStruct
    hbm = pl.BlockSpec(memory_space=pl.ANY)
    vmem = pl.BlockSpec(memory_space=pltpu.VMEM)
    smem = pl.BlockSpec(memory_space=pltpu.SMEM)
    outs = [
        ("out", shape_of((2, block, width), BF16), hbm),
        ("dx_own", shape_of((block, width), F32), hbm),
        ("dx_far", shape_of((block, width), BF16), hbm),
        ("vec", shape_of((16, wide), F32), hbm),
    ]
    grads = (
        ("down", ff, width),
        ("up", width, ff),
        ("attn", 4 * hc, width),
    )
    for name, rows, cols in grads:
        outs.append(("F_" + name, shape_of((rows, cols), BF16), hbm))

    def v(name, shape, dtype=BF16):
        return (name, pltpu.VMEM(shape, dtype))

    scratch = [
        v("X", (slots, width)),
        v("Wwa", (2, 4 * hc, width)),
        v("Wwu", (2, width, ff)),
        v("Wwd", (2, ff, width)),
        v("B", (2, 8, wide), F32),
        *(v("V" + n, a.shape, F32) for n, a in operands[-9:]),
        v("Obq", (hc,), F32),
        v("Obv", (hc,), F32),
        v("Obu", (ff,), F32),
        v("R", (8, wide), F32),
        v("XI", (block, utts, width)),
        v("CI", (block, utts, width)),
        v("XO", (block, width)),
        v("CO", (block, width)),
        v("CT", (own, width)),
        v("QP", (2 * heads, slots, 128)),
        v("KP", (2 * heads, slots, 128)),
        v("VP", (2 * heads, slots, 128)),
        v("DC", (2 * heads, slots, 128)),
        v("C", (2, slots, plan.out_cols)),
        v("E", (hc, heads * 128)),
        v("SB", (2, block, width)),
        v("RB", (2, block, width)),
        v("N1", (own, width), F32),
        v("INV", (own, 128), F32),
        v("HB", (slots, width)),
        v("G", (2, slots, ff)),
        v("SL", (2, slots, ff)),
        v("OB", (own, width)),
        v("DZ", (own, width), F32),
        v("DF", (slots, width)),
        v("DA", (slots, width)),
        v("D3", (2, slots, plan.qkv_cols)),
        v("KT", (128, slots)),
        v("DXS", (block, width)),
        v("sums", (16, wide), F32),
        v("SR", (2 + plan.bits, 16, wide), F32),
    ]
    for name, rows, cols in grads:
        scratch.append(v("G_" + name, (2, rows, cols)))
    widths = {name: cols for name, _, cols in grads}
    for key, (name, _, rows, order) in plan.streams.items():
        for k, (_, both, n, _) in enumerate(plan.steps(rows, order)):
            scratch.append(v("S_%s_%d_%d" % (*key, k), (both, n, widths[name])))
    scratch += [
        ("ssem", pltpu.SemaphoreType.DMA((192,))),
        ("rsem", pltpu.SemaphoreType.DMA((192,))),
        ("lsem", pltpu.SemaphoreType.DMA((48,))),
    ]
    names = [n for n, _ in operands] + [n for n, _, _ in outs] + [n for n, _ in scratch]
    results = pl.pallas_call(
        functools.partial(layer, plan, names),
        out_shape=[s for _, s, _ in outs],
        in_specs=[smem if n == "lens" else hbm for n, _ in operands],
        out_specs=[s for _, _, s in outs],
        scratch_shapes=[s for _, s in scratch],
        compiler_params=pltpu.CompilerParams(
            collective_id=0, has_side_effects=True, vmem_limit_bytes=63 * 2**20
        ),
        name="encoder_layer",
    )(*[a for _, a in operands])
    got = dict(zip([n for n, _, _ in outs], results))
    inner = [got[n] for n in ("out", "dx_own", "dx_far", "F_down", "F_up", "F_attn", "vec")]
    inner_names = ["out", "dx_own", "dx_far", "F_down", "F_up", "F_attn", "vec"]
    frames = (block, utts, width)
    final = [("g_down", (ff, width), F32), ("g_up", (width, ff), F32)]
    final += [("dx", frames, F32), ("rows", frames, BF16)]
    final += [(n, (hc, width), F32) for n in ("g_query", "g_key", "g_value", "g_out")]
    small = [("s_" + n, (width,)) for n in ("bo", "g1", "c1", "bd", "g2", "c2")]
    small += [("s_bu", (ff,)), ("s_bq", (hc,)), ("s_bv", (hc,))]
    buffers = [("i_" + n, a.shape, a.dtype) for n, a in zip(inner_names, inner)]
    buffers += [("o_rows", frames, BF16), ("o_dx", frames, F32)]
    buffers += [("t" + n[1:], shape, F32) for n, shape in small]
    buffers += [("o_" + n, got[n].shape, F32) for n in ("F_down", "F_up", "F_attn")]
    labels = inner_names + [n for n, _, _ in final] + [n for n, _ in small]
    labels += [n for n, _, _ in buffers] + ["sem"]
    results = pl.pallas_call(
        functools.partial(finish, labels),
        in_specs=[hbm] * len(inner),
        out_specs=[hbm] * (len(final) + len(small)),
        out_shape=[shape_of(n, t) for _, n, t in final] + [shape_of(n, F32) for _, n in small],
        scratch_shapes=[pltpu.VMEM(n, t) for _, n, t in buffers]
        + [pltpu.SemaphoreType.DMA((64,))],
        compiler_params=pltpu.CompilerParams(vmem_limit_bytes=60 * 2**20),
        name="finish",
    )(*inner)
    g_down, g_up, input_grad, outputs, g_query, g_key, g_value, g_out = results[:8]
    g_bo, g_g1, g_c1, g_bd, g_g2, g_c2, g_bu, g_bq, g_bv = results[8:]
    return (
        outputs,
        input_grad,
        g_query.T,
        g_bq,
        g_key.T,
        g_value.T,
        g_bv,
        g_out,
        g_bo,
        g_g1,
        g_c1,
        g_up,
        g_bu,
        g_down,
        g_bd,
        g_g2,
        g_c2,
    )


def solution(mesh):
    whole = P()
    rows = P("tp", "dp", None)
    cols = P(None, "tp")
    down = P("tp", None)
    shard = P("tp")
    return jax.shard_map(
        local,
        mesh=mesh,
        in_specs=(
            rows,
            P("dp"),
            cols,
            shard,
            cols,
            cols,
            shard,
            down,
            whole,
            whole,
            whole,
            cols,
            shard,
            down,
            whole,
            whole,
            whole,
            rows,
        ),
        out_specs=(
            rows,
            rows,
            cols,
            shard,
            cols,
            cols,
            shard,
            down,
            whole,
            whole,
            whole,
            cols,
            shard,
            down,
            whole,
            whole,
            whole,
        ),
        check_vma=False,
    )
```

```python
import functools
import math

import jax
import jax.numpy as jnp
from jax import lax
from jax.experimental import pallas as pl
from jax.experimental.pallas import tpu as pltpu
from jax.sharding import PartitionSpec as P

HEAD_DIM = 64
EPS = 1e-05
ROOT_HALF = 0.7071067811865476
DENSITY = 0.3989422804014327
SCALE = 0.125
NEG = -1e30
F32 = jnp.float32
BF16 = jnp.bfloat16


def dn(a, b):
    return lax.dot_general(a, b, (((1,), (0,)), ((), ())), preferred_element_type=F32)


def dnt(a, b):
    return lax.dot_general(a, b, (((1,), (1,)), ((), ())), preferred_element_type=F32)


def dtn(a, b):
    return lax.dot_general(a, b, (((0,), (0,)), ((), ())), preferred_element_type=F32)


def split3(v):
    hi = v.astype(BF16).astype(F32)
    rest = v - hi
    mid = rest.astype(BF16).astype(F32)
    return hi, mid, rest - mid


def mean(v):
    return jnp.mean(v, -1, keepdims=True)


def col_sum(v):
    return jnp.sum(v, 0, keepdims=True)


def chunk_of(n):
    for c in (96, 64, 48, 32, 16):
        if n % c == 0:
            return c
    return n


ORDERS = {
    ('down', 0): [0, 1, 2, 'x'],
    ('down', 1): [1, 0, 'x', 2],
    ('down', 2): [1, 0, 'x', 2],
    ('down', 3): ['x', 0, 1, 2],
    ('up', 0): [0, 1, 'x', 2],
    ('up', 1): [0, 'x', 1, 2],
    ('up', 2): ['x', 0, 1, 2],
    ('up', 3): ['x', 0, 1, 2],
    ('attn', 0): ['x', 0, 1, 2],
    ('attn', 1): ['x', 0, 1, 2],
    ('attn', 2): ['x', 0, 1, 2],
    ('attn', 3): [1, 0, 'x', 2],
}
SCHEDULE = {
    'hidden0': [('down', 1), ('down', 0)],
    'hidden1': [('down', 3)],
    'ctx0': [('up', 0), ('down', 2)],
    'ctx1': [('down', 0), ('up', 2)],
    ('head', 'o', 0): [('up', 0), ('up', 1)],
    ('head', 'o', 1): [('up', 0), ('up', 3), ('down', 1), ('down', 3), ('down', 0)],
    ('head', 'o', 2): [('down', 2), ('up', 1), ('down', 1), ('attn', 3)],
    ('qk', 'o'): [('up', 0), ('down', 3), ('down', 2), ('up', 2), ('down', 0), ('up', 1)],
    ('head', 's', 0): [('up', 0), ('up', 3), ('down', 1)],
    ('head', 's', 1): [('down', 3), ('attn', 3)],
    ('head', 's', 2): [('up', 0), ('down', 2), ('up', 2), ('down', 1), ('down', 0)],
    ('qk', 's'): [('up', 3), ('attn', 1), ('up', 1), ('down', 2), ('down', 3), ('attn', 0)],
    'dx0': [('up', 2), ('down', 0)],
    'dx1': [('attn', 1), ('up', 3), ('attn', 2), ('down', 1), ('attn', 3), ('up', 1), 'sums'],
    "tail": [('down', 3), ('down', 2), ('attn', 0), ('up', 2), ('attn', 1), ('attn', 2), ('up', 3), 'sums', ('attn', 3), ('up', 1), ('attn', 0), ('attn', 1), ('up', 2), ('attn', 2), ('attn', 0), ('up', 3), ('attn', 1), 'sums', ('attn', 2), ('attn', 3), ('attn', 0), 'sums', ('attn', 1), ('attn', 2), ('attn', 0), ('attn', 3), 'sums', ('attn', 2)],
}


class Plan:
    def __init__(self, block, width, head_cols, ff_local, dp):
        self.block = block
        self.slots = 4 * block
        self.own = 2 * block
        self.width = width
        self.head_cols = head_cols
        self.heads = head_cols // HEAD_DIM
        self.ff = ff_local
        self.dp = dp
        self.bits = dp.bit_length() - 1
        self.wide = max(width, ff_local, -(-3 * head_cols // 128) * 128)
        self.qkv_cols = -(-3 * head_cols // 128) * 128
        self.out_cols = -(-head_cols // 128) * 128
        self.streams = {}
        for name, rows in (("down", ff_local), ("up", width), ("attn", 4 * head_cols)):
            for k in range(4):
                n = rows // 4
                self.streams[(name, k)] = (name, k * n, n, self.order((name, k)))

    def order(self, key):
        order = [d for d in ORDERS[key] if d == "x" or d < self.bits]
        return order + list(range(3, self.bits))

    def steps(self, n, order):
        steps, both = [], 2
        for k, dim in enumerate(order):
            if dim == "x":
                both = 1
                steps.append((dim, both, n, False))
                continue
            last = both == 1 and k == len(order) - 1
            halve = not last and (n // 2) % 16 == 0
            if halve:
                n //= 2
            steps.append((dim, both, n, halve))
        return steps


    def x_first(self, key):
        return self.streams[key][3][0] == "x"

    def moves(self):
        events = []

        def point(name, *keys, tags="os"):
            events.append((name, [k for k in keys if ("o" if self.x_first(k) else "s") in tags]))

        for name in ("down", "up"):
            for j in range(2):
                for tag in "os":
                    point((name, tag, j), (name, 2 * j), (name, 2 * j + 1), tags=tag)
            if name == "down":
                point("slope")
        for name in ("hidden0", "hidden1", "ctx0", "ctx1"):
            point(name)
        point("gout", ("attn", 3))
        for tag in "os":
            for h in range(self.heads):
                point(("head", tag, h))
            point(("qk", tag), ("attn", 0), ("attn", 1), tags=tag)
            point(("v", tag), ("attn", 2), tags=tag)
        events += [("dx0", ["sums"]), ("dx1", []), ("tail", [])]
        total = {"sums": 3 + self.bits}
        for key, (_, _, n, order) in self.streams.items():
            steps = self.steps(n, order)
            total[key] = 1 + len(steps) + sum(halve for _, _, _, halve in steps)
        at, moves = {}, {}
        for name, begun in events:
            moves[name] = [(key, 0) for key in begun]
            at.update({key: 1 for key in begun})
            for key in SCHEDULE.get(name, ()):
                if key in at and at[key] < total[key]:
                    moves[name].append((key, at[key]))
                    at[key] += 1
        while any(at[key] < total[key] for key in at):
            for key in at:
                if at[key] < total[key]:
                    moves["tail"].append((key, at[key]))
                    at[key] += 1
        return moves


def layer(plan, names, *refs):
    r = dict(zip(names, refs))
    block, slots, own, width = plan.block, plan.slots, plan.own, plan.width
    hc, heads, ff, dpn, bits = plan.head_cols, plan.heads, plan.ff, plan.dp, plan.bits
    dp = lax.axis_index("dp")
    tp = lax.axis_index("tp")
    x = lax.div(tp, 2)
    c = lax.rem(tp, 2)
    ox = 1 - x
    bit = [lax.rem(lax.div(dp, 1 << b), 2) for b in range(bits)]
    part = {b: (dp + (1 << b) * (1 - 2 * bit[b]), tp) for b in range(bits)}
    part["x"] = (dp, lax.rem(tp + 2, 4))
    part["c"] = (dp, tp + 1 - 2 * c)
    mesh_id = pl.DeviceIdType.MESH

    ssem, rsem, lsem = r["ssem"], r["rsem"], r["lsem"]
    count = {"r": 0, "l": 0}
    pending = []

    def take(n):
        count["r"] += n
        return count["r"] - n

    def remote(src, dst, i, who):
        return pltpu.make_async_remote_copy(
            src_ref=src,
            dst_ref=dst,
            send_sem=ssem.at[i],
            recv_sem=rsem.at[i],
            device_id=part[who],
            device_id_type=mesh_id,
        )

    def prepare(src, dst, who, keep=True):
        copy = remote(src, dst, take(1), who)
        if keep:
            pending.append(copy)
        return copy

    def send(src, dst, who):
        copy = prepare(src, dst, who)
        copy.start()
        return copy

    def local_prepare(src, dst):
        i = count["l"]
        count["l"] += 1
        return pltpu.make_async_copy(src, dst, lsem.at[i])

    def local(src, dst):
        copy = local_prepare(src, dst)
        copy.start()
        return copy

    def mult(v, m=16):
        return pl.multiple_of(v, math.gcd(m, 128))

    def row(i):
        return pl.multiple_of(lax.rem(c * own + i * block, slots), block)

    own0 = pl.multiple_of(c * own, own)
    mine = pl.multiple_of(x * block, block)
    other = pl.multiple_of(ox * block, block)

    xs = r["X"]
    local_a = []
    for k, name in enumerate(("wq", "wk", "wv", "wo")):
        local_a.append(local(r[name], r["Wwa"].at[x, pl.ds(k * hc, hc)]))
    local_x = local(r["inputs"], r["XI"])
    local_c = local(r["cot"], r["CI"])
    vectors = ("bq", "bv", "bu", "bo", "g1", "c1", "bd", "g2", "c2")
    local_v = [local(r[n], r["V" + n]) for n in vectors]
    barrier = pltpu.get_barrier_semaphore()
    for who in part.values():
        pl.semaphore_signal(barrier, inc=1, device_id=who, device_id_type=mesh_id)
    pl.semaphore_wait(barrier, len(part))

    gbits = min(2, bits)
    parts = 1 << gbits
    piece = lax.rem(dp, parts)

    def cut(name, k, of):
        if name == "wa":
            return k * hc, hc // parts, hc // parts
        n = r[name].shape[0] // parts
        return k * n // of, n // of, n

    def weight_x(name, k, of, piece=piece):
        start, size, step_rows = cut(name, k, of)
        src = r[("wq", "wk", "wv", "wo")[k]] if name == "wa" else r[name]
        off = mult(piece * step_rows, 16)
        from_at = pl.ds(off if name == "wa" else mult(off + start, 16), size)
        return send(src.at[from_at], r["W" + name].at[x, pl.ds(mult(off + start, 16), size)], "x")

    def weight_hop(name, k, of):
        start, size, step_rows = cut(name, k, of)
        at = pl.ds(mult(piece * step_rows + start, 16), size)
        dst = r["W" + name].at[ox, at]
        return [prepare(dst, dst, b) for b in range(gbits)]

    def weight_far(name, k, of):
        if gbits < 2:
            return []
        start, size, step_rows = cut(name, k, of)
        if name == "wd" and k == 1:
            return []
        ways = [(k % 2, start, size)]
        if name == "wd":
            low = size // 2 // 16 * 16
            ways = [(0, start, low), (1, start + low, size - low)]
        copies = []
        for b, start, size in ways:
            o = 1 - b
            from_piece = piece + (1 << o) * (1 - 2 * bit[o])
            at = pl.ds(mult(from_piece * step_rows + start, 16), size)
            dst = r["W" + name].at[ox, at]
            if size:
                copies.append(prepare(dst, dst, b))
        return copies

    def arrived(copies):
        for copy in copies:
            copy.wait_recv()

    half = block // 2
    wa_x = [weight_x("wa", k, 4) for k in range(3)]
    b_x = [send(r[n], r["O" + n], "x") for n in ("bq", "bv", "bu")]

    def divide(ref):
        even, odd = ref[:, 0, :], ref[:, 1, :]
        return jnp.where(x == 0, even, odd), jnp.where(x == 0, odd, even)

    local_x.wait()
    at_mine = pl.ds(own0 + mine, block)
    own_rows, far_rows = divide(r["XI"])
    r["XO"][...] = far_rows
    xs[at_mine, :] = own_rows
    x_x = []
    for k in range(2):
        src = r["XO"].at[pl.ds(k * half, half)]
        x_x.append(send(src, xs.at[pl.ds(own0 + mine + k * half, half)], "x"))
    wa_x.append(weight_x("wa", 3, 4))
    late_x = {(name, k): weight_x(name, k, 2) for name in ("wu", "wd") for k in range(2)}
    wd_far = [weight_x("wd", 1, 2, parts - 1 - piece)] if gbits == 2 else []
    x_c = [send(xs.at[at_mine], xs.at[at_mine], "c")]
    local_c.wait()
    own_rows, far_rows = divide(r["CI"])
    r["CO"][...] = far_rows
    r["CT"][pl.ds(mine, block), :] = own_rows
    c_x = send(r["CO"], r["CT"].at[pl.ds(mine, block)], "x")
    local_w = [local(r[name], r["W" + name].at[x]) for name in ("wu", "wd")]

    bias = r["B"]
    rep = r["R"]
    lane = lax.broadcasted_iota(jnp.int32, (block, 128), 1)
    valid = r["lens"][x]
    for copy in local_v:
        copy.wait()
    for k, name in enumerate(vectors[3:]):
        rep[k : k + 1, :width] = r["V" + name][...].reshape(1, width)

    def set_bias(s, q, v, u):
        bias[s, 0:1, :] = jnp.zeros((1, plan.wide), F32)
        bias[s, 0:1, :hc] = q[...].reshape(1, hc)
        bias[s, 0:1, 2 * hc : 3 * hc] = v[...].reshape(1, hc)
        bias[s, 1:2, :ff] = u[...].reshape(1, ff)

    set_bias(x, r["Vbq"], r["Vbv"], r["Vbu"])
    def project(s, first):
        i = lax.div(first, block)
        at = pl.ds(pl.multiple_of(first, block), block)
        y = dnt(xs[at, :], r["Wwa"][s, : 3 * hc, :]) + bias[s, 0:1, : 3 * hc]
        slot0 = first + block * jnp.where(i == 1, 1, 0) - block * jnp.where(i == 2, 1, 0)
        slot = slot0 + lax.broadcasted_iota(jnp.int32, (block, 128), 0)
        masked = jnp.where(slot < valid, 0.0, NEG)
        real = lane < HEAD_DIM
        k_end = jnp.where(lane == 64, masked, jnp.where(lane < 68, 1.0, 0.0))
        q_end = jnp.where(lane == 64, 1.0, 0.0)
        v_end = jnp.where(lane < 67, 1.0, 0.0)
        for k, (name, end) in enumerate((("QP", q_end), ("KP", k_end), ("VP", v_end))):
            for h in range(heads):
                unit = k * heads + h
                tile = y[:, unit // 2 * 128 : unit // 2 * 128 + 128]
                if unit % 2:
                    tile = pltpu.roll(tile, 64, 1)
                elif unit + 1 == 3 * heads:
                    tile = jnp.concatenate([tile, end[:, HEAD_DIM:]], 1)
                if k == 0:
                    tile = tile * SCALE
                r[name][s * heads + h, at, :] = jnp.where(real, tile, end).astype(BF16)

    def started(copies):
        for copy in copies:
            copy.start()
        return copies

    def frames_at(k, offset):
        return lax.rem(own0 + k * own, slots) + offset

    for copy in local_a:
        copy.wait()
    wa_h, wa_f = [], []
    project(x, frames_at(0, mine))
    for k in range(3):
        wa_x[k].wait_recv()
        wa_h.append(started(weight_hop("wa", k, 4)))
    x_c.pop(0).wait_recv()
    project(x, frames_at(1, mine))
    for k in range(3):
        arrived(wa_h[k])
        wa_f += started(weight_far("wa", k, 4))
    arrived(b_x)
    set_bias(ox, r["Obq"], r["Obv"], r["Obu"])
    for k in range(2):
        x_x[k].wait_recv()
        at_other = pl.ds(own0 + other + k * half, half)
        x_c.append(send(xs.at[at_other], xs.at[at_other], "c"))
    arrived(wa_f)
    for copy in local_w:
        copy.wait()

    @pl.loop(0, 2)
    def _(i):
        project(ox, frames_at(i, mine))

    for k in range(2):
        if k:
            arrived(x_c)

        @pl.loop(0, 2)
        def _(s, k=k):
            project(s, frames_at(k, other))

    wa_x[3].wait_recv()
    wo_h = started(weight_hop("wa", 3, 4))
    wo_f = weight_far("wa", 3, 4)

    row_tiles = [slice(i * block, (i + 1) * block) for i in range(4)]

    def attend(hs):
        queries = [r["QP"][hs, at, :] for at in row_tiles]
        scores = [dnt(q, r["KP"][hs]) for q in queries]
        done = []
        for score in scores:
            top = jnp.max(score, -1, keepdims=True)
            done.append((dn(jnp.exp(score - top).astype(BF16), r["VP"][hs]), top))
        for at, q, (o, top) in zip(row_tiles, queries, done):
            total = o[:, HEAD_DIM : HEAD_DIM + 1]
            r["DC"][hs, at, :] = (o / total).astype(BF16)
            hi, mid, low = split3(-(top + jnp.log(total)))
            ends = jnp.where(lane == 66, mid, jnp.where(lane == 67, low, q.astype(F32)))
            r["QP"][hs, at, :] = jnp.where(lane == 65, hi, ends).astype(BF16)

    chunks = [(name, k) for name in ("wu", "wd") for k in range(2)]
    late_h = {key: weight_hop(*key, 2) for key in chunks}
    late_f = {key: weight_far(*key, 2) for key in chunks}

    def hop(name, k):
        late_x[name, k].wait_recv()
        started(late_h[name, k])

    def far(name, k):
        arrived(late_h[name, k])
        started(late_f[name, k])

    def far_out(name, k):
        arrived(wo_h)
        started(wo_f)

    progress = [(1, far_out, "wa", 3), (1, hop, "wu", 1), (2, far, "wu", 0), (3, hop, "wd", 0)]
    progress += [(4, far, "wu", 1), (5, hop, "wd", 1)]
    hop("wu", 0)

    @pl.loop(0, 2 * heads)
    def _(i):
        attend(lax.rem(x * heads + i, 2 * heads))
        for when, move, name, k in progress:

            @pl.when(i == min(when, 2 * heads - 1))
            def _(move=move, name=name, k=k):
                move(name, k)

    def join(dst, s, parts, first, last):
        @pl.loop(first, last)
        def _(i):
            at = pl.ds(pl.multiple_of(i * block, block), block)
            for t in range(0, len(parts), 2):
                ref, h = parts[t]
                tile = ref[s * heads + h, at, :].astype(F32)
                odd = jnp.zeros_like(tile)
                if t + 1 < len(parts):
                    ref, h = parts[t + 1]
                    odd = pltpu.roll(ref[s * heads + h, at, :].astype(F32), 64, 1)
                tile = jnp.where(lane < HEAD_DIM, tile, odd)
                dst[s, at, t * 64 : t * 64 + 128] = tile.astype(BF16)

    @pl.loop(0, 2)
    def _(s):
        join(r["C"], s, [(r["DC"], h) for h in range(heads)], 0, 4)

    sbuf, rbuf = r["SB"], r["RB"]

    def exchange(partial):
        base = take(2)

        @pl.loop(0, 2)
        def _(i):
            i = lax.rem(ox + i, 2)
            sbuf[i] = partial(row(2 + i)).astype(BF16)
            remote(sbuf.at[i], rbuf.at[i], base + i, "c").start()

        return base

    def received(base, i):
        remote(sbuf.at[i], rbuf.at[i], base + i, "c").wait_recv()
        return rbuf[i].astype(F32)

    def left(base):
        for i in range(2):
            remote(sbuf.at[i], rbuf.at[i], base + i, "c").wait_send()

    def share(buf, base, i):
        at = pl.ds(row(i), block)
        return remote(buf.at[at], buf.at[at], base + i, "c")

    def shared(buf):
        base = take(2)
        copies = [share(buf, base, i) for i in range(2)]
        pending.extend(copies)
        return base, copies

    sums = r["sums"]
    sums[...] = jnp.zeros_like(sums)

    def add_sum(k, v, n=None):
        n = v.shape[-1]
        sums[pl.ds(k, 1), :n] = sums[pl.ds(k, 1), :n] + v

    def attn_out(at0):
        at = pl.ds(at0, block)
        return sum(dn(r["C"][s, at, :hc], r["Wwa"][s, 3 * hc :, :]) for s in range(2))

    arrived(wo_f)
    ex = exchange(attn_out)
    hb_base, hb_c = shared(r["HB"])

    @pl.loop(0, 2)
    def _(i):
        i = lax.rem(ox + i, 2)
        a = attn_out(row(i)) + rep[0:1, :width]
        z = xs[pl.ds(row(i), block), :].astype(F32) + a + received(ex, i)
        z = z - mean(z)
        inv = lax.rsqrt(mean(z * z) + EPS)
        n1 = z * inv
        at = pl.ds(pl.multiple_of(i * block, block), block)
        r["N1"][at, :] = n1
        r["INV"][at, :] = jnp.broadcast_to(inv, (block, 128))
        r["HB"][pl.ds(row(i), block), :] = (n1 * rep[1:2, :width] + rep[2:3, :width]).astype(BF16)
        share(r["HB"], hb_base, i).start()
    left(ex)

    def up(s, first, last):
        @pl.loop(first // 2, last // 2)
        def _(i):
            at = pl.ds(pl.multiple_of(row(2 * i), own), own)
            u = dn(r["HB"][at, :], r["Wwu"][s]) + bias[s, 1:2, :ff]
            cdf = 0.5 * (1.0 + lax.erf(u * ROOT_HALF))
            r["G"][s, at, :] = (u * cdf).astype(BF16)
            r["SL"][s, at, :] = u.astype(BF16)

    up(x, 0, 2)
    far("wd", 0)
    arrived(hb_c)
    up(x, 2, 4)
    arrived(late_f["wu", 0] + late_f["wu", 1])
    up(ox, 0, 4)

    def ffn_out(at0):
        at = pl.ds(at0, block)
        return dn(r["G"][0, at, :], r["Wwd"][0]) + dn(r["G"][1, at, :], r["Wwd"][1])

    arrived(late_h["wd", 1] + late_f["wd", 0] + wd_far)
    ex = exchange(ffn_out)
    out_x = prepare(r["OB"].at[pl.ds(other, block)], r["out"].at[x], "x")
    df_base, df_c = shared(r["DF"])
    c_x.wait_recv()

    @pl.loop(0, 2)
    def _(step_):
        i = lax.rem(ox + step_, 2)
        at = pl.ds(pl.multiple_of(i * block, block), block)
        hidden = r["N1"][at, :] * rep[1:2, :width] + rep[2:3, :width]
        f = ffn_out(row(i)) + rep[3:4, :width]
        z = hidden + f + received(ex, i)
        z = z - mean(z)
        inv = lax.rsqrt(mean(z * z) + EPS)
        n2 = z * inv
        r["OB"][at, :] = (n2 * rep[4:5, :width] + rep[5:6, :width]).astype(BF16)
        pl.when(step_ == 0)(out_x.start)
        dy = r["CT"][at, :].astype(F32)
        add_sum(4, col_sum(dy * n2))
        add_sum(5, col_sum(dy))
        e2 = dy * rep[4:5, :width]
        dz = inv * (e2 - mean(e2) - n2 * mean(e2 * n2))
        r["DZ"][at, :] = dz
        df = dz.astype(BF16)
        add_sum(3, col_sum(df.astype(F32)))
        r["DF"][pl.ds(row(i), block), :] = df
        share(r["DF"], df_base, i).start()
    left(ex)
    out_l = local(r["OB"].at[pl.ds(mine, block)], r["out"].at[x])

    def adder(dst, d, row0, src, sd, n):
        size = chunk_of(n)

        @pl.loop(0, n // size)
        def _(i):
            at = pl.ds(mult(row0 + i * size), size)
            dst[d, at, :] = dst[d, at, :] + src[sd, pl.ds(mult(i * size), size), :]

    def stream(key):
        name, row0, n, order = plan.streams[key]
        grad, final = r["G_" + name], r["F_" + name]
        both, halved, copies, then = True, [], [], []
        for k, (dim, _, n, halve) in enumerate(plan.steps(n, order)):
            got = r["S_%s_%d_%d" % (*key, k)]
            if dim == "x":
                copies.append(prepare(grad.at[ox, pl.ds(row0, n)], got.at[0], "x"))
                both = False
            else:
                sent = row0
                if halve:
                    halved.append(dim)
                    sent = mult(row0 + (1 - bit[dim]) * n)
                    row0 = mult(row0 + bit[dim] * n)
                at = pl.ds(sent, n)
                src = grad.at[:, at] if both else grad.at[x, at]
                copies.append(prepare(src, got if both else got.at[0], dim, halve))

            def add(copy=copies[-1], got=got, row0=row0, n=n, both=both, wait=dim != "x" and not halve):
                if wait:
                    copy.wait_send()
                if both:
                    adder(grad, 0, row0, got, 0, n)
                    adder(grad, 1, row0, got, 1, n)
                else:
                    adder(grad, x, row0, got, 0, n)

            then.append([add])
        keep = local_prepare(grad.at[x, pl.ds(row0, n)], final.at[pl.ds(row0, n)])
        then[-1].append(keep.start)
        src = grad.at[x, pl.ds(row0, n)]
        for dim in reversed(halved):
            at = pl.ds(row0, n)
            copies.append(prepare(src, final.at[at], dim))
            then.append([])
            row0 = mult(row0 - bit[dim] * n)
            n *= 2
            src = final.at[pl.ds(row0, n)]
        then[len(plan.steps(plan.streams[key][2], order)) if halved else -1].append(keep.wait)
        return chain(copies, then)

    def chain(copies, then):
        def move(k):
            if k:
                copies[k - 1].wait_recv()
                for act in then[k - 1]:
                    act()
            if k < len(copies):
                copies[k].start()

        return move

    def sums_stream():
        copies, then = [], []
        for k, who in enumerate(["c", "x"] + list(range(bits))):
            n = 8 if who == "c" else 16
            copy = prepare(sums.at[pl.ds(0, n)], r["SR"].at[k, pl.ds(0, n)], who, False)

            def add(copy=copy, k=k, n=n):
                copy.wait_send()
                sums[0:n, :] = sums[0:n, :] + r["SR"][k, 0:n, :]

            copies.append(copy)
            then.append([add])
        return chain(copies, then)

    movers = {key: stream(key) for key in plan.streams}
    movers["sums"] = sums_stream()
    moves = plan.moves()

    def step(name, when=None):
        if not moves[name]:
            return

        def make():
            for key, k in moves[name]:
                movers[key](k)

        if when is None:
            make()
        else:
            pl.when(when)(make)

    def slope(first, last):
        @pl.loop(first, last)
        def _(i):
            at = pl.ds(row(i), block)
            grads = [dnt(r["DF"][at, :], r["Wwd"][s]) for s in range(2)]
            ups = [r["SL"][s, at, :].astype(F32) for s in range(2)]
            for s, (da, u) in enumerate(zip(grads, ups)):
                cdf = 0.5 * (1.0 + lax.erf(u * ROOT_HALF))
                du = da * (cdf + u * (DENSITY * jnp.exp(-0.5 * u * u)))
                add_sum(8 + s, col_sum(du))
                r["SL"][s, at, :] = du.astype(BF16)

    def weight_grad(name, lhs, rhs):
        dst = r["G_" + name]
        n = dst.shape[1] // 2

        @pl.loop(0, 4)
        def _(q):
            s, j = lax.rem(ox + q, 2), lax.div(q, 2)
            at = pl.ds(pl.multiple_of(j * n, n), n)
            dst[s, at, :] = dtn(lhs(s, at), rhs(s)).astype(BF16)
            for k in range(4):
                step((name, "os"[k % 2], k // 2), q == k)

    slope(0, 1)
    arrived(df_c)
    weight_grad("down", lambda s, at: r["G"][s, :, at], lambda s: r["DF"][...])
    slope(1, 4)
    step("slope")
    weight_grad("up", lambda s, at: r["HB"][:, at], lambda s: r["SL"][s])

    def hidden_back(at0):
        at = pl.ds(at0, block)
        return dnt(r["SL"][0, at, :], r["Wwu"][0]) + dnt(r["SL"][1, at, :], r["Wwu"][1])

    ex = exchange(hidden_back)
    da_base, da_c = shared(r["DA"])
    step("hidden0")

    @pl.loop(0, 2)
    def _(i):
        i = lax.rem(ox + i, 2)
        at = pl.ds(pl.multiple_of(i * block, block), block)
        dh = r["DZ"][at, :] + hidden_back(row(i))
        dh = dh + received(ex, i)
        n1 = r["N1"][at, :]
        add_sum(1, col_sum(dh * n1))
        add_sum(2, col_sum(dh))
        e1 = dh * rep[1:2, :width]
        dz = r["INV"][at, 0:1] * (e1 - mean(e1) - n1 * mean(e1 * n1))
        r["DZ"][at, :] = dz
        da = dz.astype(BF16)
        add_sum(0, col_sum(da.astype(F32)))
        r["DA"][pl.ds(row(i), block), :] = da
        share(r["DA"], da_base, i).start()
    left(ex)
    step("hidden1")

    rows_e = lax.broadcasted_iota(jnp.int32, (hc, heads * 128), 0)
    lanes_e = lax.broadcasted_iota(jnp.int32, (hc, heads * 128), 1)
    spot = lanes_e - lax.div(rows_e, HEAD_DIM) * 128
    r["E"][...] = jnp.where((spot >= 64) & (spot < 67), -1.0, 0.0).astype(BF16)

    def context_back(first, last):
        @pl.loop(first, last)
        def _(i):
            at = pl.ds(row(i), block)
            for s in range(2):
                dc = dnt(r["DA"][at, :], r["Wwa"][s, 3 * hc :, :]).astype(BF16).astype(F32)
                prod = dc * r["C"][s, at, :hc].astype(F32)
                prod_hi = prod.astype(BF16)
                prod_lo = (prod - prod_hi.astype(F32)).astype(BF16)
                ends = dn(prod_hi, r["E"][...]) + dn(prod_lo, r["E"][...])
                for h in range(heads):
                    end = ends[:, h * 128 : h * 128 + 128]
                    if 2 * h + 2 <= 2 * heads - heads % 2:
                        tile = dc[:, h // 2 * 128 : h // 2 * 128 + 128]
                        if h % 2:
                            tile = pltpu.roll(tile, 64, 1)
                    else:
                        tile = jnp.concatenate([dc[:, h * 64 :], end[:, 64:]], 1)
                    tile = jnp.where(lane < 64, tile, end)
                    hi, mid, low = split3(tile)
                    tile = jnp.where(lane == 65, mid, jnp.where(lane == 66, low, hi))
                    r["DC"][s * heads + h, at, :] = tile.astype(BF16)

    context_back(0, 2)
    step("ctx0")
    arrived(da_c)
    context_back(2, 4)
    step("ctx1")
    @pl.loop(0, 2)
    def _(s):
        r["G_attn"][s, 3 * hc :, :] = dtn(r["C"][s], r["DA"][...])[:hc].astype(BF16)

    step("gout")

    def head_back(hs):
        keys, values = r["KP"].at[hs], r["VP"].at[hs]
        r["KT"][...] = keys[...].T
        queries = [r["QP"][hs, at, :] for at in row_tiles]
        tangents = [r["DC"][hs, at, :] for at in row_tiles]
        scores = [dnt(keys[...], q) for q in queries]
        centred = [dnt(values[...], dc) for dc in tangents]
        dk = dv = 0.0
        dq = []
        for q, dc, score, middle in zip(queries, tangents, scores, centred):
            p = jnp.exp(score)
            ds = (p * middle).astype(BF16)
            dv = dv + dn(p.astype(BF16), dc)
            dk = dk + dn(ds, q)
            dq.append(dn(r["KT"][...], ds).T)
        for at, d in zip(row_tiles, dq):
            r["QP"][hs, at, :] = (d * SCALE).astype(BF16)
        r["KP"][hs] = dk.astype(BF16)
        r["VP"][hs] = dv.astype(BF16)

    g_attn = r["G_attn"]

    @pl.loop(0, 2)
    def _(i):
        s = lax.rem(ox + i, 2)

        @pl.loop(0, heads)
        def _(h):
            head_back(s * heads + h)
            for k in range(2 * heads):
                step(("head", "os"[k // heads], k % heads), i * heads + h == k)

        join(r["D3"], s, [(r[n], h) for n in ("QP", "KP", "VP") for h in range(heads)], 0, 4)
        add_sum(10 + s, col_sum(r["D3"][s].astype(F32)))
        g_attn[s, : 2 * hc, :] = dtn(r["D3"][s, :, : 2 * hc], xs[...]).astype(BF16)
        for k in range(2):
            step(("qk", "os"[k]), i == k)
        grad_v = dtn(r["D3"][s, :, 2 * hc :], xs[...])
        g_attn[s, 2 * hc : 3 * hc, :] = grad_v[:hc].astype(BF16)
        for k in range(2):
            step(("v", "os"[k]), i == k)

    def input_back(at0):
        at = pl.ds(at0, block)
        return sum(dn(r["D3"][s, at, :], r["Wwa"][s, : plan.qkv_cols, :]) for s in range(2))

    ex = exchange(input_back)
    step("dx0")

    @pl.loop(0, 2)
    def _(i):
        i = lax.rem(ox + i, 2)
        at = pl.ds(pl.multiple_of(i * block, block), block)
        dx = r["DZ"][at, :] + input_back(row(i))
        r["DZ"][at, :] = dx + received(ex, i)

    left(ex)
    r["DXS"][...] = r["DZ"][pl.ds(other, block), :].astype(BF16)
    dx_x = send(r["DXS"], r["dx_far"], "x")
    dx_l = local(r["DZ"].at[pl.ds(mine, block)], r["dx_own"])

    step("dx1")
    step("tail")
    vec_l = local(sums, r["vec"])
    out_x.wait_recv()
    dx_x.wait_recv()
    out_l.wait()
    vec_l.wait()
    dx_l.wait()
    for copy in pending:
        copy.wait_send()


def finish(names, *refs):
    r = dict(zip(names, refs))
    sem = r["sem"]
    used = []

    def copy(src, dst):
        made = pltpu.make_async_copy(src, dst, sem.at[len(used)])
        made.start()
        used.append(made)
        return made

    first = lax.axis_index("tp") < 2
    hc = r["g_query"].shape[0]
    targets = {"F_down": ["g_down"], "F_up": ["g_up"]}
    targets["F_attn"] = ["g_query", "g_key", "g_value", "g_out"]
    got = {"vec": copy(r["vec"], r["i_vec"])}
    for n in targets:
        rows = r[n].shape[0] // 4
        for k in range(4):
            at = pl.ds(k * rows, rows)
            got[n, k] = copy(r[n].at[at], r["i_" + n].at[at])
    for n in ("dx_own", "dx_far", "out"):
        got[n] = copy(r[n], r["i_" + n])
    loads = len(used)

    def vectors():
        vec = r["i_vec"]
        width, ff = r["s_bo"].shape[0], r["s_bu"].shape[0]
        got["vec"].wait()
        for k, n in enumerate(("bo", "g1", "c1", "bd", "g2", "c2")):
            r["t_" + n][...] = vec[k, :width]
        r["t_bu"][...] = jnp.where(first, vec[8, :ff], vec[9, :ff])
        b3 = jnp.where(first, vec[10:11, :], vec[11:12, :])
        r["t_bq"][...] = b3[:, :hc].reshape(hc)
        r["t_bv"][...] = b3[:, 2 * hc : 3 * hc].reshape(hc)
        for n in ("bo", "g1", "c1", "bd", "g2", "c2", "bu", "bq", "bv"):
            copy(r["t_" + n], r["s_" + n])

    for n, outs in targets.items():
        if n == "F_up":
            vectors()
        rows = r[n].shape[0] // 4
        if len(outs) > 1:
            for k in range(4):
                got[n, k].wait()
        for k in range(4):
            at = pl.ds(k * rows, rows)
            if len(outs) == 1:
                got[n, k].wait()
            r["o_" + n][at, :] = r["i_" + n][at, :].astype(F32)
            target = r[outs[k]] if len(outs) > 1 else r[outs[0]].at[at]
            copy(r["o_" + n].at[at], target)
    got["dx_own"].wait()
    got["dx_far"].wait()
    own, far = r["i_dx_own"][...], r["i_dx_far"][...].astype(F32)
    r["o_dx"][:, 0, :] = jnp.where(first, own, far)
    r["o_dx"][:, 1, :] = jnp.where(first, far, own)
    copy(r["o_dx"], r["dx"])
    got["out"].wait()
    for k in range(2):
        r["o_rows"][:, k, :] = r["i_out"][k]
    copy(r["o_rows"], r["rows"])
    for made in used[loads:]:
        made.wait()


def local(
    inputs,
    lengths,
    w_query,
    b_query,
    w_key,
    w_value,
    b_value,
    w_out,
    b_out,
    norm1_gain,
    norm1_bias,
    w_up,
    b_up,
    w_down,
    b_down,
    norm2_gain,
    norm2_bias,
    cotangent,
):
    block, utts, width = inputs.shape
    dpn = lax.axis_size("dp")
    plan = Plan(block, width, w_query.shape[1], w_up.shape[1], dpn)
    hc, ff, wide = plan.head_cols, plan.ff, plan.wide
    slots, own, heads = plan.slots, plan.own, plan.heads


    operands = [
        ("inputs", inputs),
        ("cot", cotangent),
        ("lens", lengths),
        ("wq", w_query.T),
        ("wk", w_key.T),
        ("wv", w_value.T),
        ("wo", w_out),
        ("wu", w_up),
        ("wd", w_down),
        ("bq", b_query),
        ("bv", b_value),
        ("bu", b_up),
        ("bo", b_out),
        ("g1", norm1_gain),
        ("c1", norm1_bias),
        ("bd", b_down),
        ("g2", norm2_gain),
        ("c2", norm2_bias),
    ]
    shape_of = jax.ShapeDtypeStruct
    hbm = pl.BlockSpec(memory_space=pl.ANY)
    vmem = pl.BlockSpec(memory_space=pltpu.VMEM)
    smem = pl.BlockSpec(memory_space=pltpu.SMEM)
    outs = [
        ("out", shape_of((2, block, width), BF16), hbm),
        ("dx_own", shape_of((block, width), F32), hbm),
        ("dx_far", shape_of((block, width), BF16), hbm),
        ("vec", shape_of((16, wide), F32), hbm),
    ]
    grads = (
        ("down", ff, width),
        ("up", width, ff),
        ("attn", 4 * hc, width),
    )
    for name, rows, cols in grads:
        outs.append(("F_" + name, shape_of((rows, cols), BF16), hbm))

    def v(name, shape, dtype=BF16):
        return (name, pltpu.VMEM(shape, dtype))

    scratch = [
        v("X", (slots, width)),
        v("Wwa", (2, 4 * hc, width)),
        v("Wwu", (2, width, ff)),
        v("Wwd", (2, ff, width)),
        v("B", (2, 8, wide), F32),
        *(v("V" + n, a.shape, F32) for n, a in operands[-9:]),
        v("Obq", (hc,), F32),
        v("Obv", (hc,), F32),
        v("Obu", (ff,), F32),
        v("R", (8, wide), F32),
        v("XI", (block, utts, width)),
        v("CI", (block, utts, width)),
        v("XO", (block, width)),
        v("CO", (block, width)),
        v("CT", (own, width)),
        v("QP", (2 * heads, slots, 128)),
        v("KP", (2 * heads, slots, 128)),
        v("VP", (2 * heads, slots, 128)),
        v("DC", (2 * heads, slots, 128)),
        v("C", (2, slots, plan.out_cols)),
        v("E", (hc, heads * 128)),
        v("SB", (2, block, width)),
        v("RB", (2, block, width)),
        v("N1", (own, width), F32),
        v("INV", (own, 128), F32),
        v("HB", (slots, width)),
        v("G", (2, slots, ff)),
        v("SL", (2, slots, ff)),
        v("OB", (own, width)),
        v("DZ", (own, width), F32),
        v("DF", (slots, width)),
        v("DA", (slots, width)),
        v("D3", (2, slots, plan.qkv_cols)),
        v("KT", (128, slots)),
        v("DXS", (block, width)),
        v("sums", (16, wide), F32),
        v("SR", (2 + plan.bits, 16, wide), F32),
    ]
    for name, rows, cols in grads:
        scratch.append(v("G_" + name, (2, rows, cols)))
    widths = {name: cols for name, _, cols in grads}
    for key, (name, _, rows, order) in plan.streams.items():
        for k, (_, both, n, _) in enumerate(plan.steps(rows, order)):
            scratch.append(v("S_%s_%d_%d" % (*key, k), (both, n, widths[name])))
    scratch += [
        ("ssem", pltpu.SemaphoreType.DMA((192,))),
        ("rsem", pltpu.SemaphoreType.DMA((192,))),
        ("lsem", pltpu.SemaphoreType.DMA((48,))),
    ]
    names = [n for n, _ in operands] + [n for n, _, _ in outs] + [n for n, _ in scratch]
    results = pl.pallas_call(
        functools.partial(layer, plan, names),
        out_shape=[s for _, s, _ in outs],
        in_specs=[smem if n == "lens" else hbm for n, _ in operands],
        out_specs=[s for _, _, s in outs],
        scratch_shapes=[s for _, s in scratch],
        compiler_params=pltpu.CompilerParams(
            collective_id=0, has_side_effects=True, vmem_limit_bytes=63 * 2**20
        ),
        name="encoder_layer",
    )(*[a for _, a in operands])
    got = dict(zip([n for n, _, _ in outs], results))
    inner = [got[n] for n in ("out", "dx_own", "dx_far", "F_down", "F_up", "F_attn", "vec")]
    inner_names = ["out", "dx_own", "dx_far", "F_down", "F_up", "F_attn", "vec"]
    frames = (block, utts, width)
    final = [("g_down", (ff, width), F32), ("g_up", (width, ff), F32)]
    final += [("dx", frames, F32), ("rows", frames, BF16)]
    final += [(n, (hc, width), F32) for n in ("g_query", "g_key", "g_value", "g_out")]
    small = [("s_" + n, (width,)) for n in ("bo", "g1", "c1", "bd", "g2", "c2")]
    small += [("s_bu", (ff,)), ("s_bq", (hc,)), ("s_bv", (hc,))]
    buffers = [("i_" + n, a.shape, a.dtype) for n, a in zip(inner_names, inner)]
    buffers += [("o_rows", frames, BF16), ("o_dx", frames, F32)]
    buffers += [("t" + n[1:], shape, F32) for n, shape in small]
    buffers += [("o_" + n, got[n].shape, F32) for n in ("F_down", "F_up", "F_attn")]
    labels = inner_names + [n for n, _, _ in final] + [n for n, _ in small]
    labels += [n for n, _, _ in buffers] + ["sem"]
    results = pl.pallas_call(
        functools.partial(finish, labels),
        in_specs=[hbm] * len(inner),
        out_specs=[hbm] * (len(final) + len(small)),
        out_shape=[shape_of(n, t) for _, n, t in final] + [shape_of(n, F32) for _, n in small],
        scratch_shapes=[pltpu.VMEM(n, t) for _, n, t in buffers]
        + [pltpu.SemaphoreType.DMA((64,))],
        compiler_params=pltpu.CompilerParams(vmem_limit_bytes=60 * 2**20),
        name="finish",
    )(*inner)
    g_down, g_up, input_grad, outputs, g_query, g_key, g_value, g_out = results[:8]
    g_bo, g_g1, g_c1, g_bd, g_g2, g_c2, g_bu, g_bq, g_bv = results[8:]
    return (
        outputs,
        input_grad,
        g_query.T,
        g_bq,
        g_key.T,
        g_value.T,
        g_bv,
        g_out,
        g_bo,
        g_g1,
        g_c1,
        g_up,
        g_bu,
        g_down,
        g_bd,
        g_g2,
        g_c2,
    )


def solution(mesh):
    whole = P()
    rows = P("tp", "dp", None)
    cols = P(None, "tp")
    down = P("tp", None)
    shard = P("tp")
    return jax.shard_map(
        local,
        mesh=mesh,
        in_specs=(
            rows,
            P("dp"),
            cols,
            shard,
            cols,
            cols,
            shard,
            down,
            whole,
            whole,
            whole,
            cols,
            shard,
            down,
            whole,
            whole,
            whole,
            rows,
        ),
        out_specs=(
            rows,
            rows,
            cols,
            shard,
            cols,
            cols,
            shard,
            down,
            whole,
            whole,
            whole,
            cols,
            shard,
            down,
            whole,
            whole,
            whole,
        ),
        check_vma=False,
    )
```
